32 devices in a mesh: sub: 32 (over z, y, x, core).
Axes of the slice: x: 2, y: 2, z: 4, core: 2. Of those that a mesh axis runs over, the one named last changes fastest.
Arguments:
- stiffness: bfloat16 [32, 1536, 1536], P('sub'), may hold values from -2 to 5, as said below
- local_inverse: bfloat16 [32, 1536, 1536], P('sub'), may hold values from -0.2 to 0.5, as said below
- coarse_basis: float32 [32, 48, 1536], P('sub'), may hold values from -0.15625 to 0.15625
- loads: float32 [32, 1536, 128], P('sub'), may hold values from -8 to 8
- counts: int32 [32, 1536], P('sub'), may hold values from 1 to 2, as said below
- shared_rows: int32 [32, 4, 256], P('sub'), may hold values from 0 to 1536, as said below
- coarse_map: int32 [32, 48], P('sub'), may hold values from 0 to 4095
- coarse_inverse: float32 [4096, 4096], P('sub'), may hold values from -1 to 2, as said below
Outputs:
- solution: float32 [32, 1536, 128], P('sub')
- residual: float32 [32, 1536, 128], P('sub')
The draws below stay inside these ranges and needn't reach their ends.
Inputs may be any that keep to these rules, and one draw needn't show every extreme that they name: `shared_rows`: for k = 0..3 entry [s, k, t] names a row of subdomain s shared with its slot-k neighbour, or 1536 where unused; live entries come first; entry t of s's list for a neighbour and entry t of that neighbour's list for s name the same unknown; no row appears in two lists of one subdomain; some pair of each kind has exactly 256 live entries. `counts`: 1 plus the number of lists of its subdomain that name the row. `stiffness`: Symmetric. `local_inverse`: Symmetric. `coarse_inverse`: Symmetric. `coarse_map`: A subdomain may name a coarse unknown more than once.
All inputs are finite; a program needn't handle non-finite values.
Results may differ from the reference program's by a relative error of at most 0.0081.
Values sent between devices are 32-bit elements; how exact they have to be, the bound alone decides.
No kernel may reach another device: no remote copies, remote signals or barrier semaphores. Data moves between devices by JAX's collectives and lax.ppermute only.
A program may use at most 128 MiB of HBM per device.

```python
import math
import jax
import jax.numpy as jnp
from jax import lax

NI = 1536
RHS = 128
NC = 4096
NCL = 48
CAP = 256
STRIDE = 8
ITERS = 3
NSUB = 32


def symmetric_blocks(key, number, order, low, high, spread):

    def one_block(block_key):
        key_diag, key_off = jax.random.split(block_key)
        diagonal = jax.random.uniform(key_diag, (order,), jnp.float32, low, high)
        raw = jax.random.uniform(key_off, (order, order), jnp.float32, -1.0, 1.0) * (spread / math.sqrt(order))
        mirrored = 0.5 * (raw + raw.T)
        identity = jnp.eye(order, dtype=jnp.float32)
        return mirrored * (1.0 - identity) + diagonal[:, None] * identity
    return lax.map(one_block, jax.random.split(key, number))


def interface_layout(key):
    key_perm, key_size, key_peak = jax.random.split(key, 3)
    ordering = jax.vmap(lambda one_key: jax.random.permutation(one_key, NI))(jax.random.split(key_perm, NSUB)).astype(jnp.int32)
    pair_sizes = jax.random.randint(key_size, (NSUB, 2), CAP // 8, CAP + 1)
    peaks = jax.random.randint(key_peak, (2,), 0, NSUB)
    pair_sizes = pair_sizes.at[peaks[0], 0].set(CAP).at[peaks[1], 1].set(CAP)
    slot_sizes = jnp.stack([pair_sizes[:, 0], jnp.roll(pair_sizes[:, 0], 1), pair_sizes[:, 1], jnp.roll(pair_sizes[:, 1], STRIDE)], axis=1)
    picked = ordering[:, :4 * CAP].reshape(NSUB, 4, CAP)
    live = jnp.arange(CAP, dtype=jnp.int32)[None, None, :] < slot_sizes[:, :, None]
    row_lists = jnp.where(live, picked, NI).astype(jnp.int32)
    subdomain_ids = jnp.arange(NSUB, dtype=jnp.int32)[:, None, None] + jnp.zeros_like(picked)
    multiplicity = jnp.ones((NSUB, NI), jnp.int32).at[subdomain_ids, picked].add(live.astype(jnp.int32))
    return (row_lists, multiplicity)


def draw_shared_rows(key, part):
    row_lists, multiplicity = interface_layout(key)
    return row_lists


def draw_counts(key, part):
    row_lists, multiplicity = interface_layout(key)
    return multiplicity


def draw_stiffness(key, part):
    key = jax.random.fold_in(key, 11)
    return symmetric_blocks(key, NSUB, NI, 2.0, 5.0, 2.0).astype(jnp.bfloat16)


def draw_local_inverse(key, part):
    key = jax.random.fold_in(key, 12)
    return symmetric_blocks(key, NSUB, NI, 0.2, 0.5, 0.2).astype(jnp.bfloat16)


def draw_coarse_inverse(key, part):
    key = jax.random.fold_in(key, 13)
    return symmetric_blocks(key, 1, NC, 1.0, 2.0, 1.0)[0]


def draw_loads(key, part):
    key = jax.random.fold_in(key, 14)
    key_main = jax.random.fold_in(key, 0)
    rising = 0.5 + jnp.arange(NSUB, dtype=jnp.float32) / (NSUB - 1)
    values = jnp.clip(jax.random.normal(key_main, (NSUB, NI, RHS), jnp.float32), -4.0, 4.0)
    return values * rising[:, None, None]


def place_ends(drawn, rng, least, largest):
    index_at = [jax.random.randint(jax.random.fold_in(rng, axis), (), 0, length) for axis, length in enumerate(drawn.shape)]
    main_axis = drawn.shape.index(max(drawn.shape))
    neighbour = index_at[:main_axis] + [(index_at[main_axis] + 1) % drawn.shape[main_axis]] + index_at[main_axis + 1:]
    return drawn.at[tuple(index_at)].set(least).at[tuple(neighbour)].set(largest)


def shard_levels(own_key, extent, shards, low, high):
    def one(axis_at, shards_of):
        draws = jax.random.uniform(jax.random.fold_in(jax.random.fold_in(own_key, 6), axis_at), (shards_of,), jnp.float32, low / len(shards), high / len(shards))
        return jnp.repeat(jnp.exp(draws), extent[axis_at] // shards_of).reshape((-1,) + (1,) * (len(extent) - axis_at - 1))

    factor_of = one(*shards[0])
    for cut in shards[1:]:
        factor_of = factor_of * one(*cut)
    return factor_of


def bell_draw(rng, dims, deviation, bound, cuts=(), held_as=jnp.bfloat16):
    array = deviation * jax.random.normal(rng, dims, jnp.float32)
    if cuts:
        array = array * shard_levels(rng, dims, cuts, -0.22, 0.18)
    return jnp.clip(array, -bound, bound).astype(held_as)


def setup_inputs(seed: int = 0) -> dict:
    streams_of = jax.random.split(jax.random.key(seed), 9)
    stiffness = draw_stiffness(jax.random.fold_in(streams_of[8], 71), 0)
    local_inverse = draw_local_inverse(jax.random.fold_in(streams_of[8], 71), 0)
    coarse_basis = bell_draw(streams_of[2], (NSUB, NCL, NI), NI ** -0.5, 0.15625, ((0, 32),), jnp.float32)
    loads = draw_loads(jax.random.fold_in(streams_of[8], 71), 0)
    counts = draw_counts(jax.random.fold_in(streams_of[8], 71), 0)
    shared_rows = draw_shared_rows(jax.random.fold_in(streams_of[8], 71), 0)
    coarse_map = place_ends(jax.random.randint(streams_of[6], (NSUB, NCL), 0, NC), jax.random.fold_in(streams_of[6], 1), 0, NC - 1).astype(jnp.int32)
    coarse_inverse = draw_coarse_inverse(jax.random.fold_in(streams_of[8], 71), 0)
    return {"stiffness": stiffness, "local_inverse": local_inverse, "coarse_basis": coarse_basis, "loads": loads, "counts": counts, "shared_rows": shared_rows, "coarse_map": coarse_map, "coarse_inverse": coarse_inverse}


highest = lax.Precision.HIGHEST
opposite_slot = (1, 0, 3, 2)


def assemble(local, shared_rows):
    assembled = local
    for slot_index, offset in enumerate((1, -1, STRIDE, -STRIDE)):
        outgoing = jax.vmap(lambda field, picks: jnp.take(field, picks, axis=0, mode="fill", fill_value=0.0))(local, shared_rows[:, slot_index])
        arrived = jnp.roll(outgoing, offset, axis=0)
        assembled = jax.vmap(lambda field, picks, extra: field.at[picks].add(extra, mode="drop"))(assembled, shared_rows[:, opposite_slot[slot_index]], arrived)
    return assembled


def reference(stiffness, local_inverse, coarse_basis, loads, counts, shared_rows, coarse_map, coarse_inverse):
    weights = 1.0 / counts.astype(jnp.float32)

    def inner(left, right):
        return jnp.sum(weights[:, :, None] * left * right, axis=(0, 1))

    def precond(resid):
        scaled = resid * weights[:, :, None]
        local_part = lax.map(lambda pair: jnp.dot(pair[0], pair[1].astype(jnp.bfloat16), preferred_element_type=jnp.float32), (local_inverse, scaled))
        terms = jnp.einsum("sln,snr->slr", coarse_basis, scaled, precision=highest)
        total = jnp.zeros((NC, RHS), jnp.float32).at[coarse_map.reshape(-1)].add(terms.reshape(-1, RHS))
        coarse = jnp.dot(coarse_inverse, total, precision=highest)
        picked = coarse[coarse_map]
        back = jnp.einsum("sln,slr->snr", coarse_basis, picked, precision=highest)
        return assemble(weights[:, :, None] * (local_part + back), shared_rows)

    def apply(direction):
        local_image = lax.map(lambda pair: jnp.dot(pair[0], pair[1].astype(jnp.bfloat16), preferred_element_type=jnp.float32), (stiffness, direction))
        return assemble(local_image, shared_rows)

    residual = assemble(loads, shared_rows)
    solution = jnp.zeros_like(residual)
    precond_now = precond(residual)
    direction = precond_now
    norm_now = inner(residual, precond_now)
    for iteration in range(ITERS):
        image = apply(direction)
        alpha = norm_now / inner(direction, image)
        solution = solution + alpha * direction
        residual = residual - alpha * image
        if iteration + 1 < ITERS:
            precond_now = precond(residual)
            norm_next = inner(residual, precond_now)
            direction = precond_now + (norm_next / norm_now) * direction
            norm_now = norm_next
    return solution, residual
```

```python
import jax
import jax.numpy as jnp
from jax import lax
from jax.experimental import pallas as pl
from jax.experimental.pallas import tpu as pltpu
from jax.sharding import PartitionSpec as P

STRIDE = 8
F32 = jnp.float32
BF16 = jnp.bfloat16
TILE = 512
SCAL = 8
LANES = 128

VSPEC = pl.BlockSpec(memory_space=pltpu.VMEM)
SSPEC = pl.BlockSpec(memory_space=pltpu.SMEM)


def near(shape, dtype=F32):
    return jax.ShapeDtypeStruct(shape, dtype)


def far(shape, dtype=F32):
    return jax.ShapeDtypeStruct(shape, dtype)


def call(kernel, name, args, outs, scratch=(), specs=None, flops=0):
    specs = specs or {}
    return pl.pallas_call(
        kernel,
        name=name,
        out_shape=tuple(outs),
        in_specs=[specs.get(i, VSPEC) for i in range(len(args))],
        out_specs=tuple(VSPEC for _ in outs),
        scratch_shapes=list(scratch),
        compiler_params=pltpu.CompilerParams(vmem_limit_bytes=48 * 1024 * 1024),
        cost_estimate=pl.CostEstimate(
            flops=flops, bytes_accessed=8 * 1024 * 1024, transcendentals=0
        ),
    )(*args)


def cut(x):
    high = x.astype(BF16)
    return high, (x - high.astype(F32)).astype(BF16)


def pair(x):
    return jnp.concatenate(cut(x), axis=1)


def halves(product):
    half = product.shape[1] // 2
    return product[:, :half] + product[:, half:]


def three(product, rows):
    half = product.shape[1] // 2
    return product[:rows, :half] + product[:rows, half:] + product[rows : 2 * rows, :half]


def dot(a, b):
    return jnp.dot(a, b, preferred_element_type=F32)


def tiles(total):
    step = min(TILE, total)
    return [(lo, min(step, total - lo)) for lo in range(0, total, step)]


def folded(x):
    return jnp.sum(x.reshape(-1, 8, x.shape[-1]), axis=0)


def pick_out(pick_ref, cat_ref, out_refs):
    cap = out_refs[0].shape[0]
    for j, out in enumerate(out_refs):
        out[...] = halves(dot(pick_ref[j * cap : (j + 1) * cap, :], cat_ref[...]))


def arrivals(arrived_refs, arr_cat):
    cap = arrived_refs[0].shape[0]
    for j, ref in enumerate(arrived_refs):
        arr_cat[j * cap : (j + 1) * cap, :] = pair(ref[...])


def setup_kernel(row_ref, col_ref, count_ref, basis_ref, basis_t_ref, loads_ref,
                 pick_ref, place_ref, weight_ref, basis2_ref, basis3_ref,
                 out0, out1, out2, out3, cat):
    slots, rows = pick_ref.shape
    rhs = loads_ref.shape[1]
    for lo, n in tiles(slots):
        at = lax.broadcasted_iota(jnp.int32, (n, rows), 1)
        pick_ref[lo : lo + n, :] = jnp.where(at == col_ref[lo : lo + n, :], 1.0, 0.0).astype(BF16)
    for lo, n in tiles(rows):
        cat[lo : lo + n, :] = pair(loads_ref[lo : lo + n, :])
    pick_out(pick_ref, cat, (out0, out1, out2, out3))
    for lo, n in tiles(rows):
        at = lo + lax.broadcasted_iota(jnp.int32, (n, slots), 0)
        place_ref[lo : lo + n, :] = jnp.where(at == row_ref[...], 1.0, 0.0).astype(BF16)
        weight = 1.0 / count_ref[lo : lo + n, :].astype(F32)
        weight_ref[lo : lo + n, :] = jnp.broadcast_to(weight, (n, rhs))
    ncl = basis_ref.shape[0]
    high, low = cut(basis_ref[...])
    basis2_ref[:ncl, :] = high
    basis2_ref[ncl:, :] = low
    high, low = cut(basis_t_ref[...])
    basis3_ref[...] = jnp.concatenate([high, high, low], axis=1)


def columns_kernel(map_ref, inverse_ref, out_ref, turned):
    order = inverse_ref.shape[1]
    for lo, n in tiles(order):
        turned[lo : lo + n, :] = inverse_ref[:, lo : lo + n].T

    def step(i, _):
        for k in range(8):
            m = i * 8 + k
            out_ref[pl.ds(m, 1), :] = turned[pl.ds(map_ref[m], 1), :]
        return 0

    lax.fori_loop(0, out_ref.shape[0] // 8, step, 0)


def coarse_kernel(map_ref, which_ref, got_ref, keep_ref, send_ref, turned, rowed):
    ncl, half = keep_ref.shape
    width = got_ref.shape[1]
    fill = jnp.zeros((turned.shape[1] - ncl, width), F32)
    for t in range(got_ref.shape[0] // ncl):
        block = jnp.concatenate([got_ref[t * ncl : (t + 1) * ncl, :], fill], axis=0)
        turned[t * width : (t + 1) * width, :] = block.T

    def step(i, _):
        for k in range(8):
            m = i * 8 + k
            rowed[pl.ds(m, 1), :] = turned[pl.ds(map_ref[m], 1), :]
        return 0

    lax.fori_loop(0, rowed.shape[0] // 8, step, 0)
    first = rowed[:half, :].T[:ncl, :]
    second = rowed[half:, :].T[:ncl, :]
    even = which_ref[0] == 0
    keep_ref[...] = jnp.where(even, first, second)
    send_ref[...] = jnp.where(even, second, first)


def stack_kernel(own_ref, other_ref, out_ref):
    ncl = own_ref.shape[0]
    own_high, own_low = cut(own_ref[...])
    other_high, other_low = cut(other_ref[...])
    out_ref[:ncl, :] = own_high
    out_ref[ncl : 2 * ncl, :] = other_high
    out_ref[2 * ncl : 3 * ncl, :] = own_low
    out_ref[3 * ncl :, :] = other_low


def send_terms(terms, scalars, send_ref):
    block = jnp.concatenate([terms, scalars], axis=0)
    rows = block.shape[0]
    for g in range(send_ref.shape[0] // rows):
        send_ref[g * rows : (g + 1) * rows, :] = block


def front(inverse_ref, cat, local_ref):
    for lo, n in tiles(inverse_ref.shape[0]):
        local_ref[lo : lo + n, :] = halves(dot(inverse_ref[lo : lo + n, :], cat[...]))


def first_kernel(loads_ref, a0, a1, a2, a3, place_ref, weight_ref, basis2_ref, inverse_ref,
                 resid_ref, local_ref, send_ref, cat, arr_cat):
    ncl = basis2_ref.shape[0] // 2
    rhs = loads_ref.shape[1]
    arrivals((a0, a1, a2, a3), arr_cat)
    terms = jnp.zeros((2 * ncl, 2 * rhs), F32)
    for lo, n in tiles(loads_ref.shape[0]):
        at = slice(lo, lo + n)
        resid = loads_ref[at, :] + halves(dot(place_ref[at, :], arr_cat[...]))
        resid_ref[at, :] = resid
        both = pair(weight_ref[at, :] * resid)
        cat[at, :] = both
        terms += dot(basis2_ref[:, at], both)
    send_terms(three(terms, ncl), jnp.zeros((SCAL, rhs), F32), send_ref)
    front(inverse_ref, cat, local_ref)


def coarse_solve_kernel(got_ref, g_ref, own_ref, other_ref):
    ncl = g_ref.shape[0] // 4
    rows = ncl + SCAL
    groups = got_ref.shape[0] // rows
    got = got_ref[...].reshape(groups, rows, got_ref.shape[1])
    terms = got[:, :ncl].reshape(groups * ncl, got_ref.shape[1])
    scalars = jnp.sum(got[:, ncl:], axis=0)
    values = three(dot(g_ref[...], pair(terms)), 2 * ncl)
    own_ref[:ncl, :] = values[:ncl]
    own_ref[ncl:, :] = scalars
    other_ref[:ncl, :] = values[ncl:]
    other_ref[ncl:, :] = scalars


def back_kernel(own_ref, other_ref, local_ref, weight_ref, basis3_ref, pick_ref,
                field_ref, scal_ref, out0, out1, out2, out3, cat):
    ncl = own_ref.shape[0] - SCAL
    total = own_ref[...] + other_ref[...]
    scal_ref[...] = total[ncl:]
    high, low = cut(total[:ncl])
    values = jnp.concatenate([high, low, high], axis=0)
    for lo, n in tiles(local_ref.shape[0]):
        at = slice(lo, lo + n)
        field = weight_ref[at, :] * (local_ref[at, :] + dot(basis3_ref[at, :], values))
        field_ref[at, :] = field
        cat[at, :] = pair(field)
    pick_out(pick_ref, cat, (out0, out1, out2, out3))


def apply_kernel(part_ref, a0, a1, a2, a3, place_ref, stiff_ref, pick_ref,
                 field_ref, image_ref, out0, out1, out2, out3, cat, arr_cat, cat2):
    arrivals((a0, a1, a2, a3), arr_cat)
    for lo, n in tiles(part_ref.shape[0]):
        at = slice(lo, lo + n)
        field = part_ref[at, :] + halves(dot(place_ref[at, :], arr_cat[...]))
        field_ref[at, :] = field
        cat[at, :] = pair(field)
    for lo, n in tiles(part_ref.shape[0]):
        at = slice(lo, lo + n)
        image = halves(dot(stiff_ref[at, :], cat[...]))
        image_ref[at, :] = image
        cat2[at, :] = pair(image)
    pick_out(pick_ref, cat2, (out0, out1, out2, out3))


def collect(sums, rhs):
    rows = [jnp.sum(s, axis=0, keepdims=True) for s in sums]
    rows.append(jnp.zeros((SCAL - len(rows), rhs), F32))
    return jnp.concatenate(rows, axis=0)


def start_kernel(part_ref, a0, a1, a2, a3, r_ref, u_ref,
                 place_ref, weight_ref, basis2_ref, inverse_ref,
                 w_ref, local_ref, send_ref, cat, arr_cat):
    ncl = basis2_ref.shape[0] // 2
    rhs = r_ref.shape[1]
    arrivals((a0, a1, a2, a3), arr_cat)
    terms = jnp.zeros((2 * ncl, 2 * rhs), F32)
    ru = jnp.zeros((8, rhs), F32)
    uw = jnp.zeros((8, rhs), F32)
    for lo, n in tiles(r_ref.shape[0]):
        at = slice(lo, lo + n)
        w = part_ref[at, :] + halves(dot(place_ref[at, :], arr_cat[...]))
        w_ref[at, :] = w
        weight = weight_ref[at, :]
        scaled = weight * w
        weighted = weight * u_ref[at, :]
        ru += folded(weighted * r_ref[at, :])
        uw += folded(weighted * w)
        both = pair(scaled)
        cat[at, :] = both
        terms += dot(basis2_ref[:, at], both)
    send_terms(three(terms, ncl), collect([ru, uw], rhs), send_ref)
    front(inverse_ref, cat, local_ref)


def second_kernel(part_ref, a0, a1, a2, a3, scal_ref, r_ref, u_ref, w_ref, m_ref,
                  place_ref, weight_ref, basis2_ref, inverse_ref,
                  z_ref, x1_ref, r1_ref, u1_ref, w1_ref, local_ref, send_ref,
                  cat, arr_cat):
    ncl = basis2_ref.shape[0] // 2
    rhs = r_ref.shape[1]
    arrivals((a0, a1, a2, a3), arr_cat)
    alpha = scal_ref[0:1, :] / scal_ref[1:2, :]
    terms = jnp.zeros((2 * ncl, 2 * rhs), F32)
    sums = [jnp.zeros((8, rhs), F32) for _ in range(4)]
    for lo, n in tiles(r_ref.shape[0]):
        at = slice(lo, lo + n)
        z = part_ref[at, :] + halves(dot(place_ref[at, :], arr_cat[...]))
        z_ref[at, :] = z
        weight = weight_ref[at, :]
        p, s = u_ref[at, :], w_ref[at, :]
        x1_ref[at, :] = alpha * p
        r1 = r_ref[at, :] - alpha * s
        u1 = p - alpha * m_ref[at, :]
        w1 = s - alpha * z
        r1_ref[at, :] = r1
        u1_ref[at, :] = u1
        w1_ref[at, :] = w1
        weighted = weight * u1
        scaled = weight * w1
        for k, term in enumerate((weighted * r1, weighted * w1, weighted * s, scaled * p)):
            sums[k] += folded(term)
        both = pair(scaled)
        cat[at, :] = both
        terms += dot(basis2_ref[:, at], both)
    send_terms(three(terms, ncl), collect(sums, rhs), send_ref)
    front(inverse_ref, cat, local_ref)


def step_scalars(before, now):
    beta = now[0:1, :] / before[0:1, :]
    energy = now[1:2, :] + beta * (now[2:3, :] + now[3:4, :]) + beta * beta * before[1:2, :]
    return beta, now[0:1, :] / energy, energy


def third_kernel(before_ref, scal_ref, x1_ref, r1_ref, u1_ref, w1_ref, p_ref, s_ref, q_ref, z_ref,
                 m_ref, image_ref, weight_ref,
                 x2_ref, r2_ref, u2_ref, half_ref, p1_ref, s1_ref, state_ref, send_ref):
    rhs = r1_ref.shape[1]
    beta, alpha, energy = step_scalars(before_ref[...], scal_ref[...])
    sums = [jnp.zeros((8, rhs), F32) for _ in range(4)]
    for lo, n in tiles(r1_ref.shape[0]):
        at = slice(lo, lo + n)
        p1 = u1_ref[at, :] + beta * p_ref[at, :]
        s1 = w1_ref[at, :] + beta * s_ref[at, :]
        q1 = m_ref[at, :] + beta * q_ref[at, :]
        r2 = r1_ref[at, :] - alpha * s1
        u2 = u1_ref[at, :] - alpha * q1
        half = w1_ref[at, :] - (alpha * beta) * z_ref[at, :]
        x2_ref[at, :] = x1_ref[at, :] + alpha * p1
        r2_ref[at, :] = r2
        u2_ref[at, :] = u2
        half_ref[at, :] = half
        p1_ref[at, :] = p1
        s1_ref[at, :] = s1
        weight = weight_ref[at, :]
        left = weight * half - alpha * image_ref[at, :]
        weighted = weight * u2
        for k, term in enumerate((weighted * r2, u2 * left, weighted * s1, p1 * left)):
            sums[k] += folded(term)
    block = collect(sums, rhs)
    for g in range(send_ref.shape[0] // SCAL):
        send_ref[g * SCAL : (g + 1) * SCAL, :] = block
    state_ref[...] = jnp.concatenate(
        [scal_ref[0:1, :], energy, alpha, jnp.zeros((SCAL - 3, rhs), F32)], axis=0
    )


def last_kernel(state_ref, got_ref, image_ref, a0, a1, a2, a3, place_ref,
                x2_ref, r2_ref, u2_ref, half_ref, p1_ref, s1_ref,
                x3_ref, r3_ref, arr_cat):
    arrivals((a0, a1, a2, a3), arr_cat)
    state = state_ref[...]
    now = jnp.sum(got_ref[...].reshape(-1, SCAL, got_ref.shape[1]), axis=0)
    beta, alpha, _ = step_scalars(state, now)
    old = state[2:3, :]
    for lo, n in tiles(r2_ref.shape[0]):
        at = slice(lo, lo + n)
        image = image_ref[at, :] + halves(dot(place_ref[at, :], arr_cat[...]))
        w2 = half_ref[at, :] - old * image
        x3_ref[at, :] = x2_ref[at, :] + alpha * (u2_ref[at, :] + beta * p1_ref[at, :])
        r3_ref[at, :] = r2_ref[at, :] - alpha * (w2 + beta * s1_ref[at, :])


def body(
    stiffness, local_inverse, coarse_basis, loads, counts, shared_rows, coarse_map, coarse_inverse
):
    size = lax.axis_size("sub")
    me = lax.axis_index("sub")
    rows, rhs = loads.shape[1:]
    ncl = coarse_basis.shape[1]
    slots, cap = shared_rows.shape[1:]
    order = coarse_inverse.shape[1]
    lists = slots * cap
    stiff, inverse = stiffness[0], local_inverse[0]

    def partner(distance, parity):
        def of(i):
            up = (i // distance) % 2 == parity
            return (i + distance if up else i - distance) % size

        return [(i, of(i)) for i in range(size)]

    swaps = [partner(1, 0), partner(1, 1), partner(STRIDE, 0), partner(STRIDE, 1)]

    def exchange(outs):
        got = [None] * len(outs)
        for j in (3, 2, 1, 0):
            got[j] = lax.ppermute(outs[j], "sub", swaps[j])
        return got

    cores = [[2 * i + c for i in range(size // 2)] for c in range(2)]
    groups = size // 2
    block = ncl + SCAL

    up_one = me % 2 == 0
    up_far = (me // STRIDE) % 2 == 0
    given = shared_rows[0]
    mine = jnp.concatenate(
        [
            jnp.where(up_one, given[:2], given[1::-1]),
            jnp.where(up_far, given[2:], given[:1:-1]),
        ],
        axis=0,
    )

    maps = lax.all_gather(coarse_map[0], "sub", axis=0, tiled=True)

    fields = (rows, rhs)
    out4 = [far((cap, rhs))] * 4
    wide = pltpu.VMEM((rows, 2 * rhs), BF16)
    wide_arr = pltpu.VMEM((lists, 2 * rhs), BF16)

    pick, place, weight, basis2, basis3, *outs = call(
        setup_kernel,
        "lists_and_loads",
        (
            mine.reshape(1, lists),
            mine.reshape(lists, 1),
            counts[0].reshape(rows, 1),
            coarse_basis[0],
            coarse_basis[0].T,
            loads[0],
        ),
        [
            near((lists, rows), BF16),
            near((rows, lists), BF16),
            near(fields),
            near((2 * ncl, rows), BF16),
            near((rows, 3 * ncl), BF16),
        ]
        + out4,
        [wide],
    )
    got = exchange(outs)
    r0, local, send = call(
        first_kernel,
        "residual_and_terms",
        (loads[0], *got, place, weight, basis2, inverse),
        [near(fields), near(fields), far((groups * block, rhs))],
        [wide, wide_arr],
    )

    (picked,) = call(
        columns_kernel,
        "coarse_columns",
        (maps, coarse_inverse),
        [far((size * ncl, coarse_inverse.shape[0]))],
        [pltpu.VMEM((order, coarse_inverse.shape[0]), F32)],
        {0: SSPEC},
    )
    mine_rows = lax.all_to_all(picked, "sub", 0, 0, tiled=True)
    by_core = maps.reshape(groups, 2, ncl).swapaxes(0, 1).reshape(-1)
    keep, pass_on = call(
        coarse_kernel,
        "coarse_block",
        (by_core, (me % 2).reshape(1), mine_rows),
        [far((ncl, groups * ncl)), far((ncl, groups * ncl))],
        [
            pltpu.VMEM((order, LANES), F32),
            pltpu.VMEM((size * ncl, LANES), F32),
        ],
        {0: SSPEC, 1: SSPEC},
    )
    passed = lax.ppermute(pass_on, "sub", swaps[0])
    (coarse,) = call(
        stack_kernel, "coarse_addends", (keep, passed), [near((4 * ncl, groups * ncl), BF16)]
    )

    def middle(send, local):
        got = lax.all_to_all(send, "sub", 0, 0, tiled=True, axis_index_groups=cores)
        own, other = call(
            coarse_solve_kernel,
            "coarse_solve",
            (got, coarse),
            [far((block, rhs)), far((block, rhs))],
        )
        came = lax.ppermute(other, "sub", swaps[0])
        part, scal, *outs = call(
            back_kernel,
            "coarse_back",
            (own, came, local, weight, basis3, pick),
            [near(fields), near((SCAL, rhs))] + out4,
            [wide],
        )
        arrived = exchange(outs)
        field, image, *outs = call(
            apply_kernel,
            "operator",
            (part, *arrived, place, stiff, pick),
            [near(fields), near(fields)] + out4,
            [wide, wide_arr, wide],
        )
        return scal, field, image, outs

    _, u0, image, outs = middle(send, local)
    got = exchange(outs)
    w0, local, send = call(
        start_kernel,
        "start",
        (image, *got, r0, u0, place, weight, basis2, inverse),
        [near(fields), near(fields), far((groups * block, rhs))],
        [wide, wide_arr],
    )
    scal0, m0, image, outs = middle(send, local)
    got = exchange(outs)
    z0, x1, r1, u1, w1, local, send = call(
        second_kernel,
        "first_update",
        (image, *got, scal0, r0, u0, w0, m0, place, weight, basis2, inverse),
        [near(fields)] * 6 + [far((groups * block, rhs))],
        [wide, wide_arr],
    )
    scal1, m1, image, outs = middle(send, local)
    got = exchange(outs)
    x2, r2, u2, half, p1, s1, state, send = call(
        third_kernel,
        "second_update",
        (scal0, scal1, x1, r1, u1, w1, u0, w0, m0, z0, m1, image, weight),
        [near(fields)] * 6 + [near((SCAL, rhs)), far((size * SCAL, rhs))],
    )
    sums = lax.all_to_all(send, "sub", 0, 0, tiled=True)
    x3, r3 = call(
        last_kernel,
        "last_update",
        (state, sums, image, *got, place, x2, r2, u2, half, p1, s1),
        [far(fields), far(fields)],
        [wide_arr],
    )
    return (x3[None], r3[None])


def solution(mesh):
    placed = (
        P("sub", None, None),
        P("sub", None, None),
        P("sub", None, None),
        P("sub", None, None),
        P("sub", None),
        P("sub", None, None),
        P("sub", None),
        P("sub", None),
    )
    return jax.shard_map(
        body,
        mesh=mesh,
        in_specs=placed,
        out_specs=(P("sub", None, None), P("sub", None, None)),
        check_vma=False,
    )
```

```python
import jax
import jax.numpy as jnp
from jax import lax
from jax.experimental import pallas as pl
from jax.experimental.pallas import tpu as pltpu
from jax.sharding import PartitionSpec as P

STRIDE = 8
F32 = jnp.float32
BF16 = jnp.bfloat16
TILE = 512
SCAL = 8
ORDER = (3, 1, 2, 0)
LANES = 128

VSPEC = pl.BlockSpec(memory_space=pltpu.VMEM)
SSPEC = pl.BlockSpec(memory_space=pltpu.SMEM)
ASPEC = pl.BlockSpec(memory_space=pl.ANY)


def near(shape, dtype=F32):
    return pltpu.VMEM(shape, dtype)


def far(shape, dtype=F32):
    return jax.ShapeDtypeStruct(shape, dtype)


def away(shape, dtype=F32):
    return pltpu.HBM(shape, dtype)


def held(*arrays):
    return tuple(pltpu.with_memory_space_constraint(a, pltpu.VMEM) for a in arrays)


def aside(*arrays):
    return tuple(pltpu.with_memory_space_constraint(a, pltpu.HBM) for a in arrays)


def call(kernel, name, args, outs, scratch=(), specs=None, flops=0):
    specs = specs or {}
    return pl.pallas_call(
        kernel,
        name=name,
        out_shape=tuple(outs),
        in_specs=[specs.get(i, VSPEC) for i in range(len(args))],
        out_specs=tuple(VSPEC for _ in outs),
        scratch_shapes=list(scratch),
        compiler_params=pltpu.CompilerParams(vmem_limit_bytes=20 * 1024 * 1024),
        cost_estimate=pl.CostEstimate(
            flops=flops, bytes_accessed=8 * 1024 * 1024, transcendentals=0
        ),
    )(*args)


def cut(x):
    high = x.astype(BF16)
    return high, (x - high.astype(F32)).astype(BF16)


def pair(x):
    return jnp.concatenate(cut(x), axis=1)


def halves(product):
    half = product.shape[1] // 2
    return product[:, :half] + product[:, half:]


def three(product, rows):
    half = product.shape[1] // 2
    return product[:rows, :half] + product[:rows, half:] + product[rows : 2 * rows, :half]


def dot(a, b):
    return jnp.dot(a, b, preferred_element_type=F32)


def tiles(total):
    step = min(TILE, total)
    return [(lo, min(step, total - lo)) for lo in range(0, total, step)]


def folded(x):
    return jnp.sum(x.reshape(-1, 8, x.shape[-1]), axis=0)


def pick_out(pick_ref, cat_ref, out_refs):
    cap = out_refs[0].shape[0]
    for j, out in enumerate(out_refs):
        out[...] = halves(dot(pick_ref[j * cap : (j + 1) * cap, :], cat_ref[...]))


def arrivals(arrived_refs, arr_cat):
    cap = arrived_refs[0].shape[0]
    for j, ref in enumerate(arrived_refs):
        arr_cat[j * cap : (j + 1) * cap, :] = pair(ref[...])


def fill_pick(row_ref, pick_ref):
    slots, rows = pick_ref.shape
    entries = jnp.broadcast_to(row_ref[...].astype(F32), (LANES, slots)).T
    for lo, n in tiles(slots):
        for left in range(0, rows, LANES):
            at = left + lax.broadcasted_iota(jnp.int32, (n, LANES), 1)
            same = at.astype(F32) == entries[lo : lo + n]
            pick_ref[lo : lo + n, left : left + LANES] = jnp.where(same, 1.0, 0.0).astype(BF16)


def fill_place(row_ref, place_ref):
    rows, slots = place_ref.shape
    for lo, n in tiles(rows):
        at = lo + lax.broadcasted_iota(jnp.int32, (n, slots), 0)
        place_ref[lo : lo + n, :] = jnp.where(at == row_ref[...], 1.0, 0.0).astype(BF16)


def weights_of(count_ref):
    rows = count_ref.shape[1]
    return jnp.broadcast_to(1.0 / count_ref[...].astype(F32), (LANES, rows)).T


def fill_basis2(basis_ref, basis2_ref):
    ncl = basis_ref.shape[0]
    high, low = cut(basis_ref[...])
    basis2_ref[:ncl, :] = high
    basis2_ref[ncl:, :] = low


def loads_kernel(row_ref, loads_ref, out0, out1, out2, out3, pick, cat):
    fill_pick(row_ref, pick)
    for lo, n in tiles(loads_ref.shape[0]):
        cat[lo : lo + n, :] = pair(loads_ref[lo : lo + n, :])
    pick_out(pick, cat, (out0, out1, out2, out3))


def back_tables_kernel(row_ref, count_ref, basis_ref, after_ref,
                       pick_ref, weight_ref, basis3_ref):
    fill_pick(row_ref, pick_ref)
    weight_ref[...] = weights_of(count_ref)
    ncl, rows = basis_ref.shape
    high, low = cut(basis_ref[...])
    high, low = high.astype(F32), low.astype(F32)
    fill = jnp.zeros((basis3_ref.shape[1] - 3 * ncl, rows), F32)
    basis3_ref[...] = jnp.concatenate([high, high, low, fill], axis=0).T.astype(BF16)


def tables_kernel(row_ref, basis_ref, stiff_from, inverse_from, after_ref,
                  place_ref, basis2_ref, stiff_ref, inverse_ref, sems):
    copies = [
        pltpu.make_async_copy(stiff_from, stiff_ref, sems.at[0]),
        pltpu.make_async_copy(inverse_from, inverse_ref, sems.at[1]),
    ]
    for copy in copies:
        copy.start()
    fill_place(row_ref, place_ref)
    fill_basis2(basis_ref, basis2_ref)
    for copy in copies:
        copy.wait()


def columns_kernel(map_ref, inverse_ref, out_ref, turned):
    order = inverse_ref.shape[1]
    for lo, n in tiles(order):
        turned[lo : lo + n, :] = inverse_ref[:, lo : lo + n].T

    size = map_ref.shape[0]
    ncl = out_ref.shape[0] // size

    def step(i, _):
        for k in range(ncl):
            out_ref[pl.ds(i * ncl + k, 1), :] = turned[pl.ds(map_ref[i, k], 1), :]
        return 0

    lax.fori_loop(0, size, step, 0)


def coarse_kernel(map_ref, which_ref, got_ref, keep_ref, send_ref, turned, rowed):
    ncl, half = keep_ref.shape
    width = got_ref.shape[1]
    fill = jnp.zeros((turned.shape[1] - ncl, width), F32)
    for t in range(got_ref.shape[0] // ncl):
        block = jnp.concatenate([got_ref[t * ncl : (t + 1) * ncl, :], fill], axis=0)
        turned[t * width : (t + 1) * width, :] = block.T

    size = map_ref.shape[0]

    def step(i, _):
        for c in range(2):
            for k in range(ncl):
                row = turned[pl.ds(map_ref[2 * i + c, k], 1), :]
                rowed[pl.ds(c * half + i * ncl + k, 1), :] = row
        return 0

    lax.fori_loop(0, size // 2, step, 0)
    first = rowed[:half, :].T[:ncl, :]
    second = rowed[half:, :].T[:ncl, :]
    even = which_ref[0] == 0
    keep_ref[...] = jnp.where(even, first, second)
    send_ref[...] = jnp.where(even, second, first)


def stack_kernel(own_ref, other_ref, terms_ref, out_ref, after_ref):
    after_ref[...] = jnp.zeros_like(after_ref)
    ncl = own_ref.shape[0]
    own_high, own_low = cut(own_ref[...])
    other_high, other_low = cut(other_ref[...])
    out_ref[:ncl, :] = own_high
    out_ref[ncl : 2 * ncl, :] = other_high
    out_ref[2 * ncl : 3 * ncl, :] = own_low
    out_ref[3 * ncl :, :] = other_low


def send_terms(terms, scalars, send_ref):
    block = jnp.concatenate([terms, scalars], axis=0)
    rows = block.shape[0]
    for g in range(send_ref.shape[0] // rows):
        send_ref[g * rows : (g + 1) * rows, :] = block


def front(inverse_ref, cat, local_ref):
    for lo, n in tiles(inverse_ref.shape[0]):
        local_ref[lo : lo + n, :] = halves(dot(inverse_ref[lo : lo + n, :], cat[...]))


def first_kernel(loads_ref, a0, a1, a2, a3, row_ref, count_ref, basis_ref, inverse_from,
                 resid_ref, local_ref, send_ref,
                 cat, arr_cat, place, basis2, inverse, weight, sems):
    copy = pltpu.make_async_copy(inverse_from, inverse, sems.at[0])
    copy.start()
    fill_place(row_ref, place)
    fill_basis2(basis_ref, basis2)
    weight[...] = weights_of(count_ref)
    ncl, rhs = basis_ref.shape[0], loads_ref.shape[1]
    arrivals((a0, a1, a2, a3), arr_cat)
    terms = jnp.zeros((2 * ncl, 2 * rhs), F32)
    for lo, n in tiles(loads_ref.shape[0]):
        at = slice(lo, lo + n)
        resid = loads_ref[at, :] + halves(dot(place[at, :], arr_cat[...]))
        resid_ref[at, :] = resid
        both = pair(weight[at, :] * resid)
        cat[at, :] = both
        terms += dot(basis2[:, at], both)
    send_terms(three(terms, ncl), jnp.zeros((SCAL, rhs), F32), send_ref)
    copy.wait()
    front(inverse, cat, local_ref)


def coarse_solve_kernel(got_ref, g_ref, own_ref, other_ref):
    ncl = g_ref.shape[0] // 4
    rows = ncl + SCAL
    groups = got_ref.shape[0] // rows
    got = got_ref[...].reshape(groups, rows, got_ref.shape[1])
    terms = got[:, :ncl].reshape(groups * ncl, got_ref.shape[1])
    scalars = jnp.sum(got[:, ncl:], axis=0)
    values = three(dot(g_ref[...], pair(terms)), 2 * ncl)
    own_ref[:ncl, :] = values[:ncl]
    own_ref[ncl:, :] = scalars
    other_ref[:ncl, :] = values[ncl:]
    other_ref[ncl:, :] = scalars


def back_kernel(own_ref, other_ref, local_ref, weight_ref, basis3_ref, pick_ref,
                field_ref, scal_ref, out0, out1, out2, out3, cat):
    ncl = own_ref.shape[0] - SCAL
    total = own_ref[...] + other_ref[...]
    scal_ref[...] = total[ncl:]
    high, low = cut(total[:ncl])
    fill = jnp.zeros((basis3_ref.shape[1] - 3 * ncl, high.shape[1]), BF16)
    values = jnp.concatenate([high, low, high, fill], axis=0)
    for lo, n in tiles(local_ref.shape[0]):
        at = slice(lo, lo + n)
        field = weight_ref[at, :] * (local_ref[at, :] + dot(basis3_ref[at, :], values))
        field_ref[at, :] = field
        cat[at, :] = pair(field)
    pick_out(pick_ref, cat, (out0, out1, out2, out3))


def apply_kernel(part_ref, a0, a1, a2, a3, place_ref, stiff_ref, pick_ref,
                 field_ref, image_ref, out0, out1, out2, out3, cat, arr_cat, cat2):
    arrivals((a0, a1, a2, a3), arr_cat)
    for lo, n in tiles(part_ref.shape[0]):
        at = slice(lo, lo + n)
        field = part_ref[at, :] + halves(dot(place_ref[at, :], arr_cat[...]))
        field_ref[at, :] = field
        cat[at, :] = pair(field)
    for lo, n in tiles(part_ref.shape[0]):
        at = slice(lo, lo + n)
        image = halves(dot(stiff_ref[at, :], cat[...]))
        image_ref[at, :] = image
        cat2[at, :] = pair(image)
    pick_out(pick_ref, cat2, (out0, out1, out2, out3))


def collect(sums, rhs):
    rows = [jnp.sum(s, axis=0, keepdims=True) for s in sums]
    rows.append(jnp.zeros((SCAL - len(rows), rhs), F32))
    return jnp.concatenate(rows, axis=0)


def start_kernel(part_ref, a0, a1, a2, a3, r_ref, u_ref,
                 place_ref, weight_ref, basis2_ref, inverse_ref,
                 w_ref, local_ref, send_ref, cat, arr_cat):
    ncl = basis2_ref.shape[0] // 2
    rhs = r_ref.shape[1]
    arrivals((a0, a1, a2, a3), arr_cat)
    terms = jnp.zeros((2 * ncl, 2 * rhs), F32)
    ru = jnp.zeros((8, rhs), F32)
    uw = jnp.zeros((8, rhs), F32)
    for lo, n in tiles(r_ref.shape[0]):
        at = slice(lo, lo + n)
        w = part_ref[at, :] + halves(dot(place_ref[at, :], arr_cat[...]))
        w_ref[at, :] = w
        weight = weight_ref[at, :]
        scaled = weight * w
        weighted = weight * u_ref[at, :]
        ru += folded(weighted * r_ref[at, :])
        uw += folded(weighted * w)
        both = pair(scaled)
        cat[at, :] = both
        terms += dot(basis2_ref[:, at], both)
    send_terms(three(terms, ncl), collect([ru, uw], rhs), send_ref)
    front(inverse_ref, cat, local_ref)


def second_kernel(part_ref, a0, a1, a2, a3, scal_ref, r_ref, u_ref, w_ref, m_ref,
                  place_ref, weight_ref, basis2_ref, inverse_ref,
                  z_ref, x1_ref, r1_ref, u1_ref, w1_ref, local_ref, send_ref,
                  cat, arr_cat):
    ncl = basis2_ref.shape[0] // 2
    rhs = r_ref.shape[1]
    arrivals((a0, a1, a2, a3), arr_cat)
    alpha = scal_ref[0:1, :] / scal_ref[1:2, :]
    terms = jnp.zeros((2 * ncl, 2 * rhs), F32)
    sums = [jnp.zeros((8, rhs), F32) for _ in range(4)]
    for lo, n in tiles(r_ref.shape[0]):
        at = slice(lo, lo + n)
        z = part_ref[at, :] + halves(dot(place_ref[at, :], arr_cat[...]))
        z_ref[at, :] = z
        weight = weight_ref[at, :]
        p, s = u_ref[at, :], w_ref[at, :]
        x1_ref[at, :] = alpha * p
        r1 = r_ref[at, :] - alpha * s
        u1 = p - alpha * m_ref[at, :]
        w1 = s - alpha * z
        r1_ref[at, :] = r1
        u1_ref[at, :] = u1
        w1_ref[at, :] = w1
        weighted = weight * u1
        scaled = weight * w1
        for k, term in enumerate((weighted * r1, weighted * w1, weighted * s, scaled * p)):
            sums[k] += folded(term)
        both = pair(scaled)
        cat[at, :] = both
        terms += dot(basis2_ref[:, at], both)
    send_terms(three(terms, ncl), collect(sums, rhs), send_ref)
    front(inverse_ref, cat, local_ref)


def step_scalars(before, now):
    beta = now[0:1, :] / before[0:1, :]
    energy = now[1:2, :] + beta * (now[2:3, :] + now[3:4, :]) + beta * beta * before[1:2, :]
    return beta, now[0:1, :] / energy, energy


def third_kernel(part_ref, a0, a1, a2, a3, place_ref, stiff_ref, pick_ref,
                 before_ref, scal_ref, x1_ref, r1_ref, u1_ref, w1_ref, p_ref, s_ref, q_ref, z_ref,
                 weight_ref,
                 out0, out1, out2, out3, send_ref, state_ref,
                 x2_ref, r2_ref, u2_ref, half_ref, p1_ref, s1_ref,
                 cat, arr_cat, cat2, m, image):
    apply_kernel(part_ref, a0, a1, a2, a3, place_ref, stiff_ref, pick_ref,
                 m, image, out0, out1, out2, out3, cat, arr_cat, cat2)
    rhs = r1_ref.shape[1]
    beta, alpha, energy = step_scalars(before_ref[...], scal_ref[...])
    sums = [jnp.zeros((8, rhs), F32) for _ in range(4)]
    for lo, n in tiles(r1_ref.shape[0]):
        at = slice(lo, lo + n)
        p1 = u1_ref[at, :] + beta * p_ref[at, :]
        s1 = w1_ref[at, :] + beta * s_ref[at, :]
        q1 = m[at, :] + beta * q_ref[at, :]
        r2 = r1_ref[at, :] - alpha * s1
        u2 = u1_ref[at, :] - alpha * q1
        half = w1_ref[at, :] - (alpha * beta) * z_ref[at, :]
        weight = weight_ref[at, :]
        left = weight * half - alpha * image[at, :]
        weighted = weight * u2
        for k, term in enumerate((weighted * r2, u2 * left, weighted * s1, p1 * left)):
            sums[k] += folded(term)
        x2_ref[at, :] = x1_ref[at, :] + alpha * p1
        r2_ref[at, :] = r2
        u2_ref[at, :] = u2
        half_ref[at, :] = half - alpha * image[at, :]
        p1_ref[at, :] = p1
        s1_ref[at, :] = s1
    block = collect(sums, rhs)
    for g in range(send_ref.shape[0] // SCAL):
        send_ref[g * SCAL : (g + 1) * SCAL, :] = block
    state_ref[...] = jnp.concatenate(
        [scal_ref[0:1, :], energy, alpha, jnp.zeros((SCAL - 3, rhs), F32)], axis=0
    )


def last_kernel(row_ref, state_ref, got_ref, a0, a1, a2, a3,
                x2_ref, r2_ref, u2_ref, half_ref, p1_ref, s1_ref,
                x3_ref, r3_ref, place, arr_cat):
    fill_place(row_ref, place)
    arrivals((a0, a1, a2, a3), arr_cat)
    state = state_ref[...]
    now = jnp.sum(got_ref[...].reshape(-1, SCAL, got_ref.shape[1]), axis=0)
    beta, alpha, _ = step_scalars(state, now)
    old = state[2:3, :]
    for lo, n in tiles(r2_ref.shape[0]):
        at = slice(lo, lo + n)
        w2 = half_ref[at, :] - old * halves(dot(place[at, :], arr_cat[...]))
        x3_ref[at, :] = x2_ref[at, :] + alpha * (u2_ref[at, :] + beta * p1_ref[at, :])
        r3_ref[at, :] = r2_ref[at, :] - alpha * (w2 + beta * s1_ref[at, :])


def body(
    stiffness, local_inverse, coarse_basis, loads, counts, shared_rows, coarse_map, coarse_inverse
):
    size = lax.axis_size("sub")
    me = lax.axis_index("sub")
    rows, rhs = loads.shape[1:]
    ncl = coarse_basis.shape[1]
    slots, cap = shared_rows.shape[1:]
    order = coarse_inverse.shape[1]
    lists = slots * cap
    stiff, inverse = stiffness[0], local_inverse[0]

    def partner(distance, parity):
        def of(i):
            up = (i // distance) % 2 == parity
            return (i + distance if up else i - distance) % size

        return [(i, of(i)) for i in range(size)]

    inside = partner(1, 0)
    swaps = [inside, partner(1, 1), partner(STRIDE, 0), partner(STRIDE, 1)]
    swaps = [swaps[j] for j in ORDER]

    def exchange(outs):
        return [lax.ppermute(out, "sub", swap) for out, swap in zip(outs, swaps)]

    cores = [[2 * i + c for i in range(size // 2)] for c in range(2)]
    groups = size // 2
    block = ncl + SCAL

    up_one = me % 2 == 0
    up_far = (me // STRIDE) % 2 == 0
    given = shared_rows[0]
    mine = jnp.concatenate(
        [
            jnp.where(up_one, given[:2], given[1::-1]),
            jnp.where(up_far, given[2:], given[:1:-1]),
        ],
        axis=0,
    )

    fields = (rows, rhs)
    out4 = [far((cap, rhs))] * 4
    wide = pltpu.VMEM((rows, 2 * rhs), BF16)
    wide_arr = pltpu.VMEM((lists, 2 * rhs), BF16)
    place_like = pltpu.VMEM((rows, lists), BF16)
    listed = jnp.concatenate([mine[j] for j in ORDER]).reshape(1, lists)
    basis = coarse_basis[0]

    outs = call(
        loads_kernel,
        "loads",
        (listed, loads[0]),
        out4,
        [pltpu.VMEM((lists, rows), BF16), wide],
    )
    arrived = exchange(outs)
    own_map = jnp.pad(coarse_map, ((0, 0), (0, -ncl % LANES)))
    maps = jnp.broadcast_to(own_map, (size, own_map.shape[1]))
    maps = lax.all_to_all(maps, "sub", 0, 0, tiled=True)
    maps, *arrived = lax.optimization_barrier((maps, *arrived))


    (picked,) = call(
        columns_kernel,
        "coarse_columns",
        (maps, coarse_inverse),
        [far((size * ncl, coarse_inverse.shape[0]))],
        [pltpu.VMEM((order, coarse_inverse.shape[0]), F32)],
        {0: SSPEC},
    )
    mine_rows = lax.all_to_all(picked, "sub", 0, 0, tiled=True)

    r0, local, send = call(
        first_kernel,
        "residual_and_terms",
        (loads[0], *arrived, listed, counts, basis, inverse),
        [away(fields), away(fields), far((groups * block, rhs))],
        [
            wide,
            wide_arr,
            place_like,
            pltpu.VMEM((2 * ncl, rows), BF16),
            pltpu.VMEM((rows, rows), BF16),
            pltpu.VMEM(fields, F32),
            pltpu.SemaphoreType.DMA((1,)),
        ],
        {8: ASPEC},
    )
    r0, local = aside(r0, local)

    keep, pass_on = call(
        coarse_kernel,
        "coarse_block",
        (maps, (me % 2).reshape(1), mine_rows),
        [far((ncl, groups * ncl)), far((ncl, groups * ncl))],
        [
            pltpu.VMEM((order, LANES), F32),
            pltpu.VMEM((size * ncl, LANES), F32),
        ],
        {0: SSPEC, 1: SSPEC},
    )
    passed = lax.ppermute(pass_on, "sub", inside)

    def share(send):
        return lax.all_to_all(send, "sub", 0, 0, tiled=True, axis_index_groups=cores)

    terms = share(send)
    coarse, after = call(
        stack_kernel,
        "coarse_addends",
        (keep, passed, terms),
        [near((4 * ncl, groups * ncl), BF16), far((SCAL, LANES))],
    )
    pick, weight, basis3 = call(
        back_tables_kernel,
        "back_tables",
        (listed, counts, basis, after),
        [near((lists, rows), BF16), near(fields), near((rows, 2 * LANES), BF16)],
    )
    place, basis2, stiff, inverse = call(
        tables_kernel,
        "tables",
        (listed, basis, stiff, inverse, after),
        [
            near((rows, lists), BF16),
            near((2 * ncl, rows), BF16),
            near((rows, rows), BF16),
            near((rows, rows), BF16),
        ],
        [pltpu.SemaphoreType.DMA((2,))],
        {2: ASPEC, 3: ASPEC},
    )
    coarse, pick, weight, basis3 = held(coarse, pick, weight, basis3)
    place, basis2, stiff, inverse = held(place, basis2, stiff, inverse)

    def correct(terms, local):
        own, other = call(
            coarse_solve_kernel,
            "coarse_solve",
            (terms, coarse),
            [far((block, rhs)), far((block, rhs))],
        )
        came = lax.ppermute(other, "sub", inside)
        part, scal, *outs = call(
            back_kernel,
            "coarse_back",
            (own, came, local, weight, basis3, pick),
            [near(fields), near((SCAL, rhs))] + out4,
            [wide],
        )
        return *held(part, scal), exchange(outs)

    def operate(part, arrived):
        field, image, *outs = call(
            apply_kernel,
            "operator",
            (part, *arrived, place, stiff, pick),
            [near(fields), near(fields)] + out4,
            [wide, wide_arr, wide],
        )
        return *held(field, image), exchange(outs)

    part, _, arrived = correct(terms, local)
    u0, image, arrived = operate(part, arrived)
    w0, local, send = call(
        start_kernel,
        "start",
        (image, *arrived, r0, u0, place, weight, basis2, inverse),
        [near(fields), near(fields), far((groups * block, rhs))],
        [wide, wide_arr],
    )
    w0, local = held(w0, local)
    part, scal0, arrived = correct(share(send), local)
    m0, image, arrived = operate(part, arrived)
    *news, send = call(
        second_kernel,
        "first_update",
        (image, *arrived, scal0, r0, u0, w0, m0, place, weight, basis2, inverse),
        [near(fields)] * 6 + [far((groups * block, rhs))],
        [wide, wide_arr],
    )
    z0, x1, r1, u1, w1, local = held(*news)
    part, scal1, arrived = correct(share(send), local)
    *outs, send, state, x2, r2, u2, half, p1, s1 = call(
        third_kernel,
        "second_update",
        (part, *arrived, place, stiff, pick)
        + (scal0, scal1, x1, r1, u1, w1, u0, w0, m0, z0, weight),
        out4 + [far((size * SCAL, rhs)), far((SCAL, rhs))] + [away(fields)] * 6,
        [wide, wide_arr, wide, pltpu.VMEM(fields, F32), pltpu.VMEM(fields, F32)],
    )
    x2, r2, u2, half, p1, s1 = aside(x2, r2, u2, half, p1, s1)
    arrived = exchange(outs)
    sums = lax.all_to_all(send, "sub", 0, 0, tiled=True)
    x3, r3 = call(
        last_kernel,
        "last_update",
        (listed, state, sums, *arrived, x2, r2, u2, half, p1, s1),
        [far(fields), far(fields)],
        [place_like, wide_arr],
    )
    return (x3[None], r3[None])


def solution(mesh):
    placed = (
        P("sub", None, None),
        P("sub", None, None),
        P("sub", None, None),
        P("sub", None, None),
        P("sub", None),
        P("sub", None, None),
        P("sub", None),
        P("sub", None),
    )
    return jax.shard_map(
        body,
        mesh=mesh,
        in_specs=placed,
        out_specs=(P("sub", None, None), P("sub", None, None)),
        check_vma=False,
    )
```

```python
import jax
import jax.numpy as jnp
from jax import lax
from jax.experimental import pallas as pl
from jax.experimental.pallas import tpu as pltpu
from jax.sharding import PartitionSpec as P

STRIDE = 8
F32 = jnp.float32
BF16 = jnp.bfloat16
TILE = 512
FINE = 256
SCAL = 8
ORDER = (3, 1, 2, 0)
LANES = 128

VSPEC = pl.BlockSpec(memory_space=pltpu.VMEM)
SSPEC = pl.BlockSpec(memory_space=pltpu.SMEM)
ASPEC = pl.BlockSpec(memory_space=pltpu.HBM)


def near(shape, dtype=F32):
    return pltpu.VMEM(shape, dtype)


def far(shape, dtype=F32):
    return jax.ShapeDtypeStruct(shape, dtype)


def away(shape, dtype=F32):
    return pltpu.HBM(shape, dtype)


def held(*arrays):
    return tuple(pltpu.with_memory_space_constraint(a, pltpu.VMEM) for a in arrays)


def aside(*arrays):
    return tuple(pltpu.with_memory_space_constraint(a, pltpu.HBM) for a in arrays)


def call(kernel, name, args, outs, scratch=(), specs=None, us=2, mib=16, sent=()):
    specs = specs or {}
    return pl.pallas_call(
        kernel,
        name=name,
        out_shape=tuple(outs),
        in_specs=[specs.get(i, VSPEC) for i in range(len(args))],
        out_specs=tuple(ASPEC if i in sent else VSPEC for i in range(len(outs))),
        scratch_shapes=list(scratch),
        compiler_params=pltpu.CompilerParams(vmem_limit_bytes=mib * 1024 * 1024),
        cost_estimate=pl.CostEstimate(
            flops=0, bytes_accessed=us * 3_000_000, transcendentals=0
        ),
    )(*args)


def cut(x):
    high = x.astype(BF16)
    return high, (x - high.astype(F32)).astype(BF16)


def pair(x):
    return jnp.concatenate(cut(x), axis=1)


def halves(product):
    half = product.shape[1] // 2
    return product[:, :half] + product[:, half:]


def three(product, rows):
    half = product.shape[1] // 2
    return product[:rows, :half] + product[:rows, half:] + product[rows : 2 * rows, :half]


def dot(a, b):
    return jnp.dot(a, b, preferred_element_type=F32)


def tiles(total, step=TILE):
    step = min(step, total)
    return [(lo, min(step, total - lo)) for lo in range(0, total, step)]


def folded(x):
    return jnp.sum(x.reshape(-1, 8, x.shape[-1]), axis=0)


def pick_out(pick_ref, cat_ref, out_refs):
    cap = out_refs[0].shape[0]
    for j, out in enumerate(out_refs):
        out[...] = halves(dot(pick_ref[j * cap : (j + 1) * cap, :], cat_ref[...]))


def arrivals(arrived_refs, arr_cat):
    cap = arrived_refs[0].shape[0]
    for j, ref in enumerate(arrived_refs):
        arr_cat[j * cap : (j + 1) * cap, :] = pair(ref[...])


def bring(pairs, sems):
    copies = [pltpu.make_async_copy(*p, sems.at[i]) for i, p in enumerate(pairs)]
    for copy in copies:
        copy.start()
    return copies


def fill_pick(row_ref, pick_ref):
    slots, rows = pick_ref.shape
    entries = jnp.broadcast_to(row_ref[...].astype(F32), (LANES, slots)).T
    for lo, n in tiles(slots):
        for left in range(0, rows, LANES):
            at = left + lax.broadcasted_iota(jnp.int32, (n, LANES), 1)
            same = at.astype(F32) == entries[lo : lo + n]
            pick_ref[lo : lo + n, left : left + LANES] = jnp.where(same, 1.0, 0.0).astype(BF16)


def fill_place(row_ref, place_ref):
    rows, slots = place_ref.shape
    for lo, n in tiles(rows):
        at = lo + lax.broadcasted_iota(jnp.int32, (n, slots), 0)
        place_ref[lo : lo + n, :] = jnp.where(at == row_ref[...], 1.0, 0.0).astype(BF16)


def weights_of(count_ref):
    rows = count_ref.shape[1]
    return jnp.broadcast_to(1.0 / count_ref[...].astype(F32), (LANES, rows)).T


def fill_basis2(basis_ref, basis2_ref):
    ncl = basis_ref.shape[0]
    high, low = cut(basis_ref[...])
    basis2_ref[:ncl, :] = high
    basis2_ref[ncl:, :] = low


def loads_kernel(rows_ref, loads_from, listed_ref, out0, out1, out2, out3, pick, cat, loads, sems):
    copies = bring([(loads_from, loads)], sems)
    me = lax.axis_index("sub")
    one = me % 2 == 0
    far_one = (me // STRIDE) % 2 == 0
    given = [rows_ref[k : k + 1, :] for k in range(4)]
    lists = [
        jnp.where(one, given[0], given[1]),
        jnp.where(one, given[1], given[0]),
        jnp.where(far_one, given[2], given[3]),
        jnp.where(far_one, given[3], given[2]),
    ]
    listed_ref[...] = jnp.concatenate([lists[j] for j in ORDER], axis=1)
    fill_pick(listed_ref, pick)
    for copy in copies:
        copy.wait()
    for lo, n in tiles(loads.shape[0]):
        cat[lo : lo + n, :] = pair(loads[lo : lo + n, :])
    pick_out(pick, cat, (out0, out1, out2, out3))


def fill_basis3(basis_ref, basis3_ref):
    ncl, rows = basis_ref.shape
    high, low = cut(basis_ref[...])
    high, low = high.astype(F32), low.astype(F32)
    fill = jnp.zeros((basis3_ref.shape[1] - 3 * ncl, rows), F32)
    basis3_ref[...] = jnp.concatenate([high, high, low, fill], axis=0).T.astype(BF16)


def products_kernel(row_ref, count_ref, basis_ref, stiff_from,
                    stiff_place_ref, stiff_shared_ref, basis_place_ref, pick_basis_ref,
                    pick, place, stiff, basis2, basis3, sems):
    copy = pltpu.make_async_copy(stiff_from, stiff, sems.at[0])
    copy.start()
    fill_pick(row_ref, pick)
    fill_place(row_ref, place)
    weight = 1.0 / count_ref[...].astype(F32)
    fill_basis2(basis_ref, basis2)
    scaled = basis2[...].astype(F32) * weight
    basis_place_ref[...] = dot(scaled.astype(BF16), place[...]).astype(BF16)
    fill_basis3(basis_ref, basis3)
    full = weights_of(count_ref)
    for left in range(0, basis3.shape[1], LANES):
        at = slice(left, left + LANES)
        basis3[:, at] = (basis3[:, at].astype(F32) * full).astype(BF16)
    for lo, n in tiles(pick.shape[0]):
        pick_basis_ref[lo : lo + n, :] = dot(pick[lo : lo + n, :], basis3[...]).astype(BF16)
    copy.wait()
    for lo, n in tiles(stiff.shape[0]):
        stiff_place_ref[lo : lo + n, :] = dot(stiff[lo : lo + n, :], place[...]).astype(BF16)
    for lo, n in tiles(pick.shape[0]):
        shared = dot(pick[lo : lo + n, :], stiff_place_ref[...])
        stiff_shared_ref[lo : lo + n, :] = shared.astype(BF16)


def local_products_kernel(row_ref, count_ref, after_ref, inverse_from, local_place_ref,
                          place, inverse, sems):
    copies = bring([(inverse_from, inverse)], sems)
    fill_place(row_ref, place)
    rows = place.shape[0]
    weight = jnp.broadcast_to(1.0 / count_ref[...].astype(F32), (8, rows)).astype(BF16)
    listed = dot(weight, place[...])[0:1]
    for copy in copies:
        copy.wait()
    for lo, n in tiles(rows):
        product = dot(inverse[lo : lo + n, :], place[...]) * listed
        local_place_ref[lo : lo + n, :] = product.astype(BF16)


def shared_products_kernel(local_place_ref, after_ref, pick_ref, weight_ref, local_shared_ref):
    slots = pick_ref.shape[0]
    weight = weight_ref[...].astype(BF16)
    for lo, n in tiles(slots, FINE):
        picked = pick_ref[lo : lo + n, :]
        shared = dot(picked, local_place_ref[...])
        turned = dot(picked, weight)
        for left in range(0, slots, LANES):
            scaled = shared[:, left : left + LANES] * turned
            local_shared_ref[lo : lo + n, left : left + LANES] = scaled.astype(BF16)


def tables_kernel(row_ref, count_ref, basis_ref, after_ref, stiff_from, stiff_place_from,
                  stiff_shared_from,
                  pick_ref, place_ref, weight_ref, basis2_ref, basis3_ref,
                  stiff_ref, stiff_place_ref, stiff_shared_ref, sems):
    copies = bring(
        [
            (stiff_from, stiff_ref),
            (stiff_shared_from, stiff_shared_ref),
            (stiff_place_from, stiff_place_ref),
        ],
        sems,
    )
    fill_pick(row_ref, pick_ref)
    fill_place(row_ref, place_ref)
    weight_ref[...] = weights_of(count_ref)
    fill_basis2(basis_ref, basis2_ref)
    fill_basis3(basis_ref, basis3_ref)
    for copy in copies:
        copy.wait()


def small_kernel(after_ref, first_from, second_from, first_ref, second_ref, sems):
    for copy in bring([(first_from, first_ref), (second_from, second_ref)], sems):
        copy.wait()


def columns_kernel(map_ref, inverse_from, out_ref, turned, rows, sems):
    parts = rows.shape[0]
    width = rows.shape[2]
    copies = bring(
        [(inverse_from.at[:, pl.ds(k * width, width)], rows.at[k]) for k in range(parts)], sems
    )
    for k in range(parts):
        copies[k].wait()
        turned[k * width : (k + 1) * width, :] = rows[k].T
    size = map_ref.shape[0]
    ncl = out_ref.shape[0] // size

    def step(i, _):
        for k in range(ncl):
            out_ref[pl.ds(i * ncl + k, 1), :] = turned[pl.ds(map_ref[i, k], 1), :]
        return 0

    lax.fori_loop(0, size, step, 0)


def coarse_kernel(map_ref, which_ref, got_ref, keep_ref, send_ref, turned, rowed):
    ncl, half = keep_ref.shape
    width = got_ref.shape[1]
    fill = jnp.zeros((turned.shape[1] - ncl, width), F32)
    for t in range(got_ref.shape[0] // ncl):
        block = jnp.concatenate([got_ref[t * ncl : (t + 1) * ncl, :], fill], axis=0)
        turned[t * width : (t + 1) * width, :] = block.T

    size = map_ref.shape[0]

    def step(i, _):
        for c in range(2):
            for k in range(ncl):
                row = turned[pl.ds(map_ref[2 * i + c, k], 1), :]
                rowed[pl.ds(c * half + i * ncl + k, 1), :] = row
        return 0

    lax.fori_loop(0, size // 2, step, 0)
    first = rowed[:half, :].T[:ncl, :]
    second = rowed[half:, :].T[:ncl, :]
    even = which_ref[0] == 0
    keep_ref[...] = jnp.where(even, first, second)
    send_ref[...] = jnp.where(even, second, first)


def stack_kernel(own_ref, other_ref, terms_ref, out_ref, after_ref):
    after_ref[...] = jnp.zeros_like(after_ref)
    ncl = own_ref.shape[0]
    own_high, own_low = cut(own_ref[...])
    other_high, other_low = cut(other_ref[...])
    out_ref[:ncl, :] = own_high
    out_ref[ncl : 2 * ncl, :] = other_high
    out_ref[2 * ncl : 3 * ncl, :] = own_low
    out_ref[3 * ncl :, :] = other_low


def send_terms(terms, scalars, send_ref):
    block = jnp.concatenate([terms, scalars], axis=0)
    rows = block.shape[0]
    for g in range(send_ref.shape[0] // rows):
        send_ref[g * rows : (g + 1) * rows, :] = block


def front(inverse_ref, weight_ref, pick_ref, cat, local_ref, out_ref, cat2):
    for lo, n in tiles(inverse_ref.shape[0], FINE):
        at = slice(lo, lo + n)
        local = halves(dot(inverse_ref[at, :], cat[...]))
        local_ref[at, :] = local
        cat2[at, :] = pair(weight_ref[at, :] * local)
    for lo, n in tiles(pick_ref.shape[0], FINE):
        out_ref[lo : lo + n, :] = halves(dot(pick_ref[lo : lo + n, :], cat2[...]))


def first_kernel(loads_ref, a0, a1, a2, a3, row_ref, count_ref, basis_ref, inverse_from,
                 resid_ref, local_ref, pre_ref, send_ref,
                 cat, arr_cat, place, pick, basis2, inverse, weight, cat2, sems):
    copy = pltpu.make_async_copy(inverse_from, inverse, sems.at[0])
    copy.start()
    fill_place(row_ref, place)
    fill_basis2(basis_ref, basis2)
    weight[...] = weights_of(count_ref)
    ncl, rhs = basis_ref.shape[0], loads_ref.shape[1]
    arrivals((a0, a1, a2, a3), arr_cat)
    terms = jnp.zeros((2 * ncl, 2 * rhs), F32)
    for lo, n in tiles(loads_ref.shape[0]):
        at = slice(lo, lo + n)
        resid = loads_ref[at, :] + halves(dot(place[at, :], arr_cat[...]))
        resid_ref[at, :] = resid
        both = pair(weight[at, :] * resid)
        cat[at, :] = both
        terms += dot(basis2[:, at], both)
    send_terms(three(terms, ncl), jnp.zeros((SCAL, rhs), F32), send_ref)
    fill_pick(row_ref, pick)
    copy.wait()
    front(inverse, weight, pick, cat, local_ref, pre_ref, cat2)


def coarse_solve_kernel(got_ref, g_ref, own_ref, other_ref):
    ncl = g_ref.shape[0] // 4
    rows = ncl + SCAL
    groups = got_ref.shape[0] // rows
    got = got_ref[...].reshape(groups, rows, got_ref.shape[1])
    terms = got[:, :ncl].reshape(groups * ncl, got_ref.shape[1])
    scalars = jnp.sum(got[:, ncl:], axis=0)
    values = three(dot(g_ref[...], pair(terms)), 2 * ncl)
    own_ref[:ncl, :] = values[:ncl]
    own_ref[ncl:, :] = scalars
    other_ref[:ncl, :] = values[ncl:]
    other_ref[ncl:, :] = scalars


def back_kernel(own_ref, other_ref, pre_ref, pick_basis_ref,
                values_ref, scal_ref, out0, out1, out2, out3):
    ncl = own_ref.shape[0] - SCAL
    total = own_ref[...] + other_ref[...]
    scal_ref[...] = total[ncl:]
    high, low = cut(total[:ncl])
    fill = jnp.zeros((values_ref.shape[0] - 3 * ncl, high.shape[1]), BF16)
    values = jnp.concatenate([high, low, high, fill], axis=0)
    values_ref[...] = values
    cap = out0.shape[0]
    for j, out in enumerate((out0, out1, out2, out3)):
        at = slice(j * cap, (j + 1) * cap)
        out[...] = pre_ref[at, :] + dot(pick_basis_ref[at, :], values)


def part_kernel(values_ref, local_ref, weight_ref, basis3_ref, stiff_ref, pick_ref,
                part_ref, image_ref, pre_ref, cat, cat2):
    values = values_ref[...]
    for lo, n in tiles(local_ref.shape[0], FINE):
        at = slice(lo, lo + n)
        part = weight_ref[at, :] * (local_ref[at, :] + dot(basis3_ref[at, :], values))
        part_ref[at, :] = part
        cat[at, :] = pair(part)
    for lo, n in tiles(local_ref.shape[0], FINE):
        at = slice(lo, lo + n)
        image = halves(dot(stiff_ref[at, :], cat[...]))
        image_ref[at, :] = image
        cat2[at, :] = pair(image)
    for lo, n in tiles(pick_ref.shape[0], FINE):
        pre_ref[lo : lo + n, :] = halves(dot(pick_ref[lo : lo + n, :], cat2[...]))


def shared_kernel(a0, a1, a2, a3, pre_ref, stiff_shared_ref,
                  arr_ref, out0, out1, out2, out3):
    arrivals((a0, a1, a2, a3), arr_ref)
    cap = out0.shape[0]
    for j, out in enumerate((out0, out1, out2, out3)):
        at = slice(j * cap, (j + 1) * cap)
        out[...] = pre_ref[at, :] + halves(dot(stiff_shared_ref[at, :], arr_ref[...]))


def completed(ref, at, table_ref, arr_ref):
    return ref[at, :] + halves(dot(table_ref[at, :], arr_ref[...]))


def collect(sums, rhs):
    rows = [jnp.sum(s, axis=0, keepdims=True) for s in sums]
    rows.append(jnp.zeros((SCAL - len(rows), rhs), F32))
    return jnp.concatenate(rows, axis=0)


def start_kernel(part_ref, image_ref, arr_ref, r_ref, place_ref, stiff_place_ref,
                 weight_ref, basis2_ref, inverse_from, local_place_from,
                 u_ref, w_ref, terms_ref, sums_ref,
                 inverse_ref, local_place_ref, sems):
    copies = bring(
        [
            (inverse_from, inverse_ref),
            (local_place_from, local_place_ref),
        ],
        sems,
    )
    ncl = basis2_ref.shape[0] // 2
    rhs = r_ref.shape[1]
    terms = jnp.zeros((2 * ncl, 2 * rhs), F32)
    sums = [jnp.zeros((8, rhs), F32) for _ in range(2)]
    for lo, n in tiles(r_ref.shape[0]):
        at = slice(lo, lo + n)
        u = completed(part_ref, at, place_ref, arr_ref)
        w = completed(image_ref, at, stiff_place_ref, arr_ref)
        u_ref[at, :] = u
        w_ref[at, :] = w
        weight = weight_ref[at, :]
        sums[0] += folded(weight * u * r_ref[at, :])
        sums[1] += folded(u * w)
        terms += dot(basis2_ref[:, at], pair(weight * w))
    terms_ref[...] = three(terms, ncl)
    sums_ref[...] = collect(sums, rhs)
    for copy in copies:
        copy.wait()


def second_kernel(part_ref, image_ref, arr_ref, scal_ref, r_ref, u_ref, w_ref,
                  place_ref, stiff_place_ref, weight_ref, basis2_ref,
                  m_ref, z_ref, x1_ref, r1_ref, u1_ref, w1_ref, terms_ref, sums_ref):
    ncl = basis2_ref.shape[0] // 2
    rhs = r_ref.shape[1]
    alpha = scal_ref[0:1, :] / scal_ref[1:2, :]
    terms = jnp.zeros((2 * ncl, 2 * rhs), F32)
    sums = [jnp.zeros((8, rhs), F32) for _ in range(4)]
    for lo, n in tiles(r_ref.shape[0]):
        at = slice(lo, lo + n)
        m = completed(part_ref, at, place_ref, arr_ref)
        z = completed(image_ref, at, stiff_place_ref, arr_ref)
        m_ref[at, :] = m
        z_ref[at, :] = z
        weight = weight_ref[at, :]
        p, s = u_ref[at, :], w_ref[at, :]
        x1_ref[at, :] = alpha * p
        r1 = r_ref[at, :] - alpha * s
        u1 = p - alpha * m
        w1 = s - alpha * z
        r1_ref[at, :] = r1
        u1_ref[at, :] = u1
        w1_ref[at, :] = w1
        left = weight * s - alpha * z
        weighted = weight * u1
        for k, term in enumerate((weighted * r1, u1 * left, weighted * s, p * left)):
            sums[k] += folded(term)
        terms += dot(basis2_ref[:, at], pair(weight * w1))
    terms_ref[...] = three(terms, ncl)
    sums_ref[...] = collect(sums, rhs)


def terms_kernel(a0, a1, a2, a3, terms_ref, sums_ref, basis_place_ref, *refs):
    *scal, arr_ref, send_ref = refs
    ncl = terms_ref.shape[0]
    arrivals((a0, a1, a2, a3), arr_ref)
    added = three(dot(basis_place_ref[...], arr_ref[...]), ncl)
    if scal:
        added *= -scal[0][0:1, :] / scal[0][1:2, :]
    send_terms(terms_ref[...] + added, sums_ref[...], send_ref)


def local_part_kernel(w_ref, weight_ref, inverse_ref, pick_ref, local_ref, pre_ref, cat, cat2):
    for lo, n in tiles(w_ref.shape[0], FINE):
        at = slice(lo, lo + n)
        cat[at, :] = pair(weight_ref[at, :] * w_ref[at, :])
    front(inverse_ref, weight_ref, pick_ref, cat, local_ref, pre_ref, cat2)


def local_shared_kernel(pre_ref, arr_ref, after_ref, local_shared_ref, scal_ref, out_ref):
    factor = -scal_ref[0:1, :] / scal_ref[1:2, :]
    for lo, n in tiles(pre_ref.shape[0]):
        at = slice(lo, lo + n)
        came = halves(dot(local_shared_ref[at, :], arr_ref[...]))
        out_ref[at, :] = pre_ref[at, :] + factor * came


def local_again_kernel(pre_ref, arr_ref, after_ref, local_place_ref, weight_ref, pick_ref,
                       out_ref, cat):
    for lo, n in tiles(weight_ref.shape[0], FINE):
        at = slice(lo, lo + n)
        came = halves(dot(local_place_ref[at, :], arr_ref[...]))
        cat[at, :] = pair(weight_ref[at, :] * came)
    for lo, n in tiles(pre_ref.shape[0], FINE):
        at = slice(lo, lo + n)
        out_ref[at, :] = pre_ref[at, :] + halves(dot(pick_ref[at, :], cat[...]))


def complete_kernel(w_part_ref, local_part_ref, arr_ref, after_ref, place_ref, local_place_ref,
                    *refs):
    *more, w_ref, local_ref = refs
    if more:
        scal_ref, z_part_ref, z_ref = more
        factor = -scal_ref[0:1, :] / scal_ref[1:2, :]
    for lo, n in tiles(w_ref.shape[0], FINE):
        at = slice(lo, lo + n)
        came = halves(dot(place_ref[at, :], arr_ref[...]))
        local = halves(dot(local_place_ref[at, :], arr_ref[...]))
        if more:
            z_ref[at, :] = z_part_ref[at, :] + came
            came, local = factor * came, factor * local
        w_ref[at, :] = w_part_ref[at, :] + came
        local_ref[at, :] = local_part_ref[at, :] + local


def step_scalars(before, now):
    beta = now[0:1, :] / before[0:1, :]
    energy = now[1:2, :] + beta * (now[2:3, :] + now[3:4, :]) + beta * beta * before[1:2, :]
    return beta, now[0:1, :] / energy, energy


def third_kernel(part_ref, image_ref, arr_ref, before_ref, scal_ref,
                 x1_ref, r1_ref, u1_ref, w1_ref, p_ref, s_ref, q_ref, z_ref,
                 place_ref, stiff_place_ref, weight_ref,
                 send_ref, state_ref, x2_ref, r2_ref, u2_ref, half_ref, p1_ref, s1_ref):
    rhs = r1_ref.shape[1]
    beta, alpha, energy = step_scalars(before_ref[...], scal_ref[...])
    sums = [jnp.zeros((8, rhs), F32) for _ in range(4)]
    for lo, n in tiles(r1_ref.shape[0]):
        at = slice(lo, lo + n)
        m = completed(part_ref, at, place_ref, arr_ref)
        image = completed(image_ref, at, stiff_place_ref, arr_ref)
        p1 = u1_ref[at, :] + beta * p_ref[at, :]
        s1 = w1_ref[at, :] + beta * s_ref[at, :]
        q1 = m + beta * q_ref[at, :]
        r2 = r1_ref[at, :] - alpha * s1
        u2 = u1_ref[at, :] - alpha * q1
        half = w1_ref[at, :] - (alpha * beta) * z_ref[at, :]
        weight = weight_ref[at, :]
        left = weight * half - alpha * image
        weighted = weight * u2
        for k, term in enumerate((weighted * r2, u2 * left, weighted * s1, p1 * left)):
            sums[k] += folded(term)
        x2_ref[at, :] = x1_ref[at, :] + alpha * p1
        r2_ref[at, :] = r2
        u2_ref[at, :] = u2
        half_ref[at, :] = half - alpha * image
        p1_ref[at, :] = p1
        s1_ref[at, :] = s1
    block = collect(sums, rhs)
    for g in range(send_ref.shape[0] // SCAL):
        send_ref[g * SCAL : (g + 1) * SCAL, :] = block
    state_ref[...] = jnp.concatenate(
        [scal_ref[0:1, :], energy, alpha, jnp.zeros((SCAL - 3, rhs), F32)], axis=0
    )


def last_kernel(state_ref, got_ref, a0, a1, a2, a3, place_ref,
                x2, u2, p1, r2, half, s1,
                x3_to, r3_to, arr_cat, x3, r3, out_sems):
    state = state_ref[...]
    now = jnp.sum(got_ref[...].reshape(-1, SCAL, got_ref.shape[1]), axis=0)
    beta, alpha, _ = step_scalars(state, now)
    old = state[2:3, :]
    arrivals((a0, a1, a2, a3), arr_cat)
    outs = []
    for i, (lo, n) in enumerate(tiles(r2.shape[0])):
        at = slice(lo, lo + n)
        x3[at, :] = x2[at, :] + alpha * (u2[at, :] + beta * p1[at, :])
        w2 = half[at, :] - old * halves(dot(place_ref[at, :], arr_cat[...]))
        r3[at, :] = r2[at, :] - alpha * (w2 + beta * s1[at, :])
        rows = pl.ds(lo, n)
        outs += bring(
            [(x3.at[rows, :], x3_to.at[rows, :]), (r3.at[rows, :], r3_to.at[rows, :])],
            out_sems.at[i],
        )
    for copy in outs:
        copy.wait()


def body(
    stiffness, local_inverse, coarse_basis, loads, counts, shared_rows, coarse_map, coarse_inverse
):
    size = lax.axis_size("sub")
    me = lax.axis_index("sub")
    rows, rhs = loads.shape[1:]
    ncl = coarse_basis.shape[1]
    slots, cap = shared_rows.shape[1:]
    order = coarse_inverse.shape[1]
    lists = slots * cap
    stiff, inverse = aside(stiffness[0], local_inverse[0])

    def partner(distance, parity):
        def of(i):
            up = (i // distance) % 2 == parity
            return (i + distance if up else i - distance) % size

        return [(i, of(i)) for i in range(size)]

    inside = partner(1, 0)
    swaps = [inside, partner(1, 1), partner(STRIDE, 0), partner(STRIDE, 1)]
    swaps = [swaps[j] for j in ORDER]

    def exchange(outs):
        return [lax.ppermute(out, "sub", swap) for out, swap in zip(outs, swaps)]

    cores = [[2 * i + c for i in range(size // 2)] for c in range(2)]
    groups = size // 2
    block = ncl + SCAL

    fields = (rows, rhs)
    out4 = [far((cap, rhs))] * 4
    wide = pltpu.VMEM((rows, 2 * rhs), BF16)
    wide_arr = pltpu.VMEM((lists, 2 * rhs), BF16)
    place_like = pltpu.VMEM((rows, lists), BF16)
    pick_like = pltpu.VMEM((lists, rows), BF16)
    basis = coarse_basis[0]
    (loads_aside,) = aside(loads[0])

    listed, *outs = call(
        loads_kernel,
        "loads",
        (shared_rows[0], loads_aside),
        [far((1, lists), jnp.int32)] + out4,
        [pick_like, wide, pltpu.VMEM(fields, F32), pltpu.SemaphoreType.DMA((1,))],
        {1: ASPEC},
    )
    arrived = exchange(outs)
    own_map = jnp.pad(coarse_map, ((0, 0), (0, -ncl % LANES)))
    maps = jnp.broadcast_to(own_map, (size, own_map.shape[1]))
    maps = lax.all_to_all(maps, "sub", 0, 0, tiled=True)
    maps, *arrived = lax.optimization_barrier((maps, *arrived))


    (picked,) = call(
        columns_kernel,
        "coarse_columns",
        (maps, *aside(coarse_inverse)),
        [far((size * ncl, coarse_inverse.shape[0]))],
        [
            pltpu.VMEM((order, coarse_inverse.shape[0]), F32),
            pltpu.VMEM((4, coarse_inverse.shape[0], order // 4), F32),
            pltpu.SemaphoreType.DMA((4,)),
        ],
        {0: SSPEC, 1: ASPEC},
        mib=30,
    )
    mine_rows = lax.all_to_all(picked, "sub", 0, 0, tiled=True)

    r0, local, pre, send = call(
        first_kernel,
        "residual_and_terms",
        (loads[0], *arrived, listed, counts, basis, inverse),
        [away(fields), away(fields), away((lists, rhs)), far((groups * block, rhs))],
        [
            wide,
            wide_arr,
            place_like,
            pick_like,
            pltpu.VMEM((2 * ncl, rows), BF16),
            pltpu.VMEM((rows, rows), BF16),
            pltpu.VMEM(fields, F32),
            wide,
            pltpu.SemaphoreType.DMA((1,)),
        ],
        {8: ASPEC},
        us=6,
        mib=30,
    )
    products = call(
        products_kernel,
        "products",
        (listed, counts, basis, stiff),
        [
            away((rows, lists), BF16),
            away((lists, lists), BF16),
            away((2 * ncl, lists), BF16),
            away((lists, 2 * LANES), BF16),
        ],
        [
            pick_like,
            place_like,
            pltpu.VMEM((rows, rows), BF16),
            pltpu.VMEM((2 * ncl, rows), BF16),
            pltpu.VMEM((rows, 2 * LANES), BF16),
            pltpu.SemaphoreType.DMA((1,)),
        ],
        {3: ASPEC},
        us=10,
        mib=30,
    )
    r0, local, pre = aside(r0, local, pre)

    keep, pass_on = call(
        coarse_kernel,
        "coarse_block",
        (maps, (me % 2).reshape(1), mine_rows),
        [far((ncl, groups * ncl)), far((ncl, groups * ncl))],
        [
            pltpu.VMEM((order, LANES), F32),
            pltpu.VMEM((size * ncl, LANES), F32),
        ],
        {0: SSPEC, 1: SSPEC},
        mib=30,
    )
    passed = lax.ppermute(pass_on, "sub", inside)

    def share(send):
        return lax.all_to_all(send, "sub", 0, 0, tiled=True, axis_index_groups=cores)

    send, *products = lax.optimization_barrier((send, *products))
    terms = share(send)
    local_products = call(
        local_products_kernel,
        "local_products",
        (listed, counts, send, inverse),
        [away((rows, lists), BF16)],
        [place_like, pltpu.VMEM((rows, rows), BF16), pltpu.SemaphoreType.DMA((1,))],
        {2: ASPEC, 3: ASPEC},
        us=10,
        mib=30,
    )
    terms, *local_products = lax.optimization_barrier((terms, *local_products))
    local_products = aside(*local_products)
    coarse, after = call(
        stack_kernel,
        "coarse_addends",
        (keep, passed, terms),
        [near((4 * ncl, groups * ncl), BF16), far((SCAL, LANES))],
    )
    stiff_place, stiff_shared, basis_place, pick_basis = aside(*products)
    tables = held(*call(
        tables_kernel,
        "tables",
        (listed, counts, basis, after, stiff, stiff_place, stiff_shared),
        [
            near((lists, rows), BF16),
            near((rows, lists), BF16),
            near(fields),
            near((2 * ncl, rows), BF16),
            near((rows, 2 * LANES), BF16),
            near((rows, rows), BF16),
            near((rows, lists), BF16),
            near((lists, lists), BF16),
        ],
        [pltpu.SemaphoreType.DMA((3,))],
        {4: ASPEC, 5: ASPEC, 6: ASPEC},
        us=5,
    ))
    pick, place, weight, basis2, basis3, stiff, stiff_place, stiff_shared = tables
    tables = []
    (coarse,) = held(coarse)

    def correct(terms, pre, bring_in=None):
        own, other = call(
            coarse_solve_kernel,
            "coarse_solve",
            (terms, coarse),
            [far((block, rhs)), far((block, rhs))],
            us=1,
        )
        came = lax.ppermute(other, "sub", inside)
        if bring_in:
            small.extend(bring_in(own))
        values, scal, *outs = call(
            back_kernel,
            "coarse_back",
            (own, came, pre(own), small[0]),
            [near((2 * LANES, rhs), BF16), far((SCAL, rhs))] + out4,
            us=1,
        )
        return *held(values), scal, exchange(outs)

    small = []

    def bring_small(own):
        return held(*call(
            small_kernel,
            "small_tables",
            (own, pick_basis, basis_place),
            [near(pick_basis.shape, BF16), near(basis_place.shape, BF16)],
            [pltpu.SemaphoreType.DMA((2,))],
            {1: ASPEC, 2: ASPEC},
            us=1,
        ))

    def operate(values, local, arrived, *beside):
        part, image, pre = held(*call(
            part_kernel,
            "field_part",
            (values, local, weight, basis3, stiff, pick),
            [near(fields), near(fields), near((lists, rhs))],
            [wide, wide],
            us=3,
        ))
        if beside:
            pre, table = held(*lax.optimization_barrier((pre, *beside)))
            tables.append(table)
        arr, *outs = call(
            shared_kernel,
            "image_shared",
            (*arrived, pre, stiff_shared),
            [near((lists, 2 * rhs), BF16)] + out4,
            us=1,
        )
        return part, image, *held(arr), exchange(outs)

    def share_terms(arrived, terms, sums, *scal):
        arr, send = call(
            terms_kernel,
            "terms",
            (*arrived, terms, sums, small[1], *scal),
            [near((lists, 2 * rhs), BF16), far((groups * block, rhs))],
            us=1,
        )
        return *held(arr), share(send)

    def local_part(w):
        return held(*call(
            local_part_kernel,
            "local_part",
            (w, weight, inverse, pick),
            [near(fields), near((lists, rhs))],
            [wide, wide],
            us=3,
        ))

    def local_shared(pre, arr, scal):
        def of(own):
            return held(*call(
                local_shared_kernel,
                "local_shared",
                (pre, arr, own, shared_table, scal),
                [near((lists, rhs))],
                us=1,
            ))[0]

        return of

    def local_again(pre, arr):
        def of(own):
            return held(*call(
                local_again_kernel,
                "local_again",
                (pre, arr, own, local_place, weight, pick),
                [near((lists, rhs))],
                [wide],
                us=1,
            ))[0]

        return of

    def complete(w, local, arr, after, *more):
        return held(*call(
            complete_kernel,
            "complete",
            (w, local, arr, after, place, local_place, *more),
            [near(fields)] * (3 if more else 2),
            us=2,
        ))

    values, _, arrived = correct(terms, lambda own: pre, bring_small)
    part, image, arr, arrived = operate(values, local, arrived)
    u0, w0, terms, sums, inverse, local_place = held(*call(
        start_kernel,
        "start",
        (part, image, arr, r0, place, stiff_place, weight, basis2, inverse, *local_products),
        [near(fields), near(fields), near((ncl, rhs)), near((SCAL, rhs))]
        + [near((rows, rows), BF16), near((rows, lists), BF16)],
        [pltpu.SemaphoreType.DMA((2,))],
        {8: ASPEC, 9: ASPEC},
        us=3,
    ))
    local, pre = local_part(w0)
    terms, pre = held(*lax.optimization_barrier((terms, pre)))
    arr, terms = share_terms(arrived, terms, sums)
    values, scal0, arrived = correct(terms, local_again(pre, arr))
    w0, local = complete(w0, local, arr, values)
    (shared_table,) = held(*call(
        shared_products_kernel,
        "shared_products",
        (local_place, values, pick, weight),
        [near((lists, lists), BF16)],
        us=4,
    ))

    part, image, arr, arrived = operate(values, local, arrived, shared_table)
    (shared_table,) = tables
    m0, z0, x1, r1, u1, w1, terms, sums = held(*call(
        second_kernel,
        "first_update",
        (part, image, arr, scal0, r0, u0, w0, place, stiff_place, weight, basis2),
        [near(fields)] * 6 + [near((ncl, rhs)), near((SCAL, rhs))],
        us=4,
    ))
    local, pre = local_part(w1)
    terms, pre = held(*lax.optimization_barrier((terms, pre)))
    arr, terms = share_terms(arrived, terms, sums, scal0)
    values, scal1, arrived = correct(terms, local_shared(pre, arr, scal0))
    z0, w1, local = complete(w1, local, arr, values, scal0, z0)

    part, image, arr, arrived = operate(values, local, arrived)
    pieces = len(tiles(rows))
    send, state, *news = call(
        third_kernel,
        "second_update",
        (part, image, arr, scal0, scal1, x1, r1, u1, w1, u0, w0, m0, z0)
        + (place, stiff_place, weight),
        [far((size * SCAL, rhs)), far((SCAL, rhs))] + [near(fields)] * 6,
        us=4,
    )
    x2, r2, u2, half, p1, s1 = held(*news)
    send, *arrived = lax.optimization_barrier((send, *arrived))
    sums = lax.all_to_all(send, "sub", 0, 0, tiled=True)
    sums, *arrived = lax.optimization_barrier((sums, *arrived))
    x3, r3 = call(
        last_kernel,
        "last_update",
        (state, sums, *arrived, place, x2, u2, p1, r2, half, s1),
        [far(fields), far(fields)],
        [wide_arr, pltpu.VMEM(fields, F32), pltpu.VMEM(fields, F32)]
        + [pltpu.SemaphoreType.DMA((pieces, 2))],
        sent=range(2),
    )
    return (x3[None], r3[None])


def solution(mesh):
    placed = (
        P("sub", None, None),
        P("sub", None, None),
        P("sub", None, None),
        P("sub", None, None),
        P("sub", None),
        P("sub", None, None),
        P("sub", None),
        P("sub", None),
    )
    return jax.shard_map(
        body,
        mesh=mesh,
        in_specs=placed,
        out_specs=(P("sub", None, None), P("sub", None, None)),
        check_vma=False,
    )
```

```python
import jax
import jax.numpy as jnp
from jax import lax
from jax.experimental import pallas as pl
from jax.experimental.pallas import tpu as pltpu
from jax.sharding import PartitionSpec as P

STRIDE = 8
F32 = jnp.float32
BF16 = jnp.bfloat16
TILE = 512
FINE = 256
SCAL = 8
ORDER = (3, 1, 2, 0)
LANES = 128

VSPEC = pl.BlockSpec(memory_space=pltpu.VMEM)
SSPEC = pl.BlockSpec(memory_space=pltpu.SMEM)
ASPEC = pl.BlockSpec(memory_space=pltpu.HBM)


def near(shape, dtype=F32):
    return pltpu.VMEM(shape, dtype)


def far(shape, dtype=F32):
    return jax.ShapeDtypeStruct(shape, dtype)


def away(shape, dtype=F32):
    return pltpu.HBM(shape, dtype)


def held(*arrays):
    return tuple(pltpu.with_memory_space_constraint(a, pltpu.VMEM) for a in arrays)


def aside(*arrays):
    return tuple(pltpu.with_memory_space_constraint(a, pltpu.HBM) for a in arrays)


def call(kernel, name, args, outs, scratch=(), specs=None, us=2, mib=16, sent=()):
    specs = specs or {}
    return pl.pallas_call(
        kernel,
        name=name,
        out_shape=tuple(outs),
        in_specs=[specs.get(i, VSPEC) for i in range(len(args))],
        out_specs=tuple(ASPEC if i in sent else VSPEC for i in range(len(outs))),
        scratch_shapes=list(scratch),
        compiler_params=pltpu.CompilerParams(vmem_limit_bytes=mib * 1024 * 1024),
        cost_estimate=pl.CostEstimate(
            flops=0, bytes_accessed=us * 3_000_000, transcendentals=0
        ),
    )(*args)


def cut(x):
    high = x.astype(BF16)
    return high, (x - high.astype(F32)).astype(BF16)


def pair(x):
    return jnp.concatenate(cut(x), axis=1)


def halves(product):
    half = product.shape[1] // 2
    return product[:, :half] + product[:, half:]


def three(product, rows):
    half = product.shape[1] // 2
    return product[:rows, :half] + product[:rows, half:] + product[rows : 2 * rows, :half]


def dot(a, b):
    return jnp.dot(a, b, preferred_element_type=F32)


def tiles(total, step=TILE):
    step = min(step, total)
    return [(lo, min(step, total - lo)) for lo in range(0, total, step)]


def folded(x):
    return jnp.sum(x.reshape(-1, 8, x.shape[-1]), axis=0)


def pick_out(pick_ref, cat_ref, out_refs):
    cap = out_refs[0].shape[0]
    for j, out in enumerate(out_refs):
        out[...] = halves(dot(pick_ref[j * cap : (j + 1) * cap, :], cat_ref[...]))


def arrivals(arrived_refs, arr_cat):
    cap = arrived_refs[0].shape[0]
    for j, ref in enumerate(arrived_refs):
        arr_cat[j * cap : (j + 1) * cap, :] = pair(ref[...])


def bring(pairs, sems):
    copies = [pltpu.make_async_copy(*p, sems.at[i]) for i, p in enumerate(pairs)]
    for copy in copies:
        copy.start()
    return copies


def each(total, step, work):
    def one(i, carry):
        work(pl.multiple_of(i * step, step))
        return carry

    lax.fori_loop(0, total // step, one, 0)


def fill_pick(row_ref, pick_ref):
    slots, rows = pick_ref.shape

    def some(lo):
        listed = row_ref[:, pl.ds(lo, LANES)].astype(F32)
        entries = jnp.broadcast_to(listed, (LANES, LANES)).T
        for left in range(0, rows, LANES):
            at = left + lax.broadcasted_iota(jnp.int32, (LANES, LANES), 1)
            same = jnp.where(at.astype(F32) == entries, 1.0, 0.0)
            pick_ref[pl.ds(lo, LANES), left : left + LANES] = same.astype(BF16)

    each(slots, LANES, some)


def fill_place(row_ref, place_ref):
    rows, slots = place_ref.shape

    def some(lo):
        at = lo + lax.broadcasted_iota(jnp.int32, (LANES, slots), 0)
        same = jnp.where(at == row_ref[...], 1.0, 0.0)
        place_ref[pl.ds(lo, LANES), :] = same.astype(BF16)

    each(rows, LANES, some)


def weights_of(count_ref):
    rows = count_ref.shape[1]
    return jnp.broadcast_to(1.0 / count_ref[...].astype(F32), (LANES, rows)).T


def fill_basis2(basis_ref, basis2_ref):
    ncl = basis_ref.shape[0]
    high, low = cut(basis_ref[...])
    basis2_ref[:ncl, :] = high
    basis2_ref[ncl:, :] = low


def loads_kernel(rows_ref, loads_from, listed_ref, out0, out1, out2, out3, pick, cat, loads, sems):
    copies = bring([(loads_from, loads)], sems)
    me = lax.axis_index("sub")
    one = me % 2 == 0
    far_one = (me // STRIDE) % 2 == 0
    given = [rows_ref[k : k + 1, :] for k in range(4)]
    lists = [
        jnp.where(one, given[0], given[1]),
        jnp.where(one, given[1], given[0]),
        jnp.where(far_one, given[2], given[3]),
        jnp.where(far_one, given[3], given[2]),
    ]
    listed_ref[...] = jnp.concatenate([lists[j] for j in ORDER], axis=1)
    fill_pick(listed_ref, pick)
    for copy in copies:
        copy.wait()
    for lo, n in tiles(loads.shape[0]):
        cat[lo : lo + n, :] = pair(loads[lo : lo + n, :])
    pick_out(pick, cat, (out0, out1, out2, out3))


def fill_basis3(basis_ref, basis3_ref):
    ncl, rows = basis_ref.shape
    high, low = cut(basis_ref[...])
    high, low = high.astype(F32), low.astype(F32)
    fill = jnp.zeros((basis3_ref.shape[1] - 3 * ncl, rows), F32)
    basis3_ref[...] = jnp.concatenate([high, high, low, fill], axis=0).T.astype(BF16)


def products_kernel(row_ref, count_ref, basis_ref, stiff_from,
                    stiff_place_ref, stiff_shared_ref, basis_place_ref, pick_basis_ref,
                    pick, place, stiff, basis2, basis3, sems):
    copy = pltpu.make_async_copy(stiff_from, stiff, sems.at[0])
    copy.start()
    fill_pick(row_ref, pick)
    fill_place(row_ref, place)
    weight = 1.0 / count_ref[...].astype(F32)
    fill_basis2(basis_ref, basis2)
    scaled = basis2[...].astype(F32) * weight
    basis_place_ref[...] = dot(scaled.astype(BF16), place[...]).astype(BF16)
    fill_basis3(basis_ref, basis3)
    full = weights_of(count_ref)
    for left in range(0, basis3.shape[1], LANES):
        at = slice(left, left + LANES)
        basis3[:, at] = (basis3[:, at].astype(F32) * full).astype(BF16)
    for lo, n in tiles(pick.shape[0]):
        pick_basis_ref[lo : lo + n, :] = dot(pick[lo : lo + n, :], basis3[...]).astype(BF16)
    copy.wait()

    def product(lo):
        at = pl.ds(lo, FINE)
        stiff_place_ref[at, :] = dot(stiff[at, :], place[...]).astype(BF16)

    def shared(lo):
        at = pl.ds(lo, FINE)
        stiff_shared_ref[at, :] = dot(pick[at, :], stiff_place_ref[...]).astype(BF16)

    each(stiff.shape[0], FINE, product)
    each(pick.shape[0], FINE, shared)


def local_products_kernel(row_ref, count_ref, after_ref, inverse_from, local_place_ref,
                          place, inverse, sems):
    copies = bring([(inverse_from, inverse)], sems)
    fill_place(row_ref, place)
    rows = place.shape[0]
    weight = jnp.broadcast_to(1.0 / count_ref[...].astype(F32), (8, rows)).astype(BF16)
    listed = dot(weight, place[...])[0:1]
    for copy in copies:
        copy.wait()

    def product(lo):
        at = pl.ds(lo, FINE)
        local_place_ref[at, :] = (dot(inverse[at, :], place[...]) * listed).astype(BF16)

    each(rows, FINE, product)


def shared_products_kernel(local_place_ref, after_ref, pick_ref, weight_ref, local_shared_ref):
    slots = pick_ref.shape[0]
    weight = weight_ref[...].astype(BF16)

    def some(lo):
        at = pl.ds(lo, FINE)
        shared = dot(pick_ref[at, :], local_place_ref[...])
        turned = dot(pick_ref[at, :], weight)
        for left in range(0, slots, LANES):
            scaled = shared[:, left : left + LANES] * turned
            local_shared_ref[at, left : left + LANES] = scaled.astype(BF16)

    each(slots, FINE, some)


def tables_kernel(row_ref, count_ref, basis_ref, after_ref, stiff_from, stiff_place_from,
                  stiff_shared_from,
                  pick_ref, place_ref, weight_ref, basis2_ref, basis3_ref,
                  stiff_ref, stiff_place_ref, stiff_shared_ref, sems):
    copies = bring(
        [
            (stiff_from, stiff_ref),
            (stiff_shared_from, stiff_shared_ref),
            (stiff_place_from, stiff_place_ref),
        ],
        sems,
    )
    fill_pick(row_ref, pick_ref)
    fill_place(row_ref, place_ref)
    weight_ref[...] = weights_of(count_ref)
    fill_basis2(basis_ref, basis2_ref)
    fill_basis3(basis_ref, basis3_ref)
    for copy in copies:
        copy.wait()


def small_kernel(after_ref, first_from, second_from, first_ref, second_ref, sems):
    for copy in bring([(first_from, first_ref), (second_from, second_ref)], sems):
        copy.wait()


def columns_kernel(map_ref, inverse_from, out_ref, turned, rows, sems):
    parts = rows.shape[0]
    width = rows.shape[2]
    copies = bring(
        [(inverse_from.at[:, pl.ds(k * width, width)], rows.at[k]) for k in range(parts)], sems
    )
    for k in range(parts):
        copies[k].wait()
        turned[k * width : (k + 1) * width, :] = rows[k].T
    size = map_ref.shape[0]
    ncl = out_ref.shape[0] // size

    def step(i, _):
        for k in range(ncl):
            out_ref[pl.ds(i * ncl + k, 1), :] = turned[pl.ds(map_ref[i, k], 1), :]
        return 0

    lax.fori_loop(0, size, step, 0)


def coarse_kernel(map_ref, which_ref, got_ref, keep_ref, send_ref, turned, rowed):
    ncl, half = keep_ref.shape
    width = got_ref.shape[1]
    fill = jnp.zeros((turned.shape[1] - ncl, width), F32)
    for t in range(got_ref.shape[0] // ncl):
        block = jnp.concatenate([got_ref[t * ncl : (t + 1) * ncl, :], fill], axis=0)
        turned[t * width : (t + 1) * width, :] = block.T

    size = map_ref.shape[0]

    def step(i, _):
        for c in range(2):
            for k in range(ncl):
                row = turned[pl.ds(map_ref[2 * i + c, k], 1), :]
                rowed[pl.ds(c * half + i * ncl + k, 1), :] = row
        return 0

    lax.fori_loop(0, size // 2, step, 0)
    first = rowed[:half, :].T[:ncl, :]
    second = rowed[half:, :].T[:ncl, :]
    even = which_ref[0] == 0
    keep_ref[...] = jnp.where(even, first, second)
    send_ref[...] = jnp.where(even, second, first)


def stack_kernel(own_ref, other_ref, terms_ref, out_ref, after_ref):
    after_ref[...] = jnp.zeros_like(after_ref)
    ncl = own_ref.shape[0]
    own_high, own_low = cut(own_ref[...])
    other_high, other_low = cut(other_ref[...])
    out_ref[:ncl, :] = own_high
    out_ref[ncl : 2 * ncl, :] = other_high
    out_ref[2 * ncl : 3 * ncl, :] = own_low
    out_ref[3 * ncl :, :] = other_low


def send_terms(terms, scalars, send_ref):
    block = jnp.concatenate([terms, scalars], axis=0)
    rows = block.shape[0]
    for g in range(send_ref.shape[0] // rows):
        send_ref[g * rows : (g + 1) * rows, :] = block


def front(inverse_ref, weight_ref, pick_ref, cat, local_ref, out_ref, cat2):
    for lo, n in tiles(inverse_ref.shape[0], FINE):
        at = slice(lo, lo + n)
        local = halves(dot(inverse_ref[at, :], cat[...]))
        local_ref[at, :] = local
        cat2[at, :] = pair(weight_ref[at, :] * local)
    for lo, n in tiles(pick_ref.shape[0], FINE):
        out_ref[lo : lo + n, :] = halves(dot(pick_ref[lo : lo + n, :], cat2[...]))


def first_kernel(loads_ref, a0, a1, a2, a3, row_ref, count_ref, basis_ref, inverse_from,
                 resid_ref, local_ref, pre_ref, send_ref,
                 cat, arr_cat, place, pick, basis2, inverse, weight, cat2, sems):
    copy = pltpu.make_async_copy(inverse_from, inverse, sems.at[0])
    copy.start()
    fill_place(row_ref, place)
    fill_basis2(basis_ref, basis2)
    weight[...] = weights_of(count_ref)
    ncl, rhs = basis_ref.shape[0], loads_ref.shape[1]
    arrivals((a0, a1, a2, a3), arr_cat)
    terms = jnp.zeros((2 * ncl, 2 * rhs), F32)
    for lo, n in tiles(loads_ref.shape[0]):
        at = slice(lo, lo + n)
        resid = loads_ref[at, :] + halves(dot(place[at, :], arr_cat[...]))
        resid_ref[at, :] = resid
        both = pair(weight[at, :] * resid)
        cat[at, :] = both
        terms += dot(basis2[:, at], both)
    send_terms(three(terms, ncl), jnp.zeros((SCAL, rhs), F32), send_ref)
    fill_pick(row_ref, pick)
    copy.wait()
    front(inverse, weight, pick, cat, local_ref, pre_ref, cat2)


def coarse_solve_kernel(got_ref, g_ref, own_ref, other_ref):
    ncl = g_ref.shape[0] // 4
    rows = ncl + SCAL
    groups = got_ref.shape[0] // rows
    got = got_ref[...].reshape(groups, rows, got_ref.shape[1])
    terms = got[:, :ncl].reshape(groups * ncl, got_ref.shape[1])
    scalars = jnp.sum(got[:, ncl:], axis=0)
    values = three(dot(g_ref[...], pair(terms)), 2 * ncl)
    own_ref[:ncl, :] = values[:ncl]
    own_ref[ncl:, :] = scalars
    other_ref[:ncl, :] = values[ncl:]
    other_ref[ncl:, :] = scalars


def back_kernel(own_ref, other_ref, pre_ref, pick_basis_ref,
                values_ref, scal_ref, out0, out1, out2, out3):
    ncl = own_ref.shape[0] - SCAL
    total = own_ref[...] + other_ref[...]
    scal_ref[...] = total[ncl:]
    high, low = cut(total[:ncl])
    fill = jnp.zeros((values_ref.shape[0] - 3 * ncl, high.shape[1]), BF16)
    values = jnp.concatenate([high, low, high, fill], axis=0)
    values_ref[...] = values
    cap = out0.shape[0]
    for j, out in enumerate((out0, out1, out2, out3)):
        at = slice(j * cap, (j + 1) * cap)
        out[...] = pre_ref[at, :] + dot(pick_basis_ref[at, :], values)


def part_kernel(values_ref, local_ref, weight_ref, basis3_ref, stiff_ref, pick_ref,
                part_ref, image_ref, pre_ref, cat, cat2):
    values = values_ref[...]
    for lo, n in tiles(local_ref.shape[0], FINE):
        at = slice(lo, lo + n)
        part = weight_ref[at, :] * (local_ref[at, :] + dot(basis3_ref[at, :], values))
        part_ref[at, :] = part
        cat[at, :] = pair(part)
    for lo, n in tiles(local_ref.shape[0], FINE):
        at = slice(lo, lo + n)
        image = halves(dot(stiff_ref[at, :], cat[...]))
        image_ref[at, :] = image
        cat2[at, :] = pair(image)
    for lo, n in tiles(pick_ref.shape[0], FINE):
        pre_ref[lo : lo + n, :] = halves(dot(pick_ref[lo : lo + n, :], cat2[...]))


def shared_kernel(a0, a1, a2, a3, pre_ref, stiff_shared_ref,
                  arr_ref, out0, out1, out2, out3):
    arrivals((a0, a1, a2, a3), arr_ref)
    cap = out0.shape[0]
    for j, out in enumerate((out0, out1, out2, out3)):
        at = slice(j * cap, (j + 1) * cap)
        out[...] = pre_ref[at, :] + halves(dot(stiff_shared_ref[at, :], arr_ref[...]))


def completed(ref, at, table_ref, arr_ref):
    return ref[at, :] + halves(dot(table_ref[at, :], arr_ref[...]))


def collect(sums, rhs):
    rows = [jnp.sum(s, axis=0, keepdims=True) for s in sums]
    rows.append(jnp.zeros((SCAL - len(rows), rhs), F32))
    return jnp.concatenate(rows, axis=0)


def start_kernel(part_ref, image_ref, arr_ref, r_ref, place_ref, stiff_place_ref,
                 weight_ref, basis2_ref, inverse_from, local_place_from,
                 u_ref, w_ref, terms_ref, sums_ref,
                 inverse_ref, local_place_ref, sems):
    copies = bring(
        [
            (inverse_from, inverse_ref),
            (local_place_from, local_place_ref),
        ],
        sems,
    )
    ncl = basis2_ref.shape[0] // 2
    rhs = r_ref.shape[1]
    terms = jnp.zeros((2 * ncl, 2 * rhs), F32)
    sums = [jnp.zeros((8, rhs), F32) for _ in range(2)]
    for lo, n in tiles(r_ref.shape[0]):
        at = slice(lo, lo + n)
        u = completed(part_ref, at, place_ref, arr_ref)
        w = completed(image_ref, at, stiff_place_ref, arr_ref)
        u_ref[at, :] = u
        w_ref[at, :] = w
        weight = weight_ref[at, :]
        sums[0] += folded(weight * u * r_ref[at, :])
        sums[1] += folded(u * w)
        terms += dot(basis2_ref[:, at], pair(weight * w))
    terms_ref[...] = three(terms, ncl)
    sums_ref[...] = collect(sums, rhs)
    for copy in copies:
        copy.wait()


def second_kernel(part_ref, image_ref, arr_ref, scal_ref, r_ref, u_ref, w_ref,
                  place_ref, stiff_place_ref, weight_ref, basis2_ref,
                  m_ref, z_ref, x1_ref, r1_ref, u1_ref, w1_ref, terms_ref, sums_ref):
    ncl = basis2_ref.shape[0] // 2
    rhs = r_ref.shape[1]
    alpha = scal_ref[0:1, :] / scal_ref[1:2, :]
    terms = jnp.zeros((2 * ncl, 2 * rhs), F32)
    sums = [jnp.zeros((8, rhs), F32) for _ in range(4)]
    for lo, n in tiles(r_ref.shape[0]):
        at = slice(lo, lo + n)
        m = completed(part_ref, at, place_ref, arr_ref)
        z = completed(image_ref, at, stiff_place_ref, arr_ref)
        m_ref[at, :] = m
        z_ref[at, :] = z
        weight = weight_ref[at, :]
        p, s = u_ref[at, :], w_ref[at, :]
        x1_ref[at, :] = alpha * p
        r1 = r_ref[at, :] - alpha * s
        u1 = p - alpha * m
        w1 = s - alpha * z
        r1_ref[at, :] = r1
        u1_ref[at, :] = u1
        w1_ref[at, :] = w1
        left = weight * s - alpha * z
        weighted = weight * u1
        for k, term in enumerate((weighted * r1, u1 * left, weighted * s, p * left)):
            sums[k] += folded(term)
        terms += dot(basis2_ref[:, at], pair(weight * w1))
    terms_ref[...] = three(terms, ncl)
    sums_ref[...] = collect(sums, rhs)


def terms_kernel(a0, a1, a2, a3, terms_ref, sums_ref, basis_place_ref, *refs):
    *scal, arr_ref, send_ref = refs
    ncl = terms_ref.shape[0]
    arrivals((a0, a1, a2, a3), arr_ref)
    added = three(dot(basis_place_ref[...], arr_ref[...]), ncl)
    if scal:
        added *= -scal[0][0:1, :] / scal[0][1:2, :]
    send_terms(terms_ref[...] + added, sums_ref[...], send_ref)


def local_part_kernel(w_ref, weight_ref, inverse_ref, pick_ref, local_ref, pre_ref, cat, cat2):
    for lo, n in tiles(w_ref.shape[0], FINE):
        at = slice(lo, lo + n)
        cat[at, :] = pair(weight_ref[at, :] * w_ref[at, :])
    front(inverse_ref, weight_ref, pick_ref, cat, local_ref, pre_ref, cat2)


def local_shared_kernel(pre_ref, arr_ref, after_ref, local_shared_ref, scal_ref, out_ref):
    factor = -scal_ref[0:1, :] / scal_ref[1:2, :]
    for lo, n in tiles(pre_ref.shape[0]):
        at = slice(lo, lo + n)
        came = halves(dot(local_shared_ref[at, :], arr_ref[...]))
        out_ref[at, :] = pre_ref[at, :] + factor * came


def local_again_kernel(pre_ref, arr_ref, after_ref, local_place_ref, weight_ref, pick_ref,
                       out_ref, cat):
    for lo, n in tiles(weight_ref.shape[0], FINE):
        at = slice(lo, lo + n)
        came = halves(dot(local_place_ref[at, :], arr_ref[...]))
        cat[at, :] = pair(weight_ref[at, :] * came)
    for lo, n in tiles(pre_ref.shape[0], FINE):
        at = slice(lo, lo + n)
        out_ref[at, :] = pre_ref[at, :] + halves(dot(pick_ref[at, :], cat[...]))


def complete_kernel(w_part_ref, local_part_ref, arr_ref, after_ref, place_ref, local_place_ref,
                    *refs):
    *more, w_ref, local_ref = refs
    if more:
        scal_ref, z_part_ref, z_ref = more
        factor = -scal_ref[0:1, :] / scal_ref[1:2, :]
    for lo, n in tiles(w_ref.shape[0], FINE):
        at = slice(lo, lo + n)
        came = halves(dot(place_ref[at, :], arr_ref[...]))
        local = halves(dot(local_place_ref[at, :], arr_ref[...]))
        if more:
            z_ref[at, :] = z_part_ref[at, :] + came
            came, local = factor * came, factor * local
        w_ref[at, :] = w_part_ref[at, :] + came
        local_ref[at, :] = local_part_ref[at, :] + local


def step_scalars(before, now):
    beta = now[0:1, :] / before[0:1, :]
    energy = now[1:2, :] + beta * (now[2:3, :] + now[3:4, :]) + beta * beta * before[1:2, :]
    return beta, now[0:1, :] / energy, energy


def third_kernel(part_ref, image_ref, arr_ref, before_ref, scal_ref,
                 x1_ref, r1_ref, u1_ref, w1_ref, p_ref, s_ref, q_ref, z_ref,
                 place_ref, stiff_place_ref, weight_ref,
                 send_ref, state_ref, x2_ref, r2_ref, u2_ref, half_ref, p1_ref, s1_ref):
    rhs = r1_ref.shape[1]
    beta, alpha, energy = step_scalars(before_ref[...], scal_ref[...])
    sums = [jnp.zeros((8, rhs), F32) for _ in range(4)]
    for lo, n in tiles(r1_ref.shape[0]):
        at = slice(lo, lo + n)
        m = completed(part_ref, at, place_ref, arr_ref)
        image = completed(image_ref, at, stiff_place_ref, arr_ref)
        p1 = u1_ref[at, :] + beta * p_ref[at, :]
        s1 = w1_ref[at, :] + beta * s_ref[at, :]
        q1 = m + beta * q_ref[at, :]
        r2 = r1_ref[at, :] - alpha * s1
        u2 = u1_ref[at, :] - alpha * q1
        half = w1_ref[at, :] - (alpha * beta) * z_ref[at, :]
        weight = weight_ref[at, :]
        left = weight * half - alpha * image
        weighted = weight * u2
        for k, term in enumerate((weighted * r2, u2 * left, weighted * s1, p1 * left)):
            sums[k] += folded(term)
        x2_ref[at, :] = x1_ref[at, :] + alpha * p1
        r2_ref[at, :] = r2
        u2_ref[at, :] = u2
        half_ref[at, :] = half - alpha * image
        p1_ref[at, :] = p1
        s1_ref[at, :] = s1
    block = collect(sums, rhs)
    for g in range(send_ref.shape[0] // SCAL):
        send_ref[g * SCAL : (g + 1) * SCAL, :] = block
    state_ref[...] = jnp.concatenate(
        [scal_ref[0:1, :], energy, alpha, jnp.zeros((SCAL - 3, rhs), F32)], axis=0
    )


def last_kernel(state_ref, got_ref, a0, a1, a2, a3, place_ref,
                x2, u2, p1, r2, half, s1,
                x3_to, r3_to, arr_cat, x3, r3, out_sems):
    state = state_ref[...]
    now = jnp.sum(got_ref[...].reshape(-1, SCAL, got_ref.shape[1]), axis=0)
    beta, alpha, _ = step_scalars(state, now)
    old = state[2:3, :]
    arrivals((a0, a1, a2, a3), arr_cat)
    outs = []
    for i, (lo, n) in enumerate(tiles(r2.shape[0])):
        at = slice(lo, lo + n)
        x3[at, :] = x2[at, :] + alpha * (u2[at, :] + beta * p1[at, :])
        w2 = half[at, :] - old * halves(dot(place_ref[at, :], arr_cat[...]))
        r3[at, :] = r2[at, :] - alpha * (w2 + beta * s1[at, :])
        rows = pl.ds(lo, n)
        outs += bring(
            [(x3.at[rows, :], x3_to.at[rows, :]), (r3.at[rows, :], r3_to.at[rows, :])],
            out_sems.at[i],
        )
    for copy in outs:
        copy.wait()


def body(
    stiffness, local_inverse, coarse_basis, loads, counts, shared_rows, coarse_map, coarse_inverse
):
    size = lax.axis_size("sub")
    me = lax.axis_index("sub")
    rows, rhs = loads.shape[1:]
    ncl = coarse_basis.shape[1]
    slots, cap = shared_rows.shape[1:]
    order = coarse_inverse.shape[1]
    lists = slots * cap
    stiff, inverse = aside(stiffness[0], local_inverse[0])

    def partner(distance, parity):
        def of(i):
            up = (i // distance) % 2 == parity
            return (i + distance if up else i - distance) % size

        return [(i, of(i)) for i in range(size)]

    inside = partner(1, 0)
    swaps = [inside, partner(1, 1), partner(STRIDE, 0), partner(STRIDE, 1)]
    swaps = [swaps[j] for j in ORDER]

    def exchange(outs):
        return [lax.ppermute(out, "sub", swap) for out, swap in zip(outs, swaps)]

    cores = [[2 * i + c for i in range(size // 2)] for c in range(2)]
    groups = size // 2
    block = ncl + SCAL

    fields = (rows, rhs)
    out4 = [far((cap, rhs))] * 4
    wide = pltpu.VMEM((rows, 2 * rhs), BF16)
    wide_arr = pltpu.VMEM((lists, 2 * rhs), BF16)
    place_like = pltpu.VMEM((rows, lists), BF16)
    pick_like = pltpu.VMEM((lists, rows), BF16)
    basis = coarse_basis[0]
    (loads_aside,) = aside(loads[0])

    listed, *outs = call(
        loads_kernel,
        "loads",
        (shared_rows[0], loads_aside),
        [far((1, lists), jnp.int32)] + out4,
        [pick_like, wide, pltpu.VMEM(fields, F32), pltpu.SemaphoreType.DMA((1,))],
        {1: ASPEC},
    )
    arrived = exchange(outs)
    own_map = jnp.pad(coarse_map, ((0, 0), (0, -ncl % LANES)))
    maps = jnp.broadcast_to(own_map, (size, own_map.shape[1]))
    maps = lax.all_to_all(maps, "sub", 0, 0, tiled=True)
    maps, *arrived = lax.optimization_barrier((maps, *arrived))


    (picked,) = call(
        columns_kernel,
        "coarse_columns",
        (maps, *aside(coarse_inverse)),
        [far((size * ncl, coarse_inverse.shape[0]))],
        [
            pltpu.VMEM((order, coarse_inverse.shape[0]), F32),
            pltpu.VMEM((4, coarse_inverse.shape[0], order // 4), F32),
            pltpu.SemaphoreType.DMA((4,)),
        ],
        {0: SSPEC, 1: ASPEC},
        mib=30,
    )
    mine_rows = lax.all_to_all(picked, "sub", 0, 0, tiled=True)

    r0, local, pre, send = call(
        first_kernel,
        "residual_and_terms",
        (loads[0], *arrived, listed, counts, basis, inverse),
        [away(fields), away(fields), away((lists, rhs)), far((groups * block, rhs))],
        [
            wide,
            wide_arr,
            place_like,
            pick_like,
            pltpu.VMEM((2 * ncl, rows), BF16),
            pltpu.VMEM((rows, rows), BF16),
            pltpu.VMEM(fields, F32),
            wide,
            pltpu.SemaphoreType.DMA((1,)),
        ],
        {8: ASPEC},
        us=6,
        mib=30,
    )
    products = call(
        products_kernel,
        "products",
        (listed, counts, basis, stiff),
        [
            away((rows, lists), BF16),
            away((lists, lists), BF16),
            away((2 * ncl, lists), BF16),
            away((lists, 2 * LANES), BF16),
        ],
        [
            pick_like,
            place_like,
            pltpu.VMEM((rows, rows), BF16),
            pltpu.VMEM((2 * ncl, rows), BF16),
            pltpu.VMEM((rows, 2 * LANES), BF16),
            pltpu.SemaphoreType.DMA((1,)),
        ],
        {3: ASPEC},
        us=10,
        mib=30,
    )
    r0, local, pre = aside(r0, local, pre)

    keep, pass_on = call(
        coarse_kernel,
        "coarse_block",
        (maps, (me % 2).reshape(1), mine_rows),
        [far((ncl, groups * ncl)), far((ncl, groups * ncl))],
        [
            pltpu.VMEM((order, LANES), F32),
            pltpu.VMEM((size * ncl, LANES), F32),
        ],
        {0: SSPEC, 1: SSPEC},
        mib=30,
    )
    passed = lax.ppermute(pass_on, "sub", inside)

    def share(send):
        return lax.all_to_all(send, "sub", 0, 0, tiled=True, axis_index_groups=cores)

    send, *products = lax.optimization_barrier((send, *products))
    terms = share(send)
    local_products = call(
        local_products_kernel,
        "local_products",
        (listed, counts, send, inverse),
        [away((rows, lists), BF16)],
        [place_like, pltpu.VMEM((rows, rows), BF16), pltpu.SemaphoreType.DMA((1,))],
        {2: ASPEC, 3: ASPEC},
        us=10,
        mib=30,
    )
    terms, *local_products = lax.optimization_barrier((terms, *local_products))
    local_products = aside(*local_products)
    coarse, after = call(
        stack_kernel,
        "coarse_addends",
        (keep, passed, terms),
        [near((4 * ncl, groups * ncl), BF16), far((SCAL, LANES))],
    )
    stiff_place, stiff_shared, basis_place, pick_basis = aside(*products)
    tables = held(*call(
        tables_kernel,
        "tables",
        (listed, counts, basis, after, stiff, stiff_place, stiff_shared),
        [
            near((lists, rows), BF16),
            near((rows, lists), BF16),
            near(fields),
            near((2 * ncl, rows), BF16),
            near((rows, 2 * LANES), BF16),
            near((rows, rows), BF16),
            near((rows, lists), BF16),
            near((lists, lists), BF16),
        ],
        [pltpu.SemaphoreType.DMA((3,))],
        {4: ASPEC, 5: ASPEC, 6: ASPEC},
        us=5,
    ))
    pick, place, weight, basis2, basis3, stiff, stiff_place, stiff_shared = tables
    tables = []
    (coarse,) = held(coarse)

    def correct(terms, pre, bring_in=None):
        own, other = call(
            coarse_solve_kernel,
            "coarse_solve",
            (terms, coarse),
            [far((block, rhs)), far((block, rhs))],
            us=1,
        )
        came = lax.ppermute(other, "sub", inside)
        if bring_in:
            small.extend(bring_in(own))
        values, scal, *outs = call(
            back_kernel,
            "coarse_back",
            (own, came, pre(own), small[0]),
            [near((2 * LANES, rhs), BF16), far((SCAL, rhs))] + out4,
            us=1,
        )
        return *held(values), scal, exchange(outs)

    small = []

    def bring_small(own):
        return held(*call(
            small_kernel,
            "small_tables",
            (own, pick_basis, basis_place),
            [near(pick_basis.shape, BF16), near(basis_place.shape, BF16)],
            [pltpu.SemaphoreType.DMA((2,))],
            {1: ASPEC, 2: ASPEC},
            us=1,
        ))

    def operate(values, local, arrived, *beside):
        part, image, pre = held(*call(
            part_kernel,
            "field_part",
            (values, local, weight, basis3, stiff, pick),
            [near(fields), near(fields), near((lists, rhs))],
            [wide, wide],
            us=3,
        ))
        if beside:
            pre, table = held(*lax.optimization_barrier((pre, *beside)))
            tables.append(table)
        arr, *outs = call(
            shared_kernel,
            "image_shared",
            (*arrived, pre, stiff_shared),
            [near((lists, 2 * rhs), BF16)] + out4,
            us=1,
        )
        return part, image, *held(arr), exchange(outs)

    def share_terms(arrived, terms, sums, *scal):
        arr, send = call(
            terms_kernel,
            "terms",
            (*arrived, terms, sums, small[1], *scal),
            [near((lists, 2 * rhs), BF16), far((groups * block, rhs))],
            us=1,
        )
        return *held(arr), share(send)

    def local_part(w):
        return held(*call(
            local_part_kernel,
            "local_part",
            (w, weight, inverse, pick),
            [near(fields), near((lists, rhs))],
            [wide, wide],
            us=3,
        ))

    def local_shared(pre, arr, scal):
        def of(own):
            return held(*call(
                local_shared_kernel,
                "local_shared",
                (pre, arr, own, shared_table, scal),
                [near((lists, rhs))],
                us=1,
            ))[0]

        return of

    def local_again(pre, arr):
        def of(own):
            return held(*call(
                local_again_kernel,
                "local_again",
                (pre, arr, own, local_place, weight, pick),
                [near((lists, rhs))],
                [wide],
                us=1,
            ))[0]

        return of

    def complete(w, local, arr, after, *more):
        return held(*call(
            complete_kernel,
            "complete",
            (w, local, arr, after, place, local_place, *more),
            [near(fields)] * (3 if more else 2),
            us=2,
        ))

    values, _, arrived = correct(terms, lambda own: pre, bring_small)
    part, image, arr, arrived = operate(values, local, arrived)
    u0, w0, terms, sums, inverse, local_place = held(*call(
        start_kernel,
        "start",
        (part, image, arr, r0, place, stiff_place, weight, basis2, inverse, *local_products),
        [near(fields), near(fields), near((ncl, rhs)), near((SCAL, rhs))]
        + [near((rows, rows), BF16), near((rows, lists), BF16)],
        [pltpu.SemaphoreType.DMA((2,))],
        {8: ASPEC, 9: ASPEC},
        us=3,
    ))
    local, pre = local_part(w0)
    terms, pre = held(*lax.optimization_barrier((terms, pre)))
    arr, terms = share_terms(arrived, terms, sums)
    values, scal0, arrived = correct(terms, local_again(pre, arr))
    w0, local = complete(w0, local, arr, values)
    (shared_table,) = held(*call(
        shared_products_kernel,
        "shared_products",
        (local_place, values, pick, weight),
        [near((lists, lists), BF16)],
        us=4,
    ))

    part, image, arr, arrived = operate(values, local, arrived, shared_table)
    (shared_table,) = tables
    m0, z0, x1, r1, u1, w1, terms, sums = held(*call(
        second_kernel,
        "first_update",
        (part, image, arr, scal0, r0, u0, w0, place, stiff_place, weight, basis2),
        [near(fields)] * 6 + [near((ncl, rhs)), near((SCAL, rhs))],
        us=4,
    ))
    local, pre = local_part(w1)
    terms, pre = held(*lax.optimization_barrier((terms, pre)))
    arr, terms = share_terms(arrived, terms, sums, scal0)
    values, scal1, arrived = correct(terms, local_shared(pre, arr, scal0))
    z0, w1, local = complete(w1, local, arr, values, scal0, z0)

    part, image, arr, arrived = operate(values, local, arrived)
    pieces = len(tiles(rows))
    send, state, *news = call(
        third_kernel,
        "second_update",
        (part, image, arr, scal0, scal1, x1, r1, u1, w1, u0, w0, m0, z0)
        + (place, stiff_place, weight),
        [far((size * SCAL, rhs)), far((SCAL, rhs))] + [near(fields)] * 6,
        us=4,
    )
    x2, r2, u2, half, p1, s1 = held(*news)
    send, *arrived = lax.optimization_barrier((send, *arrived))
    sums = lax.all_to_all(send, "sub", 0, 0, tiled=True)
    sums, *arrived = lax.optimization_barrier((sums, *arrived))
    x3, r3 = call(
        last_kernel,
        "last_update",
        (state, sums, *arrived, place, x2, u2, p1, r2, half, s1),
        [far(fields), far(fields)],
        [wide_arr, pltpu.VMEM(fields, F32), pltpu.VMEM(fields, F32)]
        + [pltpu.SemaphoreType.DMA((pieces, 2))],
        sent=range(2),
    )
    return (x3[None], r3[None])


def solution(mesh):
    placed = (
        P("sub", None, None),
        P("sub", None, None),
        P("sub", None, None),
        P("sub", None, None),
        P("sub", None),
        P("sub", None, None),
        P("sub", None),
        P("sub", None),
    )
    return jax.shard_map(
        body,
        mesh=mesh,
        in_specs=placed,
        out_specs=(P("sub", None, None), P("sub", None, None)),
        check_vma=False,
    )
```

```python
import functools

import jax
import jax.numpy as jnp
from jax import lax
from jax.experimental import pallas as pl
from jax.experimental.pallas import tpu as pltpu
from jax.sharding import PartitionSpec as P

STRIDE = 8
F32 = jnp.float32
BF16 = jnp.bfloat16
TILE = 512
FINE = 256
HALF = 768
SLOTS = 512
SCAL = 8
ORDER = (3, 1, 2, 0)
LANES = 128

VSPEC = pl.BlockSpec(memory_space=pltpu.VMEM)
SSPEC = pl.BlockSpec(memory_space=pltpu.SMEM)
ASPEC = pl.BlockSpec(memory_space=pltpu.HBM)


def near(shape, dtype=F32):
    return pltpu.VMEM(shape, dtype)


def far(shape, dtype=F32):
    return jax.ShapeDtypeStruct(shape, dtype)


def away(shape, dtype=F32):
    return pltpu.HBM(shape, dtype)


def held(*arrays):
    return tuple(pltpu.with_memory_space_constraint(a, pltpu.VMEM) for a in arrays)


def aside(*arrays):
    return tuple(pltpu.with_memory_space_constraint(a, pltpu.HBM) for a in arrays)


def call(kernel, name, args, outs, scratch=(), specs=None, us=2, mib=16, sent=()):
    specs = specs or {}
    return pl.pallas_call(
        kernel,
        name=name,
        out_shape=tuple(outs),
        in_specs=[specs.get(i, VSPEC) for i in range(len(args))],
        out_specs=tuple(ASPEC if i in sent else VSPEC for i in range(len(outs))),
        scratch_shapes=list(scratch),
        compiler_params=pltpu.CompilerParams(vmem_limit_bytes=mib * 1024 * 1024),
        cost_estimate=pl.CostEstimate(
            flops=0, bytes_accessed=us * 3_000_000, transcendentals=0
        ),
    )(*args)


def cut(x):
    high = x.astype(BF16)
    return high, (x - high.astype(F32)).astype(BF16)


def pair(x):
    return jnp.concatenate(cut(x), axis=1)


def halves(product):
    half = product.shape[1] // 2
    return product[:, :half] + product[:, half:]


def three(product, rows):
    half = product.shape[1] // 2
    return product[:rows, :half] + product[:rows, half:] + product[rows : 2 * rows, :half]


def dot(a, b):
    return jnp.dot(a, b, preferred_element_type=F32)


def tiles(total, step=TILE):
    step = min(step, total)
    return [(lo, min(step, total - lo)) for lo in range(0, total, step)]


def folded(x):
    return jnp.sum(x.reshape(-1, 8, x.shape[-1]), axis=0)


def pick_out(pick_ref, cat_ref, out_refs):
    cap = out_refs[0].shape[0]
    for j, out in enumerate(out_refs):
        out[...] = halves(dot(pick_ref[j * cap : (j + 1) * cap, :], cat_ref[...]))


def arrivals(arrived_refs, arr_cat):
    cap = arrived_refs[0].shape[0]
    for j, ref in enumerate(arrived_refs):
        arr_cat[j * cap : (j + 1) * cap, :] = pair(ref[...])


def bring(pairs, sems):
    copies = [pltpu.make_async_copy(*p, sems.at[i]) for i, p in enumerate(pairs)]
    for copy in copies:
        copy.start()
    return copies


def each(total, step, work, flat=False):
    if flat:
        for lo in range(0, total, step):
            work(lo)
        return

    def one(i, carry):
        work(pl.multiple_of(i * step, step))
        return carry

    lax.fori_loop(0, total // step, one, 0)


def summed(total, step, work, start):
    def one(i, carry):
        return work(pl.multiple_of(i * step, step), carry)

    return lax.fori_loop(0, total // step, one, start)


def fill_pick(row_ref, pick_ref):
    slots, rows = pick_ref.shape

    def some(lo):
        listed = row_ref[:, pl.ds(lo, LANES)].astype(F32)
        entries = jnp.broadcast_to(listed, (LANES, LANES)).T
        for left in range(0, rows, LANES):
            at = left + lax.broadcasted_iota(jnp.int32, (LANES, LANES), 1)
            same = jnp.where(at.astype(F32) == entries, 1.0, 0.0)
            pick_ref[pl.ds(lo, LANES), left : left + LANES] = same.astype(BF16)

    each(slots, LANES, some)


def fill_place(row_ref, place_ref):
    rows, slots = place_ref.shape

    def some(lo):
        at = lo + lax.broadcasted_iota(jnp.int32, (LANES, slots), 0)
        same = jnp.where(at == row_ref[...], 1.0, 0.0)
        place_ref[pl.ds(lo, LANES), :] = same.astype(BF16)

    each(rows, LANES, some)


def weights_of(count_ref):
    rows = count_ref.shape[1]
    return jnp.broadcast_to(1.0 / count_ref[...].astype(F32), (LANES, rows)).T


def fill_basis2(basis_ref, basis2_ref):
    ncl = basis_ref.shape[0]
    high, low = cut(basis_ref[...])
    basis2_ref[:ncl, :] = high
    basis2_ref[ncl:, :] = low


def loads_kernel(rows_ref, loads_from, listed_ref, out0, out1, out2, out3, pick, cat, loads, sems):
    copies = bring([(loads_from, loads)], sems)
    me = lax.axis_index("sub")
    one = me % 2 == 0
    far_one = (me // STRIDE) % 2 == 0
    given = [rows_ref[k : k + 1, :] for k in range(4)]
    lists = [
        jnp.where(one, given[0], given[1]),
        jnp.where(one, given[1], given[0]),
        jnp.where(far_one, given[2], given[3]),
        jnp.where(far_one, given[3], given[2]),
    ]
    listed_ref[...] = jnp.concatenate([lists[j] for j in ORDER], axis=1)
    fill_pick(listed_ref, pick)
    for copy in copies:
        copy.wait()
    for lo, n in tiles(loads.shape[0]):
        cat[lo : lo + n, :] = pair(loads[lo : lo + n, :])
    pick_out(pick, cat, (out0, out1, out2, out3))


def fill_basis3(basis_ref, basis3_ref):
    ncl, rows = basis_ref.shape
    high, low = cut(basis_ref[...])
    high, low = high.astype(F32), low.astype(F32)
    fill = jnp.zeros((basis3_ref.shape[1] - 3 * ncl, rows), F32)
    basis3_ref[...] = jnp.concatenate([high, high, low, fill], axis=0).T.astype(BF16)


def products_kernel(row_ref, count_ref, basis_ref, stiff_from,
                    stiff_place_ref, stiff_shared_ref, basis_place_ref, pick_basis_ref,
                    pick, place, stiff, basis2, basis3, sems):
    copy = pltpu.make_async_copy(stiff_from, stiff, sems.at[0])
    copy.start()
    fill_pick(row_ref, pick)
    fill_place(row_ref, place)
    weight = 1.0 / count_ref[...].astype(F32)
    fill_basis2(basis_ref, basis2)
    scaled = basis2[...].astype(F32) * weight
    basis_place_ref[...] = dot(scaled.astype(BF16), place[...]).astype(BF16)
    fill_basis3(basis_ref, basis3)
    full = weights_of(count_ref)
    for left in range(0, basis3.shape[1], LANES):
        at = slice(left, left + LANES)
        basis3[:, at] = (basis3[:, at].astype(F32) * full).astype(BF16)
    for lo, n in tiles(pick.shape[0]):
        pick_basis_ref[lo : lo + n, :] = dot(pick[lo : lo + n, :], basis3[...]).astype(BF16)
    copy.wait()

    def product(lo):
        at = pl.ds(lo, FINE)
        stiff_place_ref[at, :] = dot(stiff[at, :], place[...]).astype(BF16)

    def shared(lo):
        at = pl.ds(lo, FINE)
        stiff_shared_ref[at, :] = dot(pick[at, :], stiff_place_ref[...]).astype(BF16)

    each(stiff.shape[0], FINE, product)
    each(pick.shape[0], FINE, shared)


def local_products_kernel(row_ref, count_ref, after_ref, inverse_from, local_place_ref,
                          place, inverse, sems):
    copies = bring([(inverse_from, inverse)], sems)
    fill_place(row_ref, place)
    rows = place.shape[0]
    weight = jnp.broadcast_to(1.0 / count_ref[...].astype(F32), (8, rows)).astype(BF16)
    listed = dot(weight, place[...])[0:1]
    for copy in copies:
        copy.wait()

    def product(lo):
        at = pl.ds(lo, FINE)
        local_place_ref[at, :] = (dot(inverse[at, :], place[...]) * listed).astype(BF16)

    each(rows, FINE, product)


def shared_products_kernel(local_place_ref, after_ref, pick_ref, weight_ref, local_shared_ref):
    slots = pick_ref.shape[0]
    weight = weight_ref[...].astype(BF16)

    def some(lo):
        at = pl.ds(lo, FINE)
        shared = dot(pick_ref[at, :], local_place_ref[...])
        turned = dot(pick_ref[at, :], weight)
        for left in range(0, slots, LANES):
            scaled = shared[:, left : left + LANES] * turned
            local_shared_ref[at, left : left + LANES] = scaled.astype(BF16)

    each(slots, FINE, some)


def tables_kernel(row_ref, count_ref, basis_ref, after_ref, stiff_from, stiff_place_from,
                  stiff_shared_from,
                  pick_ref, place_ref, weight_ref, basis2_ref, basis3_ref,
                  stiff_ref, stiff_place_ref, stiff_shared_ref, sems):
    copies = bring(
        [
            (stiff_from, stiff_ref),
            (stiff_shared_from, stiff_shared_ref),
            (stiff_place_from, stiff_place_ref),
        ],
        sems,
    )
    fill_pick(row_ref, pick_ref)
    fill_place(row_ref, place_ref)
    weight_ref[...] = weights_of(count_ref)
    fill_basis2(basis_ref, basis2_ref)
    fill_basis3(basis_ref, basis3_ref)
    for copy in copies:
        copy.wait()


def small_kernel(after_ref, first_from, second_from, first_ref, second_ref, sems):
    for copy in bring([(first_from, first_ref), (second_from, second_ref)], sems):
        copy.wait()


def columns_kernel(map_ref, inverse_from, out_ref, turned, rows, sems):
    parts = rows.shape[0]
    width = rows.shape[2]
    copies = bring(
        [(inverse_from.at[:, pl.ds(k * width, width)], rows.at[k]) for k in range(parts)], sems
    )
    for k in range(parts):
        copies[k].wait()
        turned[k * width : (k + 1) * width, :] = rows[k].T
    size = map_ref.shape[0]
    ncl = out_ref.shape[0] // size

    def step(i, _):
        for k in range(ncl):
            out_ref[pl.ds(i * ncl + k, 1), :] = turned[pl.ds(map_ref[i, k], 1), :]
        return 0

    lax.fori_loop(0, size, step, 0)


def coarse_kernel(map_ref, which_ref, got_ref, keep_ref, send_ref, turned, rowed):
    ncl, half = keep_ref.shape
    width = got_ref.shape[1]
    fill = jnp.zeros((turned.shape[1] - ncl, width), F32)
    for t in range(got_ref.shape[0] // ncl):
        block = jnp.concatenate([got_ref[t * ncl : (t + 1) * ncl, :], fill], axis=0)
        turned[t * width : (t + 1) * width, :] = block.T

    size = map_ref.shape[0]

    def step(i, _):
        for c in range(2):
            for k in range(ncl):
                row = turned[pl.ds(map_ref[2 * i + c, k], 1), :]
                rowed[pl.ds(c * half + i * ncl + k, 1), :] = row
        return 0

    lax.fori_loop(0, size // 2, step, 0)
    first = rowed[:half, :].T[:ncl, :]
    second = rowed[half:, :].T[:ncl, :]
    even = which_ref[0] == 0
    keep_ref[...] = jnp.where(even, first, second)
    send_ref[...] = jnp.where(even, second, first)


def stack_kernel(own_ref, other_ref, terms_ref, out_ref, after_ref):
    after_ref[...] = jnp.zeros_like(after_ref)
    ncl = own_ref.shape[0]
    own_high, own_low = cut(own_ref[...])
    other_high, other_low = cut(other_ref[...])
    out_ref[:ncl, :] = own_high
    out_ref[ncl : 2 * ncl, :] = other_high
    out_ref[2 * ncl : 3 * ncl, :] = own_low
    out_ref[3 * ncl :, :] = other_low


def send_terms(terms, scalars, send_ref):
    block = jnp.concatenate([terms, scalars], axis=0)
    rows = block.shape[0]
    for g in range(send_ref.shape[0] // rows):
        send_ref[g * rows : (g + 1) * rows, :] = block


def front(inverse_ref, weight_ref, pick_ref, cat, local_ref, out_ref, cat2):
    def product(lo):
        at = pl.ds(lo, HALF)
        local = halves(dot(inverse_ref[at, :], cat[...]))
        local_ref[at, :] = local
        cat2[at, :] = pair(weight_ref[at, :] * local)

    def shared(lo):
        at = pl.ds(lo, SLOTS)
        out_ref[at, :] = halves(dot(pick_ref[at, :], cat2[...]))

    each(inverse_ref.shape[0], HALF, product)
    each(pick_ref.shape[0], SLOTS, shared)


def first_kernel(loads_ref, a0, a1, a2, a3, row_ref, count_ref, basis_ref, inverse_from,
                 resid_ref, local_ref, pre_ref, send_ref,
                 cat, arr_cat, place, pick, basis2, inverse, weight, cat2, sems):
    copy = pltpu.make_async_copy(inverse_from, inverse, sems.at[0])
    copy.start()
    fill_place(row_ref, place)
    fill_basis2(basis_ref, basis2)
    weight[...] = weights_of(count_ref)
    ncl, rhs = basis_ref.shape[0], loads_ref.shape[1]
    arrivals((a0, a1, a2, a3), arr_cat)
    terms = jnp.zeros((2 * ncl, 2 * rhs), F32)
    for lo, n in tiles(loads_ref.shape[0]):
        at = slice(lo, lo + n)
        resid = loads_ref[at, :] + halves(dot(place[at, :], arr_cat[...]))
        resid_ref[at, :] = resid
        both = pair(weight[at, :] * resid)
        cat[at, :] = both
        terms += dot(basis2[:, at], both)
    send_terms(three(terms, ncl), jnp.zeros((SCAL, rhs), F32), send_ref)
    fill_pick(row_ref, pick)
    copy.wait()
    front(inverse, weight, pick, cat, local_ref, pre_ref, cat2)


def coarse_solve_kernel(got_ref, g_ref, own_ref, other_ref):
    ncl = g_ref.shape[0] // 4
    rows = ncl + SCAL
    groups = got_ref.shape[0] // rows
    got = got_ref[...].reshape(groups, rows, got_ref.shape[1])
    terms = got[:, :ncl].reshape(groups * ncl, got_ref.shape[1])
    scalars = jnp.sum(got[:, ncl:], axis=0)
    values = three(dot(g_ref[...], pair(terms)), 2 * ncl)
    own_ref[:ncl, :] = values[:ncl]
    own_ref[ncl:, :] = scalars
    other_ref[:ncl, :] = values[ncl:]
    other_ref[ncl:, :] = scalars


def back_kernel(own_ref, other_ref, pre_ref, pick_basis_ref,
                values_ref, scal_ref, out0, out1, out2, out3):
    ncl = own_ref.shape[0] - SCAL
    total = own_ref[...] + other_ref[...]
    scal_ref[...] = total[ncl:]
    high, low = cut(total[:ncl])
    fill = jnp.zeros((values_ref.shape[0] - 3 * ncl, high.shape[1]), BF16)
    values = jnp.concatenate([high, low, high, fill], axis=0)
    values_ref[...] = values
    cap = out0.shape[0]
    for j, out in enumerate((out0, out1, out2, out3)):
        at = slice(j * cap, (j + 1) * cap)
        out[...] = pre_ref[at, :] + dot(pick_basis_ref[at, :], values)


def part_kernel(flat, values_ref, local_ref, weight_ref, basis3_ref, stiff_ref, pick_ref,
                part_ref, image_ref, pre_ref, cat, cat2):
    values = values_ref[...]
    small, large, shared_step = (FINE, FINE, FINE) if flat else (TILE, HALF, SLOTS)

    def field(lo):
        at = pl.ds(lo, small)
        part = weight_ref[at, :] * (local_ref[at, :] + dot(basis3_ref[at, :], values))
        part_ref[at, :] = part
        cat[at, :] = pair(part)

    def product(lo):
        at = pl.ds(lo, large)
        image = halves(dot(stiff_ref[at, :], cat[...]))
        image_ref[at, :] = image
        cat2[at, :] = pair(image)

    def shared(lo):
        at = pl.ds(lo, shared_step)
        pre_ref[at, :] = halves(dot(pick_ref[at, :], cat2[...]))

    each(local_ref.shape[0], small, field, flat)
    each(local_ref.shape[0], large, product, flat)
    each(pick_ref.shape[0], shared_step, shared, flat)


def shared_kernel(a0, a1, a2, a3, pre_ref, stiff_shared_ref,
                  arr_ref, out0, out1, out2, out3):
    arrivals((a0, a1, a2, a3), arr_ref)
    cap = out0.shape[0]
    for j, out in enumerate((out0, out1, out2, out3)):
        at = slice(j * cap, (j + 1) * cap)
        out[...] = pre_ref[at, :] + halves(dot(stiff_shared_ref[at, :], arr_ref[...]))


def completed(ref, at, table_ref, arr_ref):
    return ref[at, :] + halves(dot(table_ref[at, :], arr_ref[...]))


def collect(sums, rhs):
    rows = [jnp.sum(s, axis=0, keepdims=True) for s in sums]
    rows.append(jnp.zeros((SCAL - len(rows), rhs), F32))
    return jnp.concatenate(rows, axis=0)


def start_kernel(part_ref, image_ref, arr_ref, r_ref, place_ref, stiff_place_ref,
                 weight_ref, basis2_ref, inverse_from, local_place_from,
                 u_ref, w_ref, terms_ref, sums_ref,
                 inverse_ref, local_place_ref, sems):
    copies = bring(
        [
            (inverse_from, inverse_ref),
            (local_place_from, local_place_ref),
        ],
        sems,
    )
    ncl = basis2_ref.shape[0] // 2
    rhs = r_ref.shape[1]

    def some(lo, carry):
        ru, uw, terms = carry
        at = pl.ds(lo, TILE)
        u = completed(part_ref, at, place_ref, arr_ref)
        w = completed(image_ref, at, stiff_place_ref, arr_ref)
        u_ref[at, :] = u
        w_ref[at, :] = w
        weight = weight_ref[at, :]
        ru += folded(weight * u * r_ref[at, :])
        uw += folded(u * w)
        return ru, uw, terms + dot(basis2_ref[:, at], pair(weight * w))

    zero = jnp.zeros((8, rhs), F32)
    start = (zero, zero, jnp.zeros((2 * ncl, 2 * rhs), F32))
    *sums, terms = summed(r_ref.shape[0], TILE, some, start)
    terms_ref[...] = three(terms, ncl)
    sums_ref[...] = collect(sums, rhs)
    for copy in copies:
        copy.wait()


def second_kernel(part_ref, image_ref, arr_ref, scal_ref, r_ref, u_ref, w_ref,
                  place_ref, stiff_place_ref, weight_ref, basis2_ref,
                  m_ref, z_ref, x1_ref, r1_ref, u1_ref, w1_ref, terms_ref, sums_ref):
    ncl = basis2_ref.shape[0] // 2
    rhs = r_ref.shape[1]
    alpha = scal_ref[0:1, :] / scal_ref[1:2, :]

    def some(lo, carry):
        *sums, terms = carry
        at = pl.ds(lo, TILE)
        m = completed(part_ref, at, place_ref, arr_ref)
        z = completed(image_ref, at, stiff_place_ref, arr_ref)
        m_ref[at, :] = m
        z_ref[at, :] = z
        weight = weight_ref[at, :]
        p, s = u_ref[at, :], w_ref[at, :]
        x1_ref[at, :] = alpha * p
        r1 = r_ref[at, :] - alpha * s
        u1 = p - alpha * m
        w1 = s - alpha * z
        r1_ref[at, :] = r1
        u1_ref[at, :] = u1
        w1_ref[at, :] = w1
        left = weight * s - alpha * z
        weighted = weight * u1
        news = (weighted * r1, u1 * left, weighted * s, p * left)
        sums = [old + folded(new) for old, new in zip(sums, news)]
        return *sums, terms + dot(basis2_ref[:, at], pair(weight * w1))

    start = (jnp.zeros((8, rhs), F32),) * 4 + (jnp.zeros((2 * ncl, 2 * rhs), F32),)
    *sums, terms = summed(r_ref.shape[0], TILE, some, start)
    terms_ref[...] = three(terms, ncl)
    sums_ref[...] = collect(sums, rhs)


def terms_kernel(a0, a1, a2, a3, terms_ref, sums_ref, basis_place_ref, *refs):
    *scal, arr_ref, send_ref = refs
    ncl = terms_ref.shape[0]
    arrivals((a0, a1, a2, a3), arr_ref)
    added = three(dot(basis_place_ref[...], arr_ref[...]), ncl)
    if scal:
        added *= -scal[0][0:1, :] / scal[0][1:2, :]
    send_terms(terms_ref[...] + added, sums_ref[...], send_ref)


def local_part_kernel(w_ref, weight_ref, inverse_ref, pick_ref, local_ref, pre_ref, cat, cat2):
    for lo, n in tiles(w_ref.shape[0], FINE):
        at = slice(lo, lo + n)
        cat[at, :] = pair(weight_ref[at, :] * w_ref[at, :])
    front(inverse_ref, weight_ref, pick_ref, cat, local_ref, pre_ref, cat2)


def local_shared_kernel(pre_ref, arr_ref, after_ref, local_shared_ref, scal_ref, out_ref):
    factor = -scal_ref[0:1, :] / scal_ref[1:2, :]
    for lo, n in tiles(pre_ref.shape[0]):
        at = slice(lo, lo + n)
        came = halves(dot(local_shared_ref[at, :], arr_ref[...]))
        out_ref[at, :] = pre_ref[at, :] + factor * came


def local_again_kernel(pre_ref, arr_ref, after_ref, local_place_ref, weight_ref, pick_ref,
                       out_ref, cat):
    for lo, n in tiles(weight_ref.shape[0], FINE):
        at = slice(lo, lo + n)
        came = halves(dot(local_place_ref[at, :], arr_ref[...]))
        cat[at, :] = pair(weight_ref[at, :] * came)
    for lo, n in tiles(pre_ref.shape[0], FINE):
        at = slice(lo, lo + n)
        out_ref[at, :] = pre_ref[at, :] + halves(dot(pick_ref[at, :], cat[...]))


def complete_kernel(w_part_ref, local_part_ref, arr_ref, after_ref, place_ref, local_place_ref,
                    *refs):
    *more, w_ref, local_ref = refs
    if more:
        scal_ref, z_part_ref, z_ref = more
        factor = -scal_ref[0:1, :] / scal_ref[1:2, :]

    def some(lo):
        at = pl.ds(lo, TILE)
        came = halves(dot(place_ref[at, :], arr_ref[...]))
        local = halves(dot(local_place_ref[at, :], arr_ref[...]))
        if more:
            z_ref[at, :] = z_part_ref[at, :] + came
            came, local = factor * came, factor * local
        w_ref[at, :] = w_part_ref[at, :] + came
        local_ref[at, :] = local_part_ref[at, :] + local

    each(w_ref.shape[0], TILE, some)


def step_scalars(before, now):
    beta = now[0:1, :] / before[0:1, :]
    energy = now[1:2, :] + beta * (now[2:3, :] + now[3:4, :]) + beta * beta * before[1:2, :]
    return beta, now[0:1, :] / energy, energy


def third_kernel(part_ref, image_ref, arr_ref, before_ref, scal_ref,
                 x1_ref, r1_ref, u1_ref, w1_ref, p_ref, s_ref, q_ref, z_ref,
                 place_ref, stiff_place_ref, weight_ref,
                 send_ref, state_ref, x2_ref, r2_ref, u2_ref, half_ref, p1_ref, s1_ref):
    rhs = r1_ref.shape[1]
    beta, alpha, energy = step_scalars(before_ref[...], scal_ref[...])

    def some(lo, sums):
        at = pl.ds(lo, TILE)
        m = completed(part_ref, at, place_ref, arr_ref)
        image = completed(image_ref, at, stiff_place_ref, arr_ref)
        p1 = u1_ref[at, :] + beta * p_ref[at, :]
        s1 = w1_ref[at, :] + beta * s_ref[at, :]
        q1 = m + beta * q_ref[at, :]
        r2 = r1_ref[at, :] - alpha * s1
        u2 = u1_ref[at, :] - alpha * q1
        half = w1_ref[at, :] - (alpha * beta) * z_ref[at, :]
        weight = weight_ref[at, :]
        left = weight * half - alpha * image
        weighted = weight * u2
        x2_ref[at, :] = x1_ref[at, :] + alpha * p1
        r2_ref[at, :] = r2
        u2_ref[at, :] = u2
        half_ref[at, :] = half - alpha * image
        p1_ref[at, :] = p1
        s1_ref[at, :] = s1
        news = (weighted * r2, u2 * left, weighted * s1, p1 * left)
        return tuple(old + folded(new) for old, new in zip(sums, news))

    sums = summed(r1_ref.shape[0], TILE, some, (jnp.zeros((8, rhs), F32),) * 4)
    block = collect(sums, rhs)
    for g in range(send_ref.shape[0] // SCAL):
        send_ref[g * SCAL : (g + 1) * SCAL, :] = block
    state_ref[...] = jnp.concatenate(
        [scal_ref[0:1, :], energy, alpha, jnp.zeros((SCAL - 3, rhs), F32)], axis=0
    )


def last_kernel(state_ref, got_ref, a0, a1, a2, a3, place_ref,
                x2, u2, p1, r2, half, s1,
                x3_to, r3_to, arr_cat, x3, r3, out_sems):
    state = state_ref[...]
    now = jnp.sum(got_ref[...].reshape(-1, SCAL, got_ref.shape[1]), axis=0)
    beta, alpha, _ = step_scalars(state, now)
    old = state[2:3, :]
    arrivals((a0, a1, a2, a3), arr_cat)
    outs = []
    for i, (lo, n) in enumerate(tiles(r2.shape[0])):
        at = slice(lo, lo + n)
        x3[at, :] = x2[at, :] + alpha * (u2[at, :] + beta * p1[at, :])
        w2 = half[at, :] - old * halves(dot(place_ref[at, :], arr_cat[...]))
        r3[at, :] = r2[at, :] - alpha * (w2 + beta * s1[at, :])
        rows = pl.ds(lo, n)
        outs += bring(
            [(x3.at[rows, :], x3_to.at[rows, :]), (r3.at[rows, :], r3_to.at[rows, :])],
            out_sems.at[i],
        )
    for copy in outs:
        copy.wait()


def body(
    stiffness, local_inverse, coarse_basis, loads, counts, shared_rows, coarse_map, coarse_inverse
):
    size = lax.axis_size("sub")
    me = lax.axis_index("sub")
    rows, rhs = loads.shape[1:]
    ncl = coarse_basis.shape[1]
    slots, cap = shared_rows.shape[1:]
    order = coarse_inverse.shape[1]
    lists = slots * cap
    stiff, inverse = aside(stiffness[0], local_inverse[0])

    def partner(distance, parity):
        def of(i):
            up = (i // distance) % 2 == parity
            return (i + distance if up else i - distance) % size

        return [(i, of(i)) for i in range(size)]

    inside = partner(1, 0)
    swaps = [inside, partner(1, 1), partner(STRIDE, 0), partner(STRIDE, 1)]
    swaps = [swaps[j] for j in ORDER]

    def exchange(outs):
        return [lax.ppermute(out, "sub", swap) for out, swap in zip(outs, swaps)]

    cores = [[2 * i + c for i in range(size // 2)] for c in range(2)]
    groups = size // 2
    block = ncl + SCAL

    fields = (rows, rhs)
    out4 = [far((cap, rhs))] * 4
    wide = pltpu.VMEM((rows, 2 * rhs), BF16)
    wide_arr = pltpu.VMEM((lists, 2 * rhs), BF16)
    place_like = pltpu.VMEM((rows, lists), BF16)
    pick_like = pltpu.VMEM((lists, rows), BF16)
    basis = coarse_basis[0]
    (loads_aside,) = aside(loads[0])

    listed, *outs = call(
        loads_kernel,
        "loads",
        (shared_rows[0], loads_aside),
        [far((1, lists), jnp.int32)] + out4,
        [pick_like, wide, pltpu.VMEM(fields, F32), pltpu.SemaphoreType.DMA((1,))],
        {1: ASPEC},
    )
    arrived = exchange(outs)
    own_map = jnp.pad(coarse_map, ((0, 0), (0, -ncl % LANES)))
    maps = jnp.broadcast_to(own_map, (size, own_map.shape[1]))
    maps = lax.all_to_all(maps, "sub", 0, 0, tiled=True)
    maps, *arrived = lax.optimization_barrier((maps, *arrived))


    (picked,) = call(
        columns_kernel,
        "coarse_columns",
        (maps, *aside(coarse_inverse)),
        [far((size * ncl, coarse_inverse.shape[0]))],
        [
            pltpu.VMEM((order, coarse_inverse.shape[0]), F32),
            pltpu.VMEM((4, coarse_inverse.shape[0], order // 4), F32),
            pltpu.SemaphoreType.DMA((4,)),
        ],
        {0: SSPEC, 1: ASPEC},
        mib=30,
    )
    mine_rows = lax.all_to_all(picked, "sub", 0, 0, tiled=True)

    r0, local, pre, send = call(
        first_kernel,
        "residual_and_terms",
        (loads[0], *arrived, listed, counts, basis, inverse),
        [away(fields), away(fields), away((lists, rhs)), far((groups * block, rhs))],
        [
            wide,
            wide_arr,
            place_like,
            pick_like,
            pltpu.VMEM((2 * ncl, rows), BF16),
            pltpu.VMEM((rows, rows), BF16),
            pltpu.VMEM(fields, F32),
            wide,
            pltpu.SemaphoreType.DMA((1,)),
        ],
        {8: ASPEC},
        us=6,
        mib=30,
    )
    products = call(
        products_kernel,
        "products",
        (listed, counts, basis, stiff),
        [
            away((rows, lists), BF16),
            away((lists, lists), BF16),
            away((2 * ncl, lists), BF16),
            away((lists, 2 * LANES), BF16),
        ],
        [
            pick_like,
            place_like,
            pltpu.VMEM((rows, rows), BF16),
            pltpu.VMEM((2 * ncl, rows), BF16),
            pltpu.VMEM((rows, 2 * LANES), BF16),
            pltpu.SemaphoreType.DMA((1,)),
        ],
        {3: ASPEC},
        us=10,
        mib=30,
    )
    r0, local, pre = aside(r0, local, pre)

    keep, pass_on = call(
        coarse_kernel,
        "coarse_block",
        (maps, (me % 2).reshape(1), mine_rows),
        [far((ncl, groups * ncl)), far((ncl, groups * ncl))],
        [
            pltpu.VMEM((order, LANES), F32),
            pltpu.VMEM((size * ncl, LANES), F32),
        ],
        {0: SSPEC, 1: SSPEC},
        mib=30,
    )
    passed = lax.ppermute(pass_on, "sub", inside)

    def share(send):
        return lax.all_to_all(send, "sub", 0, 0, tiled=True, axis_index_groups=cores)

    send, *products = lax.optimization_barrier((send, *products))
    terms = share(send)
    local_products = call(
        local_products_kernel,
        "local_products",
        (listed, counts, send, inverse),
        [away((rows, lists), BF16)],
        [place_like, pltpu.VMEM((rows, rows), BF16), pltpu.SemaphoreType.DMA((1,))],
        {2: ASPEC, 3: ASPEC},
        us=10,
        mib=30,
    )
    terms, *local_products = lax.optimization_barrier((terms, *local_products))
    local_products = aside(*local_products)
    coarse, after = call(
        stack_kernel,
        "coarse_addends",
        (keep, passed, terms),
        [near((4 * ncl, groups * ncl), BF16), far((SCAL, LANES))],
    )
    stiff_place, stiff_shared, basis_place, pick_basis = aside(*products)
    tables = held(*call(
        tables_kernel,
        "tables",
        (listed, counts, basis, after, stiff, stiff_place, stiff_shared),
        [
            near((lists, rows), BF16),
            near((rows, lists), BF16),
            near(fields),
            near((2 * ncl, rows), BF16),
            near((rows, 2 * LANES), BF16),
            near((rows, rows), BF16),
            near((rows, lists), BF16),
            near((lists, lists), BF16),
        ],
        [pltpu.SemaphoreType.DMA((3,))],
        {4: ASPEC, 5: ASPEC, 6: ASPEC},
        us=5,
    ))
    pick, place, weight, basis2, basis3, stiff, stiff_place, stiff_shared = tables
    tables = []
    (coarse,) = held(coarse)

    def correct(terms, pre, bring_in=None):
        own, other = call(
            coarse_solve_kernel,
            "coarse_solve",
            (terms, coarse),
            [far((block, rhs)), far((block, rhs))],
            us=1,
        )
        came = lax.ppermute(other, "sub", inside)
        if bring_in:
            small.extend(bring_in(own))
        values, scal, *outs = call(
            back_kernel,
            "coarse_back",
            (own, came, pre(own), small[0]),
            [near((2 * LANES, rhs), BF16), far((SCAL, rhs))] + out4,
            us=1,
        )
        return *held(values), scal, exchange(outs)

    small = []

    def bring_small(own):
        return held(*call(
            small_kernel,
            "small_tables",
            (own, pick_basis, basis_place),
            [near(pick_basis.shape, BF16), near(basis_place.shape, BF16)],
            [pltpu.SemaphoreType.DMA((2,))],
            {1: ASPEC, 2: ASPEC},
            us=1,
        ))

    def operate(values, local, arrived, *beside):
        part, image, pre = held(*call(
            functools.partial(part_kernel, not tables),
            "field_part",
            (values, local, weight, basis3, stiff, pick),
            [near(fields), near(fields), near((lists, rhs))],
            [wide, wide],
            us=3,
        ))
        if beside:
            pre, table = held(*lax.optimization_barrier((pre, *beside)))
            tables.append(table)
        arr, *outs = call(
            shared_kernel,
            "image_shared",
            (*arrived, pre, stiff_shared),
            [near((lists, 2 * rhs), BF16)] + out4,
            us=1,
        )
        return part, image, *held(arr), exchange(outs)

    def share_terms(arrived, terms, sums, *scal):
        arr, send = call(
            terms_kernel,
            "terms",
            (*arrived, terms, sums, small[1], *scal),
            [near((lists, 2 * rhs), BF16), far((groups * block, rhs))],
            us=1,
        )
        return *held(arr), share(send)

    def local_part(w):
        return held(*call(
            local_part_kernel,
            "local_part",
            (w, weight, inverse, pick),
            [near(fields), near((lists, rhs))],
            [wide, wide],
            us=3,
        ))

    def local_shared(pre, arr, scal):
        def of(own):
            return held(*call(
                local_shared_kernel,
                "local_shared",
                (pre, arr, own, shared_table, scal),
                [near((lists, rhs))],
                us=1,
            ))[0]

        return of

    def local_again(pre, arr):
        def of(own):
            return held(*call(
                local_again_kernel,
                "local_again",
                (pre, arr, own, local_place, weight, pick),
                [near((lists, rhs))],
                [wide],
                us=1,
            ))[0]

        return of

    def complete(w, local, arr, after, *more):
        return held(*call(
            complete_kernel,
            "complete",
            (w, local, arr, after, place, local_place, *more),
            [near(fields)] * (3 if more else 2),
            us=2,
        ))

    values, _, arrived = correct(terms, lambda own: pre, bring_small)
    part, image, arr, arrived = operate(values, local, arrived)
    tables.append(None)
    u0, w0, terms, sums, inverse, local_place = held(*call(
        start_kernel,
        "start",
        (part, image, arr, r0, place, stiff_place, weight, basis2, inverse, *local_products),
        [near(fields), near(fields), near((ncl, rhs)), near((SCAL, rhs))]
        + [near((rows, rows), BF16), near((rows, lists), BF16)],
        [pltpu.SemaphoreType.DMA((2,))],
        {8: ASPEC, 9: ASPEC},
        us=3,
    ))
    local, pre = local_part(w0)
    terms, pre = held(*lax.optimization_barrier((terms, pre)))
    arr, terms = share_terms(arrived, terms, sums)
    values, scal0, arrived = correct(terms, local_again(pre, arr))
    w0, local = complete(w0, local, arr, values)
    (shared_table,) = held(*call(
        shared_products_kernel,
        "shared_products",
        (local_place, values, pick, weight),
        [near((lists, lists), BF16)],
        us=4,
    ))

    part, image, arr, arrived = operate(values, local, arrived, shared_table)
    shared_table = tables[-1]
    m0, z0, x1, r1, u1, w1, terms, sums = held(*call(
        second_kernel,
        "first_update",
        (part, image, arr, scal0, r0, u0, w0, place, stiff_place, weight, basis2),
        [near(fields)] * 6 + [near((ncl, rhs)), near((SCAL, rhs))],
        us=4,
    ))
    local, pre = local_part(w1)
    terms, pre = held(*lax.optimization_barrier((terms, pre)))
    arr, terms = share_terms(arrived, terms, sums, scal0)
    values, scal1, arrived = correct(terms, local_shared(pre, arr, scal0))
    z0, w1, local = complete(w1, local, arr, values, scal0, z0)

    part, image, arr, arrived = operate(values, local, arrived)
    pieces = len(tiles(rows))
    send, state, *news = call(
        third_kernel,
        "second_update",
        (part, image, arr, scal0, scal1, x1, r1, u1, w1, u0, w0, m0, z0)
        + (place, stiff_place, weight),
        [far((size * SCAL, rhs)), far((SCAL, rhs))] + [near(fields)] * 6,
        us=4,
    )
    x2, r2, u2, half, p1, s1 = held(*news)
    send, *arrived = lax.optimization_barrier((send, *arrived))
    sums = lax.all_to_all(send, "sub", 0, 0, tiled=True)
    sums, *arrived = lax.optimization_barrier((sums, *arrived))
    x3, r3 = call(
        last_kernel,
        "last_update",
        (state, sums, *arrived, place, x2, u2, p1, r2, half, s1),
        [far(fields), far(fields)],
        [wide_arr, pltpu.VMEM(fields, F32), pltpu.VMEM(fields, F32)]
        + [pltpu.SemaphoreType.DMA((pieces, 2))],
        sent=range(2),
    )
    return (x3[None], r3[None])


def solution(mesh):
    placed = (
        P("sub", None, None),
        P("sub", None, None),
        P("sub", None, None),
        P("sub", None, None),
        P("sub", None),
        P("sub", None, None),
        P("sub", None),
        P("sub", None),
    )
    return jax.shard_map(
        body,
        mesh=mesh,
        in_specs=placed,
        out_specs=(P("sub", None, None), P("sub", None, None)),
        check_vma=False,
    )
```

```python
import functools

import jax
import jax.numpy as jnp
from jax import lax
from jax.experimental import pallas as pl
from jax.experimental.pallas import tpu as pltpu
from jax.sharding import PartitionSpec as P

STRIDE = 8
F32 = jnp.float32
BF16 = jnp.bfloat16
TILE = 512
FINE = 256
HALF = 768
SLOTS = 512
SCAL = 8
ORDER = (3, 1, 2, 0)
LANES = 128

VSPEC = pl.BlockSpec(memory_space=pltpu.VMEM)
SSPEC = pl.BlockSpec(memory_space=pltpu.SMEM)
ASPEC = pl.BlockSpec(memory_space=pltpu.HBM)


def near(shape, dtype=F32):
    return pltpu.VMEM(shape, dtype)


def far(shape, dtype=F32):
    return jax.ShapeDtypeStruct(shape, dtype)


def away(shape, dtype=F32):
    return pltpu.HBM(shape, dtype)


def held(*arrays):
    return tuple(pltpu.with_memory_space_constraint(a, pltpu.VMEM) for a in arrays)


def aside(*arrays):
    return tuple(pltpu.with_memory_space_constraint(a, pltpu.HBM) for a in arrays)


def call(kernel, name, args, outs, scratch=(), specs=None, us=2, mib=16, sent=()):
    specs = specs or {}
    return pl.pallas_call(
        kernel,
        name=name,
        out_shape=tuple(outs),
        in_specs=[specs.get(i, VSPEC) for i in range(len(args))],
        out_specs=tuple(ASPEC if i in sent else VSPEC for i in range(len(outs))),
        scratch_shapes=list(scratch),
        compiler_params=pltpu.CompilerParams(vmem_limit_bytes=mib * 1024 * 1024),
        cost_estimate=pl.CostEstimate(
            flops=0, bytes_accessed=us * 3_000_000, transcendentals=0
        ),
    )(*args)


def cut(x):
    high = x.astype(BF16)
    return high, (x - high.astype(F32)).astype(BF16)


def pair(x):
    return jnp.concatenate(cut(x), axis=1)


def halves(product):
    half = product.shape[1] // 2
    return product[:, :half] + product[:, half:]


def three(product, rows):
    half = product.shape[1] // 2
    return product[:rows, :half] + product[:rows, half:] + product[rows : 2 * rows, :half]


def dot(a, b):
    return jnp.dot(a, b, preferred_element_type=F32)


def tiles(total, step=TILE):
    step = min(step, total)
    return [(lo, min(step, total - lo)) for lo in range(0, total, step)]


def folded(x):
    return jnp.sum(x.reshape(-1, 8, x.shape[-1]), axis=0)


def pick_out(pick_ref, cat_ref, out_refs):
    cap = out_refs[0].shape[0]
    for j, out in enumerate(out_refs):
        out[...] = halves(dot(pick_ref[j * cap : (j + 1) * cap, :], cat_ref[...]))


def arrivals(arrived_refs, arr_cat):
    cap = arrived_refs[0].shape[0]
    for j, ref in enumerate(arrived_refs):
        arr_cat[j * cap : (j + 1) * cap, :] = pair(ref[...])


def bring(pairs, sems):
    copies = [pltpu.make_async_copy(*p, sems.at[i]) for i, p in enumerate(pairs)]
    for copy in copies:
        copy.start()
    return copies


def each(total, step, work, flat=False):
    if flat:
        for lo in range(0, total, step):
            work(lo)
        return

    def one(i, carry):
        work(pl.multiple_of(i * step, step))
        return carry

    lax.fori_loop(0, total // step, one, 0)


def summed(total, step, work, start):
    def one(i, carry):
        return work(pl.multiple_of(i * step, step), carry)

    return lax.fori_loop(0, total // step, one, start)


def fill_pick(row_ref, pick_ref):
    slots, rows = pick_ref.shape

    def some(lo):
        listed = row_ref[:, pl.ds(lo, LANES)].astype(F32)
        entries = jnp.broadcast_to(listed, (LANES, LANES)).T
        for left in range(0, rows, LANES):
            at = left + lax.broadcasted_iota(jnp.int32, (LANES, LANES), 1)
            same = jnp.where(at.astype(F32) == entries, 1.0, 0.0)
            pick_ref[pl.ds(lo, LANES), left : left + LANES] = same.astype(BF16)

    each(slots, LANES, some)


def fill_place(row_ref, place_ref):
    rows, slots = place_ref.shape

    def some(lo):
        at = lo + lax.broadcasted_iota(jnp.int32, (LANES, slots), 0)
        same = jnp.where(at == row_ref[...], 1.0, 0.0)
        place_ref[pl.ds(lo, LANES), :] = same.astype(BF16)

    each(rows, LANES, some)


def weights_of(count_ref):
    rows = count_ref.shape[1]
    return jnp.broadcast_to(1.0 / count_ref[...].astype(F32), (LANES, rows)).T


def fill_basis2(basis_ref, basis2_ref):
    ncl = basis_ref.shape[0]
    high, low = cut(basis_ref[...])
    basis2_ref[:ncl, :] = high
    basis2_ref[ncl:, :] = low


def loads_kernel(rows_from, loads_from, map_from, listed_ref, maps_ref, out0, out1, out2, out3,
                 pick, cat, loads, rows_ref, map_ref, sems):
    *firsts, last = bring([(rows_from, rows_ref), (map_from, map_ref), (loads_from, loads)], sems)
    copies = [last]
    for copy in firsts:
        copy.wait()
    size, ncl = maps_ref.shape[0], map_ref.shape[1]
    maps_ref[...] = jnp.zeros_like(maps_ref)
    maps_ref[:, :ncl] = jnp.broadcast_to(map_ref[...], (size, ncl))
    me = lax.axis_index("sub")
    one = me % 2 == 0
    far_one = (me // STRIDE) % 2 == 0
    given = [rows_ref[k : k + 1, :] for k in range(4)]
    lists = [
        jnp.where(one, given[0], given[1]),
        jnp.where(one, given[1], given[0]),
        jnp.where(far_one, given[2], given[3]),
        jnp.where(far_one, given[3], given[2]),
    ]
    listed_ref[...] = jnp.concatenate([lists[j] for j in ORDER], axis=1)
    fill_pick(listed_ref, pick)
    for copy in copies:
        copy.wait()
    for lo, n in tiles(loads.shape[0]):
        cat[lo : lo + n, :] = pair(loads[lo : lo + n, :])
    pick_out(pick, cat, (out0, out1, out2, out3))


def fill_basis3(basis_ref, basis3_ref):
    ncl, rows = basis_ref.shape
    high, low = cut(basis_ref[...])
    high, low = high.astype(F32), low.astype(F32)
    fill = jnp.zeros((basis3_ref.shape[1] - 3 * ncl, rows), F32)
    basis3_ref[...] = jnp.concatenate([high, high, low, fill], axis=0).T.astype(BF16)


def products_kernel(row_ref, count_ref, basis_ref, stiff_from,
                    stiff_place_ref, stiff_shared_ref, basis_place_ref, pick_basis_ref,
                    pick, place, stiff, basis2, basis3, sems):
    copy = pltpu.make_async_copy(stiff_from, stiff, sems.at[0])
    copy.start()
    fill_pick(row_ref, pick)
    fill_place(row_ref, place)
    weight = 1.0 / count_ref[...].astype(F32)
    fill_basis2(basis_ref, basis2)
    scaled = basis2[...].astype(F32) * weight
    basis_place_ref[...] = dot(scaled.astype(BF16), place[...]).astype(BF16)
    fill_basis3(basis_ref, basis3)
    full = weights_of(count_ref)
    for left in range(0, basis3.shape[1], LANES):
        at = slice(left, left + LANES)
        basis3[:, at] = (basis3[:, at].astype(F32) * full).astype(BF16)
    for lo, n in tiles(pick.shape[0]):
        pick_basis_ref[lo : lo + n, :] = dot(pick[lo : lo + n, :], basis3[...]).astype(BF16)
    copy.wait()

    def product(lo):
        at = pl.ds(lo, FINE)
        stiff_place_ref[at, :] = dot(stiff[at, :], place[...]).astype(BF16)

    def shared(lo):
        at = pl.ds(lo, FINE)
        stiff_shared_ref[at, :] = dot(pick[at, :], stiff_place_ref[...]).astype(BF16)

    each(stiff.shape[0], FINE, product)
    each(pick.shape[0], FINE, shared)


def local_products_kernel(row_ref, count_ref, after_ref, inverse_from, local_place_ref,
                          place, inverse, sems):
    copies = bring([(inverse_from, inverse)], sems)
    fill_place(row_ref, place)
    rows = place.shape[0]
    weight = jnp.broadcast_to(1.0 / count_ref[...].astype(F32), (8, rows)).astype(BF16)
    listed = dot(weight, place[...])[0:1]
    for copy in copies:
        copy.wait()

    def product(lo):
        at = pl.ds(lo, FINE)
        local_place_ref[at, :] = (dot(inverse[at, :], place[...]) * listed).astype(BF16)

    each(rows, FINE, product)


def tables_kernel(row_ref, count_ref, basis_ref, after_ref, stiff_from, stiff_place_from,
                  stiff_shared_from, local_from,
                  pick_ref, place_ref, weight_ref, basis2_ref, basis3_ref,
                  stiff_ref, stiff_place_ref, stiff_shared_ref, local_ref, sems):
    copies = bring(
        [
            (local_from, local_ref),
            (stiff_from, stiff_ref),
            (stiff_shared_from, stiff_shared_ref),
            (stiff_place_from, stiff_place_ref),
        ],
        sems,
    )
    fill_pick(row_ref, pick_ref)
    fill_place(row_ref, place_ref)
    weight_ref[...] = weights_of(count_ref)
    fill_basis2(basis_ref, basis2_ref)
    fill_basis3(basis_ref, basis3_ref)
    for copy in copies:
        copy.wait()


def small_kernel(after_ref, *refs):
    *refs, sems = refs
    number = len(refs) // 2
    for copy in bring(list(zip(refs[:number], refs[number:])), sems):
        copy.wait()


def columns_kernel(map_ref, inverse_from, out_ref, turned, rows, sems):
    parts = rows.shape[0]
    width = rows.shape[2]
    copies = bring(
        [(inverse_from.at[:, pl.ds(k * width, width)], rows.at[k]) for k in range(parts)], sems
    )
    for k in range(parts):
        copies[k].wait()
        turned[k * width : (k + 1) * width, :] = rows[k].T
    size = map_ref.shape[0]
    ncl = out_ref.shape[0] // size

    def step(i, _):
        for k in range(ncl):
            out_ref[pl.ds(i * ncl + k, 1), :] = turned[pl.ds(map_ref[i, k], 1), :]
        return 0

    lax.fori_loop(0, size, step, 0)


def coarse_kernel(map_ref, which_ref, got_ref, keep_ref, send_ref, turned, rowed):
    ncl, half = keep_ref.shape
    width = got_ref.shape[1]
    fill = jnp.zeros((turned.shape[1] - ncl, width), F32)
    for t in range(got_ref.shape[0] // ncl):
        block = jnp.concatenate([got_ref[t * ncl : (t + 1) * ncl, :], fill], axis=0)
        turned[t * width : (t + 1) * width, :] = block.T

    size = map_ref.shape[0]

    def step(i, _):
        for c in range(2):
            for k in range(ncl):
                row = turned[pl.ds(map_ref[2 * i + c, k], 1), :]
                rowed[pl.ds(c * half + i * ncl + k, 1), :] = row
        return 0

    lax.fori_loop(0, size // 2, step, 0)
    first = rowed[:half, :].T[:ncl, :]
    second = rowed[half:, :].T[:ncl, :]
    even = which_ref[0] == 0
    keep_ref[...] = jnp.where(even, first, second)
    send_ref[...] = jnp.where(even, second, first)


def stack_kernel(own_ref, other_ref, terms_ref, out_ref, after_ref):
    after_ref[...] = jnp.zeros_like(after_ref)
    ncl = own_ref.shape[0]
    own_high, own_low = cut(own_ref[...])
    other_high, other_low = cut(other_ref[...])
    out_ref[:ncl, :] = own_high
    out_ref[ncl : 2 * ncl, :] = other_high
    out_ref[2 * ncl : 3 * ncl, :] = own_low
    out_ref[3 * ncl :, :] = other_low


def send_terms(terms, scalars, send_ref):
    block = jnp.concatenate([terms, scalars], axis=0)
    rows = block.shape[0]
    for g in range(send_ref.shape[0] // rows):
        send_ref[g * rows : (g + 1) * rows, :] = block


def front(inverse_ref, weight_ref, pick_ref, cat, local_ref, out_ref, cat2, flat=False):
    large, small = (FINE, FINE) if flat else (HALF, SLOTS)

    def product(lo):
        at = pl.ds(lo, large)
        local = halves(dot(inverse_ref[at, :], cat[...]))
        local_ref[at, :] = local
        cat2[at, :] = pair(weight_ref[at, :] * local)

    def shared(lo):
        at = pl.ds(lo, small)
        out_ref[at, :] = halves(dot(pick_ref[at, :], cat2[...]))

    each(inverse_ref.shape[0], large, product, flat)
    each(pick_ref.shape[0], small, shared, flat)


def first_kernel(loads_ref, a0, a1, a2, a3, row_ref, count_ref, basis_ref, inverse_from,
                 resid_ref, local_ref, pre_ref, send_ref,
                 cat, arr_cat, place, pick, basis2, inverse, weight, cat2, sems):
    copy = pltpu.make_async_copy(inverse_from, inverse, sems.at[0])
    copy.start()
    fill_place(row_ref, place)
    fill_basis2(basis_ref, basis2)
    weight[...] = weights_of(count_ref)
    ncl, rhs = basis_ref.shape[0], loads_ref.shape[1]
    arrivals((a0, a1, a2, a3), arr_cat)
    terms = jnp.zeros((2 * ncl, 2 * rhs), F32)
    for lo, n in tiles(loads_ref.shape[0]):
        at = slice(lo, lo + n)
        resid = loads_ref[at, :] + halves(dot(place[at, :], arr_cat[...]))
        resid_ref[at, :] = resid
        both = pair(weight[at, :] * resid)
        cat[at, :] = both
        terms += dot(basis2[:, at], both)
    send_terms(three(terms, ncl), jnp.zeros((SCAL, rhs), F32), send_ref)
    fill_pick(row_ref, pick)
    copy.wait()
    front(inverse, weight, pick, cat, local_ref, pre_ref, cat2)


def coarse_solve_kernel(got_ref, g_ref, own_ref, other_ref):
    ncl = g_ref.shape[0] // 4
    rows = ncl + SCAL
    groups = got_ref.shape[0] // rows
    got = got_ref[...].reshape(groups, rows, got_ref.shape[1])
    terms = got[:, :ncl].reshape(groups * ncl, got_ref.shape[1])
    scalars = jnp.sum(got[:, ncl:], axis=0)
    values = three(dot(g_ref[...], pair(terms)), 2 * ncl)
    own_ref[:ncl, :] = values[:ncl]
    own_ref[ncl:, :] = scalars
    other_ref[:ncl, :] = values[ncl:]
    other_ref[ncl:, :] = scalars


def back_kernel(own_ref, other_ref, pre_ref, pick_basis_ref,
                values_ref, scal_ref, out0, out1, out2, out3):
    ncl = own_ref.shape[0] - SCAL
    total = own_ref[...] + other_ref[...]
    scal_ref[...] = total[ncl:]
    high, low = cut(total[:ncl])
    fill = jnp.zeros((values_ref.shape[0] - 3 * ncl, high.shape[1]), BF16)
    values = jnp.concatenate([high, low, high, fill], axis=0)
    values_ref[...] = values
    cap = out0.shape[0]
    for j, out in enumerate((out0, out1, out2, out3)):
        at = slice(j * cap, (j + 1) * cap)
        out[...] = pre_ref[at, :] + dot(pick_basis_ref[at, :], values)


def part_kernel(flat, values_ref, local_ref, weight_ref, basis3_ref, stiff_ref, pick_ref,
                part_ref, image_ref, pre_ref, cat, cat2):
    values = values_ref[...]
    small, large, shared_step = (FINE, FINE, FINE) if flat else (TILE, HALF, SLOTS)

    def field(lo):
        at = pl.ds(lo, small)
        part = weight_ref[at, :] * (local_ref[at, :] + dot(basis3_ref[at, :], values))
        part_ref[at, :] = part
        cat[at, :] = pair(part)

    def product(lo):
        at = pl.ds(lo, large)
        image = halves(dot(stiff_ref[at, :], cat[...]))
        image_ref[at, :] = image
        cat2[at, :] = pair(image)

    def shared(lo):
        at = pl.ds(lo, shared_step)
        pre_ref[at, :] = halves(dot(pick_ref[at, :], cat2[...]))

    each(local_ref.shape[0], small, field, flat)
    each(local_ref.shape[0], large, product, flat)
    each(pick_ref.shape[0], shared_step, shared, flat)


def shared_kernel(a0, a1, a2, a3, pre_ref, stiff_shared_ref,
                  arr_ref, out0, out1, out2, out3):
    arrivals((a0, a1, a2, a3), arr_ref)
    cap = out0.shape[0]
    for j, out in enumerate((out0, out1, out2, out3)):
        at = slice(j * cap, (j + 1) * cap)
        out[...] = pre_ref[at, :] + halves(dot(stiff_shared_ref[at, :], arr_ref[...]))


def completed(ref, at, table_ref, arr_ref):
    return ref[at, :] + halves(dot(table_ref[at, :], arr_ref[...]))


def collect(sums, rhs):
    rows = [jnp.sum(s, axis=0, keepdims=True) for s in sums]
    rows.append(jnp.zeros((SCAL - len(rows), rhs), F32))
    return jnp.concatenate(rows, axis=0)


def start_kernel(part_ref, image_ref, arr_ref, r_ref, place_ref, stiff_place_ref,
                 weight_ref, basis2_ref, inverse_from, local_place_from,
                 u_ref, w_ref, terms_ref, sums_ref,
                 inverse_ref, local_place_ref, sems):
    copies = bring(
        [
            (inverse_from, inverse_ref),
            (local_place_from, local_place_ref),
        ],
        sems,
    )
    ncl = basis2_ref.shape[0] // 2
    rhs = r_ref.shape[1]

    def some(lo, carry):
        ru, uw, terms = carry
        at = pl.ds(lo, TILE)
        u = completed(part_ref, at, place_ref, arr_ref)
        w = completed(image_ref, at, stiff_place_ref, arr_ref)
        u_ref[at, :] = u
        w_ref[at, :] = w
        weight = weight_ref[at, :]
        ru += folded(weight * u * r_ref[at, :])
        uw += folded(u * w)
        return ru, uw, terms + dot(basis2_ref[:, at], pair(weight * w))

    zero = jnp.zeros((8, rhs), F32)
    start = (zero, zero, jnp.zeros((2 * ncl, 2 * rhs), F32))
    *sums, terms = summed(r_ref.shape[0], TILE, some, start)
    terms_ref[...] = three(terms, ncl)
    sums_ref[...] = collect(sums, rhs)
    for copy in copies:
        copy.wait()


def second_kernel(part_ref, image_ref, arr_ref, scal_ref, r_ref, u_ref, w_ref,
                  place_ref, stiff_place_ref, weight_ref, basis2_ref,
                  m_ref, z_ref, x1_ref, r1_ref, u1_ref, w1_ref, terms_ref, sums_ref):
    ncl = basis2_ref.shape[0] // 2
    rhs = r_ref.shape[1]
    alpha = scal_ref[0:1, :] / scal_ref[1:2, :]

    def some(lo, carry):
        *sums, terms = carry
        at = pl.ds(lo, TILE)
        m = completed(part_ref, at, place_ref, arr_ref)
        z = completed(image_ref, at, stiff_place_ref, arr_ref)
        m_ref[at, :] = m
        z_ref[at, :] = z
        weight = weight_ref[at, :]
        p, s = u_ref[at, :], w_ref[at, :]
        x1_ref[at, :] = alpha * p
        r1 = r_ref[at, :] - alpha * s
        u1 = p - alpha * m
        w1 = s - alpha * z
        r1_ref[at, :] = r1
        u1_ref[at, :] = u1
        w1_ref[at, :] = w1
        left = weight * s - alpha * z
        weighted = weight * u1
        news = (weighted * r1, u1 * left, weighted * s, p * left)
        sums = [old + folded(new) for old, new in zip(sums, news)]
        return *sums, terms + dot(basis2_ref[:, at], pair(weight * w1))

    start = (jnp.zeros((8, rhs), F32),) * 4 + (jnp.zeros((2 * ncl, 2 * rhs), F32),)
    *sums, terms = summed(r_ref.shape[0], TILE, some, start)
    terms_ref[...] = three(terms, ncl)
    sums_ref[...] = collect(sums, rhs)


def terms_kernel(a0, a1, a2, a3, terms_ref, sums_ref, basis_place_ref, *refs):
    *scal, arr_ref, send_ref = refs
    ncl = terms_ref.shape[0]
    arrivals((a0, a1, a2, a3), arr_ref)
    added = three(dot(basis_place_ref[...], arr_ref[...]), ncl)
    if scal:
        added *= -scal[0][0:1, :] / scal[0][1:2, :]
    send_terms(terms_ref[...] + added, sums_ref[...], send_ref)


def local_part_kernel(w_ref, weight_ref, inverse_ref, pick_ref, local_ref, pre_ref, cat, cat2):
    for lo, n in tiles(w_ref.shape[0], FINE):
        at = slice(lo, lo + n)
        cat[at, :] = pair(weight_ref[at, :] * w_ref[at, :])
    front(inverse_ref, weight_ref, pick_ref, cat, local_ref, pre_ref, cat2, True)


def local_shared_kernel(pre_ref, arr_ref, after_ref, local_place_ref, weight_ref, pick_ref,
                        *refs):
    *scal, out_ref, cat = refs
    for lo, n in tiles(weight_ref.shape[0], FINE):
        at = slice(lo, lo + n)
        came = halves(dot(local_place_ref[at, :], arr_ref[...]))
        cat[at, :] = pair(weight_ref[at, :] * came)
    for lo, n in tiles(pre_ref.shape[0], FINE):
        at = slice(lo, lo + n)
        came = halves(dot(pick_ref[at, :], cat[...]))
        if scal:
            came *= -scal[0][0:1, :] / scal[0][1:2, :]
        out_ref[at, :] = pre_ref[at, :] + came


def complete_kernel(w_part_ref, local_part_ref, arr_ref, after_ref, place_ref, local_place_ref,
                    *refs):
    *more, w_ref, local_ref = refs
    if more:
        scal_ref, z_part_ref, z_ref = more
        factor = -scal_ref[0:1, :] / scal_ref[1:2, :]

    def some(lo):
        at = pl.ds(lo, TILE)
        came = halves(dot(place_ref[at, :], arr_ref[...]))
        local = halves(dot(local_place_ref[at, :], arr_ref[...]))
        if more:
            z_ref[at, :] = z_part_ref[at, :] + came
            came, local = factor * came, factor * local
        w_ref[at, :] = w_part_ref[at, :] + came
        local_ref[at, :] = local_part_ref[at, :] + local

    each(w_ref.shape[0], TILE, some)


def step_scalars(before, now):
    beta = now[0:1, :] / before[0:1, :]
    energy = now[1:2, :] + beta * (now[2:3, :] + now[3:4, :]) + beta * beta * before[1:2, :]
    return beta, now[0:1, :] / energy, energy


def third_kernel(part_ref, image_ref, arr_ref, before_ref, scal_ref,
                 x1_ref, r1_ref, u1_ref, w1_ref, p_ref, s_ref, q_ref, z_ref,
                 place_ref, stiff_place_ref, weight_ref,
                 send_ref, state_ref, x2_ref, r2_ref, u2_ref, half_ref, p1_ref, s1_ref):
    rhs = r1_ref.shape[1]
    beta, alpha, energy = step_scalars(before_ref[...], scal_ref[...])

    def some(lo, sums):
        at = pl.ds(lo, TILE)
        m = completed(part_ref, at, place_ref, arr_ref)
        image = completed(image_ref, at, stiff_place_ref, arr_ref)
        p1 = u1_ref[at, :] + beta * p_ref[at, :]
        s1 = w1_ref[at, :] + beta * s_ref[at, :]
        q1 = m + beta * q_ref[at, :]
        r2 = r1_ref[at, :] - alpha * s1
        u2 = u1_ref[at, :] - alpha * q1
        half = w1_ref[at, :] - (alpha * beta) * z_ref[at, :]
        weight = weight_ref[at, :]
        left = weight * half - alpha * image
        weighted = weight * u2
        x2_ref[at, :] = x1_ref[at, :] + alpha * p1
        r2_ref[at, :] = r2
        u2_ref[at, :] = u2
        half_ref[at, :] = half - alpha * image
        p1_ref[at, :] = p1
        s1_ref[at, :] = s1
        news = (weighted * r2, u2 * left, weighted * s1, p1 * left)
        return tuple(old + folded(new) for old, new in zip(sums, news))

    sums = summed(r1_ref.shape[0], TILE, some, (jnp.zeros((8, rhs), F32),) * 4)
    wide = jnp.concatenate([jnp.sum(s, axis=0, keepdims=True) for s in sums], axis=1)
    send_ref[...] = jnp.broadcast_to(wide, send_ref.shape)
    state_ref[...] = jnp.concatenate(
        [scal_ref[0:1, :], energy, alpha, jnp.zeros((SCAL - 3, rhs), F32)], axis=0
    )


def last_kernel(state_ref, got_ref, a0, a1, a2, a3, place_ref,
                x2, u2, p1, r2, half, s1,
                x3_to, r3_to, arr_cat, x3, r3, out_sems):
    state = state_ref[...]
    total = jnp.sum(got_ref[...], axis=0, keepdims=True)
    rhs = state.shape[1]
    now = jnp.concatenate([total[:, k * rhs : (k + 1) * rhs] for k in range(4)], axis=0)
    beta, alpha, _ = step_scalars(state, now)
    old = state[2:3, :]
    arrivals((a0, a1, a2, a3), arr_cat)
    outs = []
    for i, (lo, n) in enumerate(tiles(r2.shape[0])):
        at = slice(lo, lo + n)
        x3[at, :] = x2[at, :] + alpha * (u2[at, :] + beta * p1[at, :])
        w2 = half[at, :] - old * halves(dot(place_ref[at, :], arr_cat[...]))
        r3[at, :] = r2[at, :] - alpha * (w2 + beta * s1[at, :])
        rows = pl.ds(lo, n)
        outs += bring(
            [(x3.at[rows, :], x3_to.at[rows, :]), (r3.at[rows, :], r3_to.at[rows, :])],
            out_sems.at[i],
        )
    for copy in outs:
        copy.wait()


def body(
    stiffness, local_inverse, coarse_basis, loads, counts, shared_rows, coarse_map, coarse_inverse
):
    size = lax.axis_size("sub")
    me = lax.axis_index("sub")
    rows, rhs = loads.shape[1:]
    ncl = coarse_basis.shape[1]
    slots, cap = shared_rows.shape[1:]
    order = coarse_inverse.shape[1]
    lists = slots * cap
    stiff, inverse = aside(stiffness[0], local_inverse[0])

    def partner(distance, parity):
        def of(i):
            up = (i // distance) % 2 == parity
            return (i + distance if up else i - distance) % size

        return [(i, of(i)) for i in range(size)]

    inside = partner(1, 0)
    swaps = [inside, partner(1, 1), partner(STRIDE, 0), partner(STRIDE, 1)]
    swaps = [swaps[j] for j in ORDER]

    def exchange(outs):
        return [lax.ppermute(out, "sub", swap) for out, swap in zip(outs, swaps)]

    cores = [[2 * i + c for i in range(size // 2)] for c in range(2)]
    groups = size // 2
    block = ncl + SCAL

    fields = (rows, rhs)
    out4 = [far((cap, rhs))] * 4
    wide = pltpu.VMEM((rows, 2 * rhs), BF16)
    wide_arr = pltpu.VMEM((lists, 2 * rhs), BF16)
    place_like = pltpu.VMEM((rows, lists), BF16)
    pick_like = pltpu.VMEM((lists, rows), BF16)
    basis = coarse_basis[0]
    (loads_aside,) = aside(loads[0])

    listed, maps, *outs = call(
        loads_kernel,
        "loads",
        (*aside(shared_rows[0]), loads_aside, *aside(coarse_map)),
        [far((1, lists), jnp.int32), far((size, LANES * pl.cdiv(ncl, LANES)), jnp.int32)] + out4,
        [
            pick_like,
            wide,
            pltpu.VMEM(fields, F32),
            pltpu.VMEM((slots, cap), jnp.int32),
            pltpu.VMEM((1, ncl), jnp.int32),
            pltpu.SemaphoreType.DMA((3,)),
        ],
        {0: ASPEC, 1: ASPEC, 2: ASPEC},
    )
    arrived = exchange(outs)
    maps = lax.all_to_all(maps, "sub", 0, 0, tiled=True)
    maps, *arrived = lax.optimization_barrier((maps, *arrived))


    (picked,) = call(
        columns_kernel,
        "coarse_columns",
        (maps, *aside(coarse_inverse)),
        [far((size * ncl, coarse_inverse.shape[0]))],
        [
            pltpu.VMEM((order, coarse_inverse.shape[0]), F32),
            pltpu.VMEM((4, coarse_inverse.shape[0], order // 4), F32),
            pltpu.SemaphoreType.DMA((4,)),
        ],
        {0: SSPEC, 1: ASPEC},
        mib=30,
    )
    mine_rows = lax.all_to_all(picked, "sub", 0, 0, tiled=True)

    r0, local, pre, send = call(
        first_kernel,
        "residual_and_terms",
        (loads[0], *arrived, listed, counts, basis, inverse),
        [away(fields), away(fields), away((lists, rhs)), far((groups * block, rhs))],
        [
            wide,
            wide_arr,
            place_like,
            pick_like,
            pltpu.VMEM((2 * ncl, rows), BF16),
            pltpu.VMEM((rows, rows), BF16),
            pltpu.VMEM(fields, F32),
            wide,
            pltpu.SemaphoreType.DMA((1,)),
        ],
        {8: ASPEC},
        us=6,
        mib=30,
    )
    products = call(
        products_kernel,
        "products",
        (listed, counts, basis, stiff),
        [
            away((rows, lists), BF16),
            away((lists, lists), BF16),
            away((2 * ncl, lists), BF16),
            away((lists, 2 * LANES), BF16),
        ],
        [
            pick_like,
            place_like,
            pltpu.VMEM((rows, rows), BF16),
            pltpu.VMEM((2 * ncl, rows), BF16),
            pltpu.VMEM((rows, 2 * LANES), BF16),
            pltpu.SemaphoreType.DMA((1,)),
        ],
        {3: ASPEC},
        us=10,
        mib=30,
    )
    r0, local, pre = aside(r0, local, pre)

    keep, pass_on = call(
        coarse_kernel,
        "coarse_block",
        (maps, (me % 2).reshape(1), mine_rows),
        [far((ncl, groups * ncl)), far((ncl, groups * ncl))],
        [
            pltpu.VMEM((order, LANES), F32),
            pltpu.VMEM((size * ncl, LANES), F32),
        ],
        {0: SSPEC, 1: SSPEC},
        mib=30,
    )
    passed = lax.ppermute(pass_on, "sub", inside)

    def share(send):
        return lax.all_to_all(send, "sub", 0, 0, tiled=True, axis_index_groups=cores)

    send, *products = lax.optimization_barrier((send, *products))
    terms = share(send)
    local_products = call(
        local_products_kernel,
        "local_products",
        (listed, counts, send, inverse),
        [away((rows, lists), BF16)],
        [place_like, pltpu.VMEM((rows, rows), BF16), pltpu.SemaphoreType.DMA((1,))],
        {2: ASPEC, 3: ASPEC},
        us=10,
        mib=30,
    )
    terms, *local_products = lax.optimization_barrier((terms, *local_products))
    local_products = aside(*local_products)
    coarse, after = call(
        stack_kernel,
        "coarse_addends",
        (keep, passed, terms),
        [near((4 * ncl, groups * ncl), BF16), far((SCAL, LANES))],
    )
    stiff_place, stiff_shared, basis_place, pick_basis = aside(*products)
    tables = held(*call(
        tables_kernel,
        "tables",
        (listed, counts, basis, after, stiff, stiff_place, stiff_shared, local),
        [
            near((lists, rows), BF16),
            near((rows, lists), BF16),
            near(fields),
            near((2 * ncl, rows), BF16),
            near((rows, 2 * LANES), BF16),
            near((rows, rows), BF16),
            near((rows, lists), BF16),
            near((lists, lists), BF16),
            near(fields),
        ],
        [pltpu.SemaphoreType.DMA((4,))],
        {4: ASPEC, 5: ASPEC, 6: ASPEC, 7: ASPEC},
        us=5,
    ))
    pick, place, weight, basis2, basis3, stiff, stiff_place, stiff_shared, local = tables
    (coarse,) = held(coarse)

    def correct(terms, pre, bring_in=None):
        own, other = call(
            coarse_solve_kernel,
            "coarse_solve",
            (terms, coarse),
            [far((block, rhs)), far((block, rhs))],
            us=1,
        )
        came = lax.ppermute(other, "sub", inside)
        if bring_in:
            small.extend(bring_in(own))
        values, scal, *outs = call(
            back_kernel,
            "coarse_back",
            (own, came, pre(own), small[0]),
            [near((2 * LANES, rhs), BF16), far((SCAL, rhs))] + out4,
            us=1,
        )
        return *held(values), scal, exchange(outs)

    small = []

    def bring_small(own):
        return held(*call(
            small_kernel,
            "small_tables",
            (own, pick_basis, basis_place, pre),
            [near(pick_basis.shape, BF16), near(basis_place.shape, BF16), near(pre.shape)],
            [pltpu.SemaphoreType.DMA((3,))],
            {1: ASPEC, 2: ASPEC, 3: ASPEC},
            us=1,
        ))

    def operate(values, local, arrived, flat=False):
        part, image, pre = held(*call(
            functools.partial(part_kernel, flat),
            "field_part",
            (values, local, weight, basis3, stiff, pick),
            [near(fields), near(fields), near((lists, rhs))],
            [wide, wide],
            us=3,
        ))
        arr, *outs = call(
            shared_kernel,
            "image_shared",
            (*arrived, pre, stiff_shared),
            [near((lists, 2 * rhs), BF16)] + out4,
            us=1,
        )
        return part, image, *held(arr), exchange(outs)

    def share_terms(arrived, terms, sums, *scal):
        arr, send = call(
            terms_kernel,
            "terms",
            (*arrived, terms, sums, small[1], *scal),
            [near((lists, 2 * rhs), BF16), far((groups * block, rhs))],
            us=1,
        )
        return *held(arr), share(send)

    def local_part(w):
        return held(*call(
            local_part_kernel,
            "local_part",
            (w, weight, inverse, pick),
            [near(fields), near((lists, rhs))],
            [wide, wide],
            us=3,
        ))

    def local_shared(pre, arr, *scal):
        def of(own):
            return held(*call(
                local_shared_kernel,
                "local_shared",
                (pre, arr, own, local_place, weight, pick, *scal),
                [near((lists, rhs))],
                [wide],
                us=1,
            ))[0]

        return of

    def complete(w, local, arr, after, *more):
        return held(*call(
            complete_kernel,
            "complete",
            (w, local, arr, after, place, local_place, *more),
            [near(fields)] * (3 if more else 2),
            us=2,
        ))

    values, _, arrived = correct(terms, lambda own: small[2], bring_small)
    part, image, arr, arrived = operate(values, local, arrived, True)
    u0, w0, terms, sums, inverse, local_place = held(*call(
        start_kernel,
        "start",
        (part, image, arr, r0, place, stiff_place, weight, basis2, inverse, *local_products),
        [near(fields), near(fields), near((ncl, rhs)), near((SCAL, rhs))]
        + [near((rows, rows), BF16), near((rows, lists), BF16)],
        [pltpu.SemaphoreType.DMA((2,))],
        {8: ASPEC, 9: ASPEC},
        us=3,
    ))
    local, pre = local_part(w0)
    terms, pre = held(*lax.optimization_barrier((terms, pre)))
    arr, terms = share_terms(arrived, terms, sums)
    values, scal0, arrived = correct(terms, local_shared(pre, arr))
    w0, local = complete(w0, local, arr, values)
    part, image, arr, arrived = operate(values, local, arrived)
    m0, z0, x1, r1, u1, w1, terms, sums = held(*call(
        second_kernel,
        "first_update",
        (part, image, arr, scal0, r0, u0, w0, place, stiff_place, weight, basis2),
        [near(fields)] * 6 + [near((ncl, rhs)), near((SCAL, rhs))],
        us=4,
    ))
    local, pre = local_part(w1)
    terms, pre = held(*lax.optimization_barrier((terms, pre)))
    arr, terms = share_terms(arrived, terms, sums, scal0)
    values, scal1, arrived = correct(terms, local_shared(pre, arr, scal0))
    z0, w1, local = complete(w1, local, arr, values, scal0, z0)

    part, image, arr, arrived = operate(values, local, arrived)
    pieces = len(tiles(rows))
    send, state, *news = call(
        third_kernel,
        "second_update",
        (part, image, arr, scal0, scal1, x1, r1, u1, w1, u0, w0, m0, z0)
        + (place, stiff_place, weight),
        [far((size, 4 * rhs)), far((SCAL, rhs))] + [near(fields)] * 6,
        us=4,
    )
    x2, r2, u2, half, p1, s1 = held(*news)
    send, *arrived = lax.optimization_barrier((send, *arrived))
    sums = lax.all_to_all(send, "sub", 0, 0, tiled=True)
    sums, *arrived = lax.optimization_barrier((sums, *arrived))
    x3, r3 = call(
        last_kernel,
        "last_update",
        (state, sums, *arrived, place, x2, u2, p1, r2, half, s1),
        [far(fields), far(fields)],
        [wide_arr, pltpu.VMEM(fields, F32), pltpu.VMEM(fields, F32)]
        + [pltpu.SemaphoreType.DMA((pieces, 2))],
        sent=range(2),
    )
    return (x3[None], r3[None])


def solution(mesh):
    placed = (
        P("sub", None, None),
        P("sub", None, None),
        P("sub", None, None),
        P("sub", None, None),
        P("sub", None),
        P("sub", None, None),
        P("sub", None),
        P("sub", None),
    )
    return jax.shard_map(
        body,
        mesh=mesh,
        in_specs=placed,
        out_specs=(P("sub", None, None), P("sub", None, None)),
        check_vma=False,
    )
```

```python
import functools

import jax
import jax.numpy as jnp
from jax import lax
from jax.experimental import pallas as pl
from jax.experimental.pallas import tpu as pltpu
from jax.sharding import PartitionSpec as P

STRIDE = 8
F32 = jnp.float32
BF16 = jnp.bfloat16
TILE = 512
FINE = 256
HALF = 768
SLOTS = 512
SCAL = 8
ORDER = (3, 0, 1, 2)
LANES = 128

VSPEC = pl.BlockSpec(memory_space=pltpu.VMEM)
SSPEC = pl.BlockSpec(memory_space=pltpu.SMEM)
ASPEC = pl.BlockSpec(memory_space=pltpu.HBM)


def near(shape, dtype=F32):
    return pltpu.VMEM(shape, dtype)


def far(shape, dtype=F32):
    return jax.ShapeDtypeStruct(shape, dtype)


def away(shape, dtype=F32):
    return pltpu.HBM(shape, dtype)


def held(*arrays):
    return tuple(pltpu.with_memory_space_constraint(a, pltpu.VMEM) for a in arrays)


def aside(*arrays):
    return tuple(pltpu.with_memory_space_constraint(a, pltpu.HBM) for a in arrays)


def call(kernel, name, args, outs, scratch=(), specs=None, us=2, mib=16, sent=()):
    specs = specs or {}
    return pl.pallas_call(
        kernel,
        name=name,
        out_shape=tuple(outs),
        in_specs=[specs.get(i, VSPEC) for i in range(len(args))],
        out_specs=tuple(ASPEC if i in sent else VSPEC for i in range(len(outs))),
        scratch_shapes=list(scratch),
        compiler_params=pltpu.CompilerParams(vmem_limit_bytes=mib * 1024 * 1024),
        cost_estimate=pl.CostEstimate(
            flops=0, bytes_accessed=us * 3_000_000, transcendentals=0
        ),
    )(*args)


def cut(x):
    high = x.astype(BF16)
    return high, (x - high.astype(F32)).astype(BF16)


def pair(x):
    return jnp.concatenate(cut(x), axis=1)


def halves(product):
    half = product.shape[1] // 2
    return product[:, :half] + product[:, half:]


def three(product, rows):
    half = product.shape[1] // 2
    return product[:rows, :half] + product[:rows, half:] + product[rows : 2 * rows, :half]


def dot(a, b):
    return jnp.dot(a, b, preferred_element_type=F32)


def tiles(total, step=TILE):
    step = min(step, total)
    return [(lo, min(step, total - lo)) for lo in range(0, total, step)]


def folded(x):
    return jnp.sum(x.reshape(-1, 8, x.shape[-1]), axis=0)


def pick_out(pick_ref, cat_ref, out_refs):
    cap = out_refs[0].shape[0]
    for j, out in enumerate(out_refs):
        out[...] = halves(dot(pick_ref[j * cap : (j + 1) * cap, :], cat_ref[...]))


def arrivals(arrived_refs, arr_cat):
    cap = arrived_refs[0].shape[0]
    for j, ref in enumerate(arrived_refs):
        arr_cat[j * cap : (j + 1) * cap, :] = pair(ref[...])


def bring(pairs, sems):
    copies = [pltpu.make_async_copy(*p, sems.at[i]) for i, p in enumerate(pairs)]
    for copy in copies:
        copy.start()
    return copies


def each(total, step, work, flat=False):
    if flat:
        for lo in range(0, total, step):
            work(lo)
        return

    def one(i, carry):
        work(pl.multiple_of(i * step, step))
        return carry

    lax.fori_loop(0, total // step, one, 0)


def summed(total, step, work, start):
    def one(i, carry):
        return work(pl.multiple_of(i * step, step), carry)

    return lax.fori_loop(0, total // step, one, start)


def fill_pick(row_ref, pick_ref):
    slots, rows = pick_ref.shape

    def some(lo):
        listed = row_ref[:, pl.ds(lo, LANES)].astype(F32)
        entries = jnp.broadcast_to(listed, (LANES, LANES)).T
        for left in range(0, rows, LANES):
            at = left + lax.broadcasted_iota(jnp.int32, (LANES, LANES), 1)
            same = jnp.where(at.astype(F32) == entries, 1.0, 0.0)
            pick_ref[pl.ds(lo, LANES), left : left + LANES] = same.astype(BF16)

    each(slots, LANES, some)


def fill_place(row_ref, place_ref):
    rows, slots = place_ref.shape

    def some(lo):
        at = lo + lax.broadcasted_iota(jnp.int32, (LANES, slots), 0)
        same = jnp.where(at == row_ref[...], 1.0, 0.0)
        place_ref[pl.ds(lo, LANES), :] = same.astype(BF16)

    each(rows, LANES, some)


def weights_of(count_ref):
    rows = count_ref.shape[1]
    return jnp.broadcast_to(1.0 / count_ref[...].astype(F32), (LANES, rows)).T


def fill_basis2(basis_ref, basis2_ref):
    ncl = basis_ref.shape[0]
    high, low = cut(basis_ref[...])
    basis2_ref[:ncl, :] = high
    basis2_ref[ncl:, :] = low


def loads_kernel(rows_from, loads_from, map_from, listed_ref, maps_ref, out0, out1, out2, out3,
                 pick, cat, loads, rows_ref, map_ref, sems):
    *firsts, last = bring([(rows_from, rows_ref), (map_from, map_ref), (loads_from, loads)], sems)
    copies = [last]
    for copy in firsts:
        copy.wait()
    size, ncl = maps_ref.shape[0], map_ref.shape[1]
    maps_ref[...] = jnp.zeros_like(maps_ref)
    maps_ref[:, :ncl] = jnp.broadcast_to(map_ref[...], (size, ncl))
    me = lax.axis_index("sub")
    one = me % 2 == 0
    far_one = (me // STRIDE) % 2 == 0
    given = [rows_ref[k : k + 1, :] for k in range(4)]
    lists = [
        jnp.where(one, given[0], given[1]),
        jnp.where(one, given[1], given[0]),
        jnp.where(far_one, given[2], given[3]),
        jnp.where(far_one, given[3], given[2]),
    ]
    listed_ref[...] = jnp.concatenate([lists[j] for j in ORDER], axis=1)
    fill_pick(listed_ref, pick)
    for copy in copies:
        copy.wait()
    for lo, n in tiles(loads.shape[0]):
        cat[lo : lo + n, :] = pair(loads[lo : lo + n, :])
    pick_out(pick, cat, (out0, out1, out2, out3))


def fill_basis3(basis_ref, basis3_ref):
    ncl, rows = basis_ref.shape
    high, low = cut(basis_ref[...])
    high, low = high.astype(F32), low.astype(F32)
    fill = jnp.zeros((basis3_ref.shape[1] - 3 * ncl, rows), F32)
    basis3_ref[...] = jnp.concatenate([high, high, low, fill], axis=0).T.astype(BF16)


def products_kernel(row_ref, count_ref, basis_ref, stiff_from,
                    stiff_place_ref, stiff_shared_ref, basis_place_ref, pick_basis_ref,
                    pick, place, stiff, basis2, basis3, sems):
    copy = pltpu.make_async_copy(stiff_from, stiff, sems.at[0])
    copy.start()
    fill_pick(row_ref, pick)
    fill_place(row_ref, place)
    weight = 1.0 / count_ref[...].astype(F32)
    fill_basis2(basis_ref, basis2)
    scaled = basis2[...].astype(F32) * weight
    basis_place_ref[...] = dot(scaled.astype(BF16), place[...]).astype(BF16)
    fill_basis3(basis_ref, basis3)
    full = weights_of(count_ref)
    for left in range(0, basis3.shape[1], LANES):
        at = slice(left, left + LANES)
        basis3[:, at] = (basis3[:, at].astype(F32) * full).astype(BF16)
    for lo, n in tiles(pick.shape[0]):
        pick_basis_ref[lo : lo + n, :] = dot(pick[lo : lo + n, :], basis3[...]).astype(BF16)
    copy.wait()

    def product(lo):
        at = pl.ds(lo, FINE)
        stiff_place_ref[at, :] = dot(stiff[at, :], place[...]).astype(BF16)

    def shared(lo):
        at = pl.ds(lo, FINE)
        stiff_shared_ref[at, :] = dot(pick[at, :], stiff_place_ref[...]).astype(BF16)

    each(stiff.shape[0], FINE, product)
    each(pick.shape[0], FINE, shared)


def local_products_kernel(row_ref, count_ref, after_ref, inverse_from, local_place_ref,
                          place, inverse, sems):
    copies = bring([(inverse_from, inverse)], sems)
    fill_place(row_ref, place)
    rows = place.shape[0]
    weight = jnp.broadcast_to(1.0 / count_ref[...].astype(F32), (8, rows)).astype(BF16)
    listed = dot(weight, place[...])[0:1]
    for copy in copies:
        copy.wait()

    def product(lo):
        at = pl.ds(lo, FINE)
        local_place_ref[at, :] = (dot(inverse[at, :], place[...]) * listed).astype(BF16)

    each(rows, FINE, product)


def tables_kernel(row_ref, count_ref, basis_ref, after_ref, stiff_from, stiff_place_from,
                  stiff_shared_from, local_from,
                  pick_ref, place_ref, weight_ref, basis2_ref, basis3_ref,
                  stiff_ref, stiff_place_ref, stiff_shared_ref, local_ref, sems):
    copies = bring(
        [
            (local_from, local_ref),
            (stiff_from, stiff_ref),
            (stiff_shared_from, stiff_shared_ref),
            (stiff_place_from, stiff_place_ref),
        ],
        sems,
    )
    fill_pick(row_ref, pick_ref)
    fill_place(row_ref, place_ref)
    weight_ref[...] = weights_of(count_ref)
    fill_basis2(basis_ref, basis2_ref)
    fill_basis3(basis_ref, basis3_ref)
    for copy in copies:
        copy.wait()


def small_kernel(after_ref, *refs):
    *refs, sems = refs
    number = len(refs) // 2
    for copy in bring(list(zip(refs[:number], refs[number:])), sems):
        copy.wait()


def columns_kernel(map_ref, inverse_from, out_ref, turned, rows, sems):
    parts = rows.shape[0]
    width = rows.shape[2]
    copies = bring(
        [(inverse_from.at[:, pl.ds(k * width, width)], rows.at[k]) for k in range(parts)], sems
    )
    for k in range(parts):
        copies[k].wait()
        turned[k * width : (k + 1) * width, :] = rows[k].T
    size = map_ref.shape[0]
    ncl = out_ref.shape[0] // size

    def step(i, _):
        for k in range(ncl):
            out_ref[pl.ds(i * ncl + k, 1), :] = turned[pl.ds(map_ref[i, k], 1), :]
        return 0

    lax.fori_loop(0, size, step, 0)


def coarse_kernel(map_ref, which_ref, got_ref, keep_ref, send_ref, turned, rowed):
    ncl, half = keep_ref.shape
    width = got_ref.shape[1]
    fill = jnp.zeros((turned.shape[1] - ncl, width), F32)
    for t in range(got_ref.shape[0] // ncl):
        block = jnp.concatenate([got_ref[t * ncl : (t + 1) * ncl, :], fill], axis=0)
        turned[t * width : (t + 1) * width, :] = block.T

    size = map_ref.shape[0]

    def step(i, _):
        for c in range(2):
            for k in range(ncl):
                row = turned[pl.ds(map_ref[2 * i + c, k], 1), :]
                rowed[pl.ds(c * half + i * ncl + k, 1), :] = row
        return 0

    lax.fori_loop(0, size // 2, step, 0)
    first = rowed[:half, :].T[:ncl, :]
    second = rowed[half:, :].T[:ncl, :]
    even = which_ref[0] == 0
    keep_ref[...] = jnp.where(even, first, second)
    send_ref[...] = jnp.where(even, second, first)


def stack_kernel(own_ref, other_ref, terms_ref, out_ref, after_ref):
    after_ref[...] = jnp.zeros_like(after_ref)
    ncl = own_ref.shape[0]
    own_high, own_low = cut(own_ref[...])
    other_high, other_low = cut(other_ref[...])
    out_ref[:ncl, :] = own_high
    out_ref[ncl : 2 * ncl, :] = other_high
    out_ref[2 * ncl : 3 * ncl, :] = own_low
    out_ref[3 * ncl :, :] = other_low


def send_terms(terms, scalars, send_ref):
    block = jnp.concatenate([terms, scalars], axis=0)
    rows = block.shape[0]
    for g in range(send_ref.shape[0] // rows):
        send_ref[g * rows : (g + 1) * rows, :] = block


def front(inverse_ref, weight_ref, pick_ref, cat, local_ref, out_ref, cat2, flat=False):
    large, small = (FINE, FINE) if flat else (HALF, SLOTS)

    def product(lo):
        at = pl.ds(lo, large)
        local = halves(dot(inverse_ref[at, :], cat[...]))
        local_ref[at, :] = local
        cat2[at, :] = pair(weight_ref[at, :] * local)

    def shared(lo):
        at = pl.ds(lo, small)
        out_ref[at, :] = halves(dot(pick_ref[at, :], cat2[...]))

    each(inverse_ref.shape[0], large, product, flat)
    each(pick_ref.shape[0], small, shared, flat)


def first_kernel(loads_ref, a0, a1, a2, a3, row_ref, count_ref, basis_ref, inverse_from,
                 resid_ref, local_ref, pre_ref, send_ref,
                 cat, arr_cat, place, pick, basis2, inverse, weight, cat2, sems):
    copy = pltpu.make_async_copy(inverse_from, inverse, sems.at[0])
    copy.start()
    fill_place(row_ref, place)
    fill_basis2(basis_ref, basis2)
    weight[...] = weights_of(count_ref)
    ncl, rhs = basis_ref.shape[0], loads_ref.shape[1]
    arrivals((a0, a1, a2, a3), arr_cat)
    terms = jnp.zeros((2 * ncl, 2 * rhs), F32)
    for lo, n in tiles(loads_ref.shape[0]):
        at = slice(lo, lo + n)
        resid = loads_ref[at, :] + halves(dot(place[at, :], arr_cat[...]))
        resid_ref[at, :] = resid
        both = pair(weight[at, :] * resid)
        cat[at, :] = both
        terms += dot(basis2[:, at], both)
    send_terms(three(terms, ncl), jnp.zeros((SCAL, rhs), F32), send_ref)
    fill_pick(row_ref, pick)
    copy.wait()
    front(inverse, weight, pick, cat, local_ref, pre_ref, cat2)


def coarse_solve_kernel(got_ref, g_ref, own_ref, other_ref):
    ncl = g_ref.shape[0] // 4
    rows = ncl + SCAL
    groups = got_ref.shape[0] // rows
    got = got_ref[...].reshape(groups, rows, got_ref.shape[1])
    terms = got[:, :ncl].reshape(groups * ncl, got_ref.shape[1])
    scalars = jnp.sum(got[:, ncl:], axis=0)
    values = three(dot(g_ref[...], pair(terms)), 2 * ncl)
    own_ref[:ncl, :] = values[:ncl]
    own_ref[ncl:, :] = scalars
    other_ref[:ncl, :] = values[ncl:]
    other_ref[ncl:, :] = scalars


def back_kernel(own_ref, other_ref, pre_ref, pick_basis_ref,
                values_ref, scal_ref, out0, out1, out2, out3):
    ncl = own_ref.shape[0] - SCAL
    total = own_ref[...] + other_ref[...]
    scal_ref[...] = total[ncl:]
    high, low = cut(total[:ncl])
    fill = jnp.zeros((values_ref.shape[0] - 3 * ncl, high.shape[1]), BF16)
    values = jnp.concatenate([high, low, high, fill], axis=0)
    values_ref[...] = values
    cap = out0.shape[0]
    for j, out in enumerate((out0, out1, out2, out3)):
        at = slice(j * cap, (j + 1) * cap)
        out[...] = pre_ref[at, :] + dot(pick_basis_ref[at, :], values)


def part_kernel(flat, values_ref, local_ref, weight_ref, basis3_ref, stiff_ref, pick_ref,
                part_ref, image_ref, pre_ref, cat, cat2):
    values = values_ref[...]
    small, large, shared_step = (FINE, FINE, FINE) if flat else (TILE, HALF, SLOTS)

    def field(lo):
        at = pl.ds(lo, small)
        part = weight_ref[at, :] * (local_ref[at, :] + dot(basis3_ref[at, :], values))
        part_ref[at, :] = part
        cat[at, :] = pair(part)

    def product(lo):
        at = pl.ds(lo, large)
        image = halves(dot(stiff_ref[at, :], cat[...]))
        image_ref[at, :] = image
        cat2[at, :] = pair(image)

    def shared(lo):
        at = pl.ds(lo, shared_step)
        pre_ref[at, :] = halves(dot(pick_ref[at, :], cat2[...]))

    each(local_ref.shape[0], small, field, flat)
    each(local_ref.shape[0], large, product, flat)
    each(pick_ref.shape[0], shared_step, shared, flat)


def shared_kernel(a0, a1, a2, a3, pre_ref, stiff_shared_ref,
                  arr_ref, out0, out1, out2, out3):
    arrivals((a0, a1, a2, a3), arr_ref)
    cap = out0.shape[0]
    for j, out in enumerate((out0, out1, out2, out3)):
        at = slice(j * cap, (j + 1) * cap)
        out[...] = pre_ref[at, :] + halves(dot(stiff_shared_ref[at, :], arr_ref[...]))


def completed(ref, at, table_ref, arr_ref):
    return ref[at, :] + halves(dot(table_ref[at, :], arr_ref[...]))


def collect(sums, rhs):
    rows = [jnp.sum(s, axis=0, keepdims=True) for s in sums]
    rows.append(jnp.zeros((SCAL - len(rows), rhs), F32))
    return jnp.concatenate(rows, axis=0)


def start_kernel(part_ref, image_ref, arr_ref, r_ref, place_ref, stiff_place_ref,
                 weight_ref, basis2_ref, inverse_from, local_place_from,
                 u_ref, w_ref, terms_ref, sums_ref,
                 inverse_ref, local_place_ref, sems):
    copies = bring(
        [
            (inverse_from, inverse_ref),
            (local_place_from, local_place_ref),
        ],
        sems,
    )
    ncl = basis2_ref.shape[0] // 2
    rhs = r_ref.shape[1]

    def some(lo, carry):
        ru, uw, terms = carry
        at = pl.ds(lo, TILE)
        u = completed(part_ref, at, place_ref, arr_ref)
        w = completed(image_ref, at, stiff_place_ref, arr_ref)
        u_ref[at, :] = u
        w_ref[at, :] = w
        weight = weight_ref[at, :]
        ru += folded(weight * u * r_ref[at, :])
        uw += folded(u * w)
        return ru, uw, terms + dot(basis2_ref[:, at], pair(weight * w))

    zero = jnp.zeros((8, rhs), F32)
    start = (zero, zero, jnp.zeros((2 * ncl, 2 * rhs), F32))
    *sums, terms = summed(r_ref.shape[0], TILE, some, start)
    terms_ref[...] = three(terms, ncl)
    sums_ref[...] = collect(sums, rhs)
    for copy in copies:
        copy.wait()


def second_kernel(part_ref, image_ref, arr_ref, scal_ref, r_ref, u_ref, w_ref,
                  place_ref, stiff_place_ref, weight_ref, basis2_ref,
                  m_ref, z_ref, x1_ref, r1_ref, u1_ref, w1_ref, terms_ref, sums_ref):
    ncl = basis2_ref.shape[0] // 2
    rhs = r_ref.shape[1]
    alpha = scal_ref[0:1, :] / scal_ref[1:2, :]

    def some(lo, carry):
        *sums, terms = carry
        at = pl.ds(lo, TILE)
        m = completed(part_ref, at, place_ref, arr_ref)
        z = completed(image_ref, at, stiff_place_ref, arr_ref)
        m_ref[at, :] = m
        z_ref[at, :] = z
        weight = weight_ref[at, :]
        p, s = u_ref[at, :], w_ref[at, :]
        x1_ref[at, :] = alpha * p
        r1 = r_ref[at, :] - alpha * s
        u1 = p - alpha * m
        w1 = s - alpha * z
        r1_ref[at, :] = r1
        u1_ref[at, :] = u1
        w1_ref[at, :] = w1
        left = weight * s - alpha * z
        weighted = weight * u1
        news = (weighted * r1, u1 * left, weighted * s, p * left)
        sums = [old + folded(new) for old, new in zip(sums, news)]
        return *sums, terms + dot(basis2_ref[:, at], pair(weight * w1))

    start = (jnp.zeros((8, rhs), F32),) * 4 + (jnp.zeros((2 * ncl, 2 * rhs), F32),)
    *sums, terms = summed(r_ref.shape[0], TILE, some, start)
    terms_ref[...] = three(terms, ncl)
    sums_ref[...] = collect(sums, rhs)


def terms_kernel(a0, a1, a2, a3, terms_ref, sums_ref, basis_place_ref, *refs):
    *scal, arr_ref, send_ref = refs
    ncl = terms_ref.shape[0]
    arrivals((a0, a1, a2, a3), arr_ref)
    added = three(dot(basis_place_ref[...], arr_ref[...]), ncl)
    if scal:
        added *= -scal[0][0:1, :] / scal[0][1:2, :]
    send_terms(terms_ref[...] + added, sums_ref[...], send_ref)


def local_part_kernel(w_ref, weight_ref, inverse_ref, pick_ref, local_ref, pre_ref, cat, cat2):
    for lo, n in tiles(w_ref.shape[0], FINE):
        at = slice(lo, lo + n)
        cat[at, :] = pair(weight_ref[at, :] * w_ref[at, :])
    front(inverse_ref, weight_ref, pick_ref, cat, local_ref, pre_ref, cat2, True)


def local_shared_kernel(pre_ref, arr_ref, after_ref, local_place_ref, weight_ref, pick_ref,
                        *refs):
    *scal, out_ref, cat = refs
    for lo, n in tiles(weight_ref.shape[0], FINE):
        at = slice(lo, lo + n)
        came = halves(dot(local_place_ref[at, :], arr_ref[...]))
        cat[at, :] = pair(weight_ref[at, :] * came)
    for lo, n in tiles(pre_ref.shape[0], FINE):
        at = slice(lo, lo + n)
        came = halves(dot(pick_ref[at, :], cat[...]))
        if scal:
            came *= -scal[0][0:1, :] / scal[0][1:2, :]
        out_ref[at, :] = pre_ref[at, :] + came


def complete_kernel(w_part_ref, local_part_ref, arr_ref, after_ref, place_ref, local_place_ref,
                    *refs):
    *more, w_ref, local_ref = refs
    if more:
        scal_ref, z_part_ref, z_ref = more
        factor = -scal_ref[0:1, :] / scal_ref[1:2, :]

    def some(lo):
        at = pl.ds(lo, TILE)
        came = halves(dot(place_ref[at, :], arr_ref[...]))
        local = halves(dot(local_place_ref[at, :], arr_ref[...]))
        if more:
            z_ref[at, :] = z_part_ref[at, :] + came
            came, local = factor * came, factor * local
        w_ref[at, :] = w_part_ref[at, :] + came
        local_ref[at, :] = local_part_ref[at, :] + local

    each(w_ref.shape[0], TILE, some)


def step_scalars(before, now):
    beta = now[0:1, :] / before[0:1, :]
    energy = now[1:2, :] + beta * (now[2:3, :] + now[3:4, :]) + beta * beta * before[1:2, :]
    return beta, now[0:1, :] / energy, energy


def third_kernel(part_ref, image_ref, arr_ref, before_ref, scal_ref,
                 x1_ref, r1_ref, u1_ref, w1_ref, p_ref, s_ref, q_ref, z_ref,
                 place_ref, stiff_place_ref, weight_ref,
                 send_ref, state_ref, x2_ref, r2_ref, u2_ref, half_ref, p1_ref, s1_ref):
    rhs = r1_ref.shape[1]
    beta, alpha, energy = step_scalars(before_ref[...], scal_ref[...])

    def some(lo, sums):
        at = pl.ds(lo, TILE)
        m = completed(part_ref, at, place_ref, arr_ref)
        image = completed(image_ref, at, stiff_place_ref, arr_ref)
        p1 = u1_ref[at, :] + beta * p_ref[at, :]
        s1 = w1_ref[at, :] + beta * s_ref[at, :]
        q1 = m + beta * q_ref[at, :]
        r2 = r1_ref[at, :] - alpha * s1
        u2 = u1_ref[at, :] - alpha * q1
        half = w1_ref[at, :] - (alpha * beta) * z_ref[at, :]
        weight = weight_ref[at, :]
        left = weight * half - alpha * image
        weighted = weight * u2
        x2_ref[at, :] = x1_ref[at, :] + alpha * p1
        r2_ref[at, :] = r2
        u2_ref[at, :] = u2
        half_ref[at, :] = half - alpha * image
        p1_ref[at, :] = p1
        s1_ref[at, :] = s1
        news = (weighted * r2, u2 * left, weighted * s1, p1 * left)
        return tuple(old + folded(new) for old, new in zip(sums, news))

    sums = summed(r1_ref.shape[0], TILE, some, (jnp.zeros((8, rhs), F32),) * 4)
    wide = jnp.concatenate([jnp.sum(s, axis=0, keepdims=True) for s in sums], axis=1)
    send_ref[...] = jnp.broadcast_to(wide, send_ref.shape)
    state_ref[...] = jnp.concatenate(
        [scal_ref[0:1, :], energy, alpha, jnp.zeros((SCAL - 3, rhs), F32)], axis=0
    )


def last_kernel(state_ref, got_ref, a0, a1, a2, a3, place_ref,
                x2, u2, p1, r2, half, s1,
                x3_to, r3_to, arr_cat, x3, r3, out_sems):
    state = state_ref[...]
    total = jnp.sum(got_ref[...], axis=0, keepdims=True)
    rhs = state.shape[1]
    now = jnp.concatenate([total[:, k * rhs : (k + 1) * rhs] for k in range(4)], axis=0)
    beta, alpha, _ = step_scalars(state, now)
    old = state[2:3, :]
    arrivals((a0, a1, a2, a3), arr_cat)
    outs = []
    for i, (lo, n) in enumerate(tiles(r2.shape[0])):
        at = slice(lo, lo + n)
        x3[at, :] = x2[at, :] + alpha * (u2[at, :] + beta * p1[at, :])
        w2 = half[at, :] - old * halves(dot(place_ref[at, :], arr_cat[...]))
        r3[at, :] = r2[at, :] - alpha * (w2 + beta * s1[at, :])
        rows = pl.ds(lo, n)
        outs += bring(
            [(x3.at[rows, :], x3_to.at[rows, :]), (r3.at[rows, :], r3_to.at[rows, :])],
            out_sems.at[i],
        )
    for copy in outs:
        copy.wait()


def body(
    stiffness, local_inverse, coarse_basis, loads, counts, shared_rows, coarse_map, coarse_inverse
):
    size = lax.axis_size("sub")
    me = lax.axis_index("sub")
    rows, rhs = loads.shape[1:]
    ncl = coarse_basis.shape[1]
    slots, cap = shared_rows.shape[1:]
    order = coarse_inverse.shape[1]
    lists = slots * cap
    stiff, inverse = aside(stiffness[0], local_inverse[0])

    def partner(distance, parity):
        def of(i):
            up = (i // distance) % 2 == parity
            return (i + distance if up else i - distance) % size

        return [(i, of(i)) for i in range(size)]

    inside = partner(1, 0)
    swaps = [inside, partner(1, 1), partner(STRIDE, 0), partner(STRIDE, 1)]
    swaps = [swaps[j] for j in ORDER]

    def exchange(outs):
        return [lax.ppermute(out, "sub", swap) for out, swap in zip(outs, swaps)]

    cores = [[2 * i + c for i in range(size // 2)] for c in range(2)]
    groups = size // 2
    block = ncl + SCAL

    fields = (rows, rhs)
    out4 = [far((cap, rhs))] * 4
    wide = pltpu.VMEM((rows, 2 * rhs), BF16)
    wide_arr = pltpu.VMEM((lists, 2 * rhs), BF16)
    place_like = pltpu.VMEM((rows, lists), BF16)
    pick_like = pltpu.VMEM((lists, rows), BF16)
    basis = coarse_basis[0]
    (loads_aside,) = aside(loads[0])

    listed, maps, *outs = call(
        loads_kernel,
        "loads",
        (*aside(shared_rows[0]), loads_aside, *aside(coarse_map)),
        [far((1, lists), jnp.int32), far((size, LANES * pl.cdiv(ncl, LANES)), jnp.int32)] + out4,
        [
            pick_like,
            wide,
            pltpu.VMEM(fields, F32),
            pltpu.VMEM((slots, cap), jnp.int32),
            pltpu.VMEM((1, ncl), jnp.int32),
            pltpu.SemaphoreType.DMA((3,)),
        ],
        {0: ASPEC, 1: ASPEC, 2: ASPEC},
    )
    arrived = exchange(outs)
    maps = lax.all_to_all(maps, "sub", 0, 0, tiled=True)
    maps, *arrived = lax.optimization_barrier((maps, *arrived))


    (picked,) = call(
        columns_kernel,
        "coarse_columns",
        (maps, *aside(coarse_inverse)),
        [far((size * ncl, coarse_inverse.shape[0]))],
        [
            pltpu.VMEM((order, coarse_inverse.shape[0]), F32),
            pltpu.VMEM((4, coarse_inverse.shape[0], order // 4), F32),
            pltpu.SemaphoreType.DMA((4,)),
        ],
        {0: SSPEC, 1: ASPEC},
        mib=30,
    )
    mine_rows = lax.all_to_all(picked, "sub", 0, 0, tiled=True)

    r0, local, pre, send = call(
        first_kernel,
        "residual_and_terms",
        (loads[0], *arrived, listed, counts, basis, inverse),
        [away(fields), away(fields), away((lists, rhs)), far((groups * block, rhs))],
        [
            wide,
            wide_arr,
            place_like,
            pick_like,
            pltpu.VMEM((2 * ncl, rows), BF16),
            pltpu.VMEM((rows, rows), BF16),
            pltpu.VMEM(fields, F32),
            wide,
            pltpu.SemaphoreType.DMA((1,)),
        ],
        {8: ASPEC},
        us=6,
        mib=30,
    )
    products = call(
        products_kernel,
        "products",
        (listed, counts, basis, stiff),
        [
            away((rows, lists), BF16),
            away((lists, lists), BF16),
            away((2 * ncl, lists), BF16),
            away((lists, 2 * LANES), BF16),
        ],
        [
            pick_like,
            place_like,
            pltpu.VMEM((rows, rows), BF16),
            pltpu.VMEM((2 * ncl, rows), BF16),
            pltpu.VMEM((rows, 2 * LANES), BF16),
            pltpu.SemaphoreType.DMA((1,)),
        ],
        {3: ASPEC},
        us=10,
        mib=30,
    )
    r0, local, pre = aside(r0, local, pre)

    keep, pass_on = call(
        coarse_kernel,
        "coarse_block",
        (maps, (me % 2).reshape(1), mine_rows),
        [far((ncl, groups * ncl)), far((ncl, groups * ncl))],
        [
            pltpu.VMEM((order, LANES), F32),
            pltpu.VMEM((size * ncl, LANES), F32),
        ],
        {0: SSPEC, 1: SSPEC},
        mib=30,
    )
    passed = lax.ppermute(pass_on, "sub", inside)

    def share(send):
        return lax.all_to_all(send, "sub", 0, 0, tiled=True, axis_index_groups=cores)

    send, *products = lax.optimization_barrier((send, *products))
    terms = share(send)
    local_products = call(
        local_products_kernel,
        "local_products",
        (listed, counts, send, inverse),
        [away((rows, lists), BF16)],
        [place_like, pltpu.VMEM((rows, rows), BF16), pltpu.SemaphoreType.DMA((1,))],
        {2: ASPEC, 3: ASPEC},
        us=10,
        mib=30,
    )
    terms, *local_products = lax.optimization_barrier((terms, *local_products))
    local_products = aside(*local_products)
    coarse, after = call(
        stack_kernel,
        "coarse_addends",
        (keep, passed, terms),
        [near((4 * ncl, groups * ncl), BF16), far((SCAL, LANES))],
    )
    stiff_place, stiff_shared, basis_place, pick_basis = aside(*products)
    tables = held(*call(
        tables_kernel,
        "tables",
        (listed, counts, basis, after, stiff, stiff_place, stiff_shared, local),
        [
            near((lists, rows), BF16),
            near((rows, lists), BF16),
            near(fields),
            near((2 * ncl, rows), BF16),
            near((rows, 2 * LANES), BF16),
            near((rows, rows), BF16),
            near((rows, lists), BF16),
            near((lists, lists), BF16),
            near(fields),
        ],
        [pltpu.SemaphoreType.DMA((4,))],
        {4: ASPEC, 5: ASPEC, 6: ASPEC, 7: ASPEC},
        us=5,
    ))
    pick, place, weight, basis2, basis3, stiff, stiff_place, stiff_shared, local = tables
    (coarse,) = held(coarse)

    def correct(terms, pre, bring_in=None):
        own, other = call(
            coarse_solve_kernel,
            "coarse_solve",
            (terms, coarse),
            [far((block, rhs)), far((block, rhs))],
            us=1,
        )
        came = lax.ppermute(other, "sub", inside)
        if bring_in:
            small.extend(bring_in(own))
        values, scal, *outs = call(
            back_kernel,
            "coarse_back",
            (own, came, pre(own), small[0]),
            [near((2 * LANES, rhs), BF16), far((SCAL, rhs))] + out4,
            us=1,
        )
        return *held(values), scal, exchange(outs)

    small = []

    def bring_small(own):
        return held(*call(
            small_kernel,
            "small_tables",
            (own, pick_basis, basis_place, pre),
            [near(pick_basis.shape, BF16), near(basis_place.shape, BF16), near(pre.shape)],
            [pltpu.SemaphoreType.DMA((3,))],
            {1: ASPEC, 2: ASPEC, 3: ASPEC},
            us=1,
        ))

    def operate(values, local, arrived, flat=False):
        part, image, pre = held(*call(
            functools.partial(part_kernel, flat),
            "field_part",
            (values, local, weight, basis3, stiff, pick),
            [near(fields), near(fields), near((lists, rhs))],
            [wide, wide],
            us=3,
        ))
        arr, *outs = call(
            shared_kernel,
            "image_shared",
            (*arrived, pre, stiff_shared),
            [near((lists, 2 * rhs), BF16)] + out4,
            us=1,
        )
        return part, image, *held(arr), exchange(outs)

    def share_terms(arrived, terms, sums, *scal):
        arr, send = call(
            terms_kernel,
            "terms",
            (*arrived, terms, sums, small[1], *scal),
            [near((lists, 2 * rhs), BF16), far((groups * block, rhs))],
            us=1,
        )
        return *held(arr), share(send)

    def local_part(w):
        return held(*call(
            local_part_kernel,
            "local_part",
            (w, weight, inverse, pick),
            [near(fields), near((lists, rhs))],
            [wide, wide],
            us=3,
        ))

    def local_shared(pre, arr, *scal):
        def of(own):
            return held(*call(
                local_shared_kernel,
                "local_shared",
                (pre, arr, own, local_place, weight, pick, *scal),
                [near((lists, rhs))],
                [wide],
                us=1,
            ))[0]

        return of

    def complete(w, local, arr, after, *more):
        return held(*call(
            complete_kernel,
            "complete",
            (w, local, arr, after, place, local_place, *more),
            [near(fields)] * (3 if more else 2),
            us=2,
        ))

    values, _, arrived = correct(terms, lambda own: small[2], bring_small)
    part, image, arr, arrived = operate(values, local, arrived, True)
    u0, w0, terms, sums, inverse, local_place = held(*call(
        start_kernel,
        "start",
        (part, image, arr, r0, place, stiff_place, weight, basis2, inverse, *local_products),
        [near(fields), near(fields), near((ncl, rhs)), near((SCAL, rhs))]
        + [near((rows, rows), BF16), near((rows, lists), BF16)],
        [pltpu.SemaphoreType.DMA((2,))],
        {8: ASPEC, 9: ASPEC},
        us=3,
    ))
    local, pre = local_part(w0)
    terms, pre = held(*lax.optimization_barrier((terms, pre)))
    arr, terms = share_terms(arrived, terms, sums)
    values, scal0, arrived = correct(terms, local_shared(pre, arr))
    w0, local = complete(w0, local, arr, values)
    part, image, arr, arrived = operate(values, local, arrived)
    m0, z0, x1, r1, u1, w1, terms, sums = held(*call(
        second_kernel,
        "first_update",
        (part, image, arr, scal0, r0, u0, w0, place, stiff_place, weight, basis2),
        [near(fields)] * 6 + [near((ncl, rhs)), near((SCAL, rhs))],
        us=4,
    ))
    local, pre = local_part(w1)
    terms, pre = held(*lax.optimization_barrier((terms, pre)))
    arr, terms = share_terms(arrived, terms, sums, scal0)
    values, scal1, arrived = correct(terms, local_shared(pre, arr, scal0))
    z0, w1, local = complete(w1, local, arr, values, scal0, z0)

    part, image, arr, arrived = operate(values, local, arrived)
    pieces = len(tiles(rows))
    send, state, *news = call(
        third_kernel,
        "second_update",
        (part, image, arr, scal0, scal1, x1, r1, u1, w1, u0, w0, m0, z0)
        + (place, stiff_place, weight),
        [far((size, 4 * rhs)), far((SCAL, rhs))] + [near(fields)] * 6,
        us=4,
    )
    x2, r2, u2, half, p1, s1 = held(*news)
    send, *arrived = lax.optimization_barrier((send, *arrived))
    sums = lax.all_to_all(send, "sub", 0, 0, tiled=True)
    sums, *arrived = lax.optimization_barrier((sums, *arrived))
    x3, r3 = call(
        last_kernel,
        "last_update",
        (state, sums, *arrived, place, x2, u2, p1, r2, half, s1),
        [far(fields), far(fields)],
        [wide_arr, pltpu.VMEM(fields, F32), pltpu.VMEM(fields, F32)]
        + [pltpu.SemaphoreType.DMA((pieces, 2))],
        sent=range(2),
    )
    return (x3[None], r3[None])


def solution(mesh):
    placed = (
        P("sub", None, None),
        P("sub", None, None),
        P("sub", None, None),
        P("sub", None, None),
        P("sub", None),
        P("sub", None, None),
        P("sub", None),
        P("sub", None),
    )
    return jax.shard_map(
        body,
        mesh=mesh,
        in_specs=placed,
        out_specs=(P("sub", None, None), P("sub", None, None)),
        check_vma=False,
    )
```

```python
import functools

import jax
import jax.numpy as jnp
from jax import lax
from jax.experimental import pallas as pl
from jax.experimental.pallas import tpu as pltpu
from jax.sharding import PartitionSpec as P

STRIDE = 8
F32 = jnp.float32
BF16 = jnp.bfloat16
TILE = 512
FINE = 256
HALF = 768
SLOTS = 512
SCAL = 8
ORDER = (3, 0, 1, 2)
LANES = 128

VSPEC = pl.BlockSpec(memory_space=pltpu.VMEM)
SSPEC = pl.BlockSpec(memory_space=pltpu.SMEM)
ASPEC = pl.BlockSpec(memory_space=pltpu.HBM)


def near(shape, dtype=F32):
    return pltpu.VMEM(shape, dtype)


def far(shape, dtype=F32):
    return jax.ShapeDtypeStruct(shape, dtype)


def away(shape, dtype=F32):
    return pltpu.HBM(shape, dtype)


def held(*arrays):
    return tuple(pltpu.with_memory_space_constraint(a, pltpu.VMEM) for a in arrays)


def aside(*arrays):
    return tuple(pltpu.with_memory_space_constraint(a, pltpu.HBM) for a in arrays)


def call(kernel, name, args, outs, scratch=(), specs=None, us=2, mib=16, sent=()):
    specs = specs or {}
    return pl.pallas_call(
        kernel,
        name=name,
        out_shape=tuple(outs),
        in_specs=[specs.get(i, VSPEC) for i in range(len(args))],
        out_specs=tuple(ASPEC if i in sent else VSPEC for i in range(len(outs))),
        scratch_shapes=list(scratch),
        compiler_params=pltpu.CompilerParams(vmem_limit_bytes=mib * 1024 * 1024),
        cost_estimate=pl.CostEstimate(
            flops=0, bytes_accessed=us * 3_000_000, transcendentals=0
        ),
    )(*args)


def cut(x):
    high = x.astype(BF16)
    return high, (x - high.astype(F32)).astype(BF16)


def pair(x):
    return jnp.concatenate(cut(x), axis=1)


def halves(product):
    half = product.shape[1] // 2
    return product[:, :half] + product[:, half:]


def three(product, rows):
    half = product.shape[1] // 2
    return product[:rows, :half] + product[:rows, half:] + product[rows : 2 * rows, :half]


def dot(a, b):
    return jnp.dot(a, b, preferred_element_type=F32)


def tiles(total, step=TILE):
    step = min(step, total)
    return [(lo, min(step, total - lo)) for lo in range(0, total, step)]


def folded(x):
    return jnp.sum(x.reshape(-1, 8, x.shape[-1]), axis=0)


def pick_out(pick_ref, cat_ref, out_refs):
    cap = out_refs[0].shape[0]
    for j, out in enumerate(out_refs):
        out[...] = halves(dot(pick_ref[j * cap : (j + 1) * cap, :], cat_ref[...]))


def arrivals(arrived_refs, arr_cat):
    cap = arrived_refs[0].shape[0]
    for j, ref in enumerate(arrived_refs):
        arr_cat[j * cap : (j + 1) * cap, :] = pair(ref[...])


def bring(pairs, sems):
    copies = [pltpu.make_async_copy(*p, sems.at[i]) for i, p in enumerate(pairs)]
    for copy in copies:
        copy.start()
    return copies


def each(total, step, work, flat=False):
    if flat:
        for lo in range(0, total, step):
            work(lo)
        return

    def one(i, carry):
        work(pl.multiple_of(i * step, step))
        return carry

    lax.fori_loop(0, total // step, one, 0)


def summed(total, step, work, start):
    def one(i, carry):
        return work(pl.multiple_of(i * step, step), carry)

    return lax.fori_loop(0, total // step, one, start)


def fill_pick(row_ref, pick_ref):
    slots, rows = pick_ref.shape

    def some(lo):
        listed = row_ref[:, pl.ds(lo, LANES)].astype(F32)
        entries = jnp.broadcast_to(listed, (LANES, LANES)).T
        for left in range(0, rows, LANES):
            at = left + lax.broadcasted_iota(jnp.int32, (LANES, LANES), 1)
            same = jnp.where(at.astype(F32) == entries, 1.0, 0.0)
            pick_ref[pl.ds(lo, LANES), left : left + LANES] = same.astype(BF16)

    each(slots, LANES, some)


def fill_place(row_ref, place_ref):
    rows, slots = place_ref.shape

    def some(lo):
        at = lo + lax.broadcasted_iota(jnp.int32, (LANES, slots), 0)
        same = jnp.where(at == row_ref[...], 1.0, 0.0)
        place_ref[pl.ds(lo, LANES), :] = same.astype(BF16)

    each(rows, LANES, some)


def weights_of(count_ref):
    rows = count_ref.shape[1]
    return jnp.broadcast_to(1.0 / count_ref[...].astype(F32), (LANES, rows)).T


def fill_basis2(basis_ref, basis2_ref):
    ncl = basis_ref.shape[0]
    high, low = cut(basis_ref[...])
    basis2_ref[:ncl, :] = high
    basis2_ref[ncl:, :] = low


def loads_kernel(rows_from, loads_from, map_from, listed_ref, maps_ref, out0, out1, out2, out3,
                 pick, cat, loads, rows_ref, map_ref, sems):
    *firsts, last = bring([(rows_from, rows_ref), (map_from, map_ref), (loads_from, loads)], sems)
    copies = [last]
    for copy in firsts:
        copy.wait()
    size, ncl = maps_ref.shape[0], map_ref.shape[1]
    maps_ref[...] = jnp.zeros_like(maps_ref)
    maps_ref[:, :ncl] = jnp.broadcast_to(map_ref[...], (size, ncl))
    me = lax.axis_index("sub")
    one = me % 2 == 0
    far_one = (me // STRIDE) % 2 == 0
    given = [rows_ref[k : k + 1, :] for k in range(4)]
    lists = [
        jnp.where(one, given[0], given[1]),
        jnp.where(one, given[1], given[0]),
        jnp.where(far_one, given[2], given[3]),
        jnp.where(far_one, given[3], given[2]),
    ]
    listed_ref[...] = jnp.concatenate([lists[j] for j in ORDER], axis=1)
    fill_pick(listed_ref, pick)
    for copy in copies:
        copy.wait()
    for lo, n in tiles(loads.shape[0]):
        cat[lo : lo + n, :] = pair(loads[lo : lo + n, :])
    pick_out(pick, cat, (out0, out1, out2, out3))


def fill_basis3(basis_ref, basis3_ref):
    ncl, rows = basis_ref.shape
    high, low = cut(basis_ref[...])
    high, low = high.astype(F32), low.astype(F32)
    fill = jnp.zeros((basis3_ref.shape[1] - 3 * ncl, rows), F32)
    basis3_ref[...] = jnp.concatenate([high, high, low, fill], axis=0).T.astype(BF16)


def products_kernel(row_ref, count_ref, basis_ref, stiff_from,
                    stiff_place_ref, stiff_shared_ref, basis_place_ref, pick_basis_ref,
                    pick, place, stiff, basis2, basis3, sems):
    copy = pltpu.make_async_copy(stiff_from, stiff, sems.at[0])
    copy.start()
    fill_pick(row_ref, pick)
    fill_place(row_ref, place)
    weight = 1.0 / count_ref[...].astype(F32)
    fill_basis2(basis_ref, basis2)
    scaled = basis2[...].astype(F32) * weight
    basis_place_ref[...] = dot(scaled.astype(BF16), place[...]).astype(BF16)
    fill_basis3(basis_ref, basis3)
    full = weights_of(count_ref)
    for left in range(0, basis3.shape[1], LANES):
        at = slice(left, left + LANES)
        basis3[:, at] = (basis3[:, at].astype(F32) * full).astype(BF16)
    for lo, n in tiles(pick.shape[0]):
        pick_basis_ref[lo : lo + n, :] = dot(pick[lo : lo + n, :], basis3[...]).astype(BF16)
    copy.wait()

    def product(lo):
        at = pl.ds(lo, TILE)
        stiff_place_ref[at, :] = dot(stiff[at, :], place[...]).astype(BF16)

    def shared(lo):
        at = pl.ds(lo, TILE)
        stiff_shared_ref[at, :] = dot(pick[at, :], stiff_place_ref[...]).astype(BF16)

    each(stiff.shape[0], TILE, product)
    each(pick.shape[0], TILE, shared)


def local_products_kernel(row_ref, count_ref, after_ref, inverse_from, local_place_ref,
                          place, inverse, sems):
    copies = bring([(inverse_from, inverse)], sems)
    fill_place(row_ref, place)
    rows = place.shape[0]
    weight = jnp.broadcast_to(1.0 / count_ref[...].astype(F32), (8, rows)).astype(BF16)
    listed = dot(weight, place[...])[0:1]
    for copy in copies:
        copy.wait()

    def product(lo):
        at = pl.ds(lo, TILE)
        local_place_ref[at, :] = (dot(inverse[at, :], place[...]) * listed).astype(BF16)

    each(rows, TILE, product)


def tables_kernel(row_ref, count_ref, basis_ref, after_ref, stiff_from, stiff_place_from,
                  stiff_shared_from, local_from,
                  pick_ref, place_ref, weight_ref, basis2_ref, basis3_ref,
                  stiff_ref, stiff_place_ref, stiff_shared_ref, local_ref, sems):
    copies = bring(
        [
            (local_from, local_ref),
            (stiff_from, stiff_ref),
            (stiff_shared_from, stiff_shared_ref),
            (stiff_place_from, stiff_place_ref),
        ],
        sems,
    )
    fill_pick(row_ref, pick_ref)
    fill_place(row_ref, place_ref)
    weight_ref[...] = weights_of(count_ref)
    fill_basis2(basis_ref, basis2_ref)
    fill_basis3(basis_ref, basis3_ref)
    for copy in copies:
        copy.wait()


def small_kernel(after_ref, *refs):
    *refs, sems = refs
    number = len(refs) // 2
    for copy in bring(list(zip(refs[:number], refs[number:])), sems):
        copy.wait()


def columns_kernel(map_ref, inverse_from, out_ref, turned, rows, sems):
    parts = rows.shape[0]
    width = rows.shape[2]
    copies = bring(
        [(inverse_from.at[:, pl.ds(k * width, width)], rows.at[k]) for k in range(parts)], sems
    )
    for k in range(parts):
        copies[k].wait()
        turned[k * width : (k + 1) * width, :] = rows[k].T
    size = map_ref.shape[0]
    ncl = out_ref.shape[0] // size

    def step(i, _):
        for k in range(ncl):
            out_ref[pl.ds(i * ncl + k, 1), :] = turned[pl.ds(map_ref[i, k], 1), :]
        return 0

    lax.fori_loop(0, size, step, 0)


def coarse_kernel(map_ref, which_ref, got_ref, keep_ref, send_ref, turned, rowed):
    ncl, half = keep_ref.shape
    width = got_ref.shape[1]
    fill = jnp.zeros((turned.shape[1] - ncl, width), F32)
    for t in range(got_ref.shape[0] // ncl):
        block = jnp.concatenate([got_ref[t * ncl : (t + 1) * ncl, :], fill], axis=0)
        turned[t * width : (t + 1) * width, :] = block.T

    size = map_ref.shape[0]

    def step(i, _):
        for c in range(2):
            for k in range(ncl):
                row = turned[pl.ds(map_ref[2 * i + c, k], 1), :]
                rowed[pl.ds(c * half + i * ncl + k, 1), :] = row
        return 0

    lax.fori_loop(0, size // 2, step, 0)
    first = rowed[:half, :].T[:ncl, :]
    second = rowed[half:, :].T[:ncl, :]
    even = which_ref[0] == 0
    keep_ref[...] = jnp.where(even, first, second)
    send_ref[...] = jnp.where(even, second, first)


def stack_kernel(own_ref, other_ref, terms_ref, out_ref, after_ref):
    after_ref[...] = jnp.zeros_like(after_ref)
    ncl = own_ref.shape[0]
    own_high, own_low = cut(own_ref[...])
    other_high, other_low = cut(other_ref[...])
    out_ref[:ncl, :] = own_high
    out_ref[ncl : 2 * ncl, :] = other_high
    out_ref[2 * ncl : 3 * ncl, :] = own_low
    out_ref[3 * ncl :, :] = other_low


def send_terms(terms, scalars, send_ref):
    block = terms if scalars is None else jnp.concatenate([terms, scalars], axis=0)
    rows = block.shape[0]
    for g in range(send_ref.shape[0] // rows):
        send_ref[g * rows : (g + 1) * rows, :] = block


def front(inverse_ref, weight_ref, pick_ref, cat, local_ref, out_ref, cat2, flat=False):
    large, small = (FINE, FINE) if flat else (HALF, SLOTS)

    def product(lo):
        at = pl.ds(lo, large)
        local = halves(dot(inverse_ref[at, :], cat[...]))
        local_ref[at, :] = local
        cat2[at, :] = pair(weight_ref[at, :] * local)

    def shared(lo):
        at = pl.ds(lo, small)
        out_ref[at, :] = halves(dot(pick_ref[at, :], cat2[...]))

    each(inverse_ref.shape[0], large, product, flat)
    each(pick_ref.shape[0], small, shared, flat)


def first_kernel(loads_ref, a0, a1, a2, a3, row_ref, count_ref, basis_ref, inverse_from,
                 resid_ref, local_ref, pre_ref, send_ref,
                 cat, arr_cat, place, pick, basis2, inverse, weight, cat2, sems):
    copy = pltpu.make_async_copy(inverse_from, inverse, sems.at[0])
    copy.start()
    fill_place(row_ref, place)
    fill_basis2(basis_ref, basis2)
    weight[...] = weights_of(count_ref)
    ncl, rhs = basis_ref.shape[0], loads_ref.shape[1]
    arrivals((a0, a1, a2, a3), arr_cat)
    terms = jnp.zeros((2 * ncl, 2 * rhs), F32)
    for lo, n in tiles(loads_ref.shape[0]):
        at = slice(lo, lo + n)
        resid = loads_ref[at, :] + halves(dot(place[at, :], arr_cat[...]))
        resid_ref[at, :] = resid
        both = pair(weight[at, :] * resid)
        cat[at, :] = both
        terms += dot(basis2[:, at], both)
    send_terms(three(terms, ncl), None, send_ref)
    fill_pick(row_ref, pick)
    copy.wait()
    front(inverse, weight, pick, cat, local_ref, pre_ref, cat2)


def coarse_solve_kernel(extra, got_ref, g_ref, own_ref, other_ref):
    ncl = g_ref.shape[0] // 4
    rows = ncl + extra
    groups = got_ref.shape[0] // rows
    got = got_ref[...].reshape(groups, rows, got_ref.shape[1])
    terms = got[:, :ncl].reshape(groups * ncl, got_ref.shape[1])
    scalars = jnp.zeros((SCAL, got_ref.shape[1]), F32)
    if extra:
        scalars = jnp.sum(got[:, ncl:], axis=0)
    values = three(dot(g_ref[...], pair(terms)), 2 * ncl)
    own_ref[:ncl, :] = values[:ncl]
    own_ref[ncl:, :] = scalars
    other_ref[:ncl, :] = values[ncl:]
    other_ref[ncl:, :] = scalars


def back_kernel(own_ref, other_ref, pre_ref, pick_basis_ref,
                values_ref, scal_ref, out0, out1, out2, out3):
    ncl = own_ref.shape[0] - SCAL
    total = own_ref[...] + other_ref[...]
    scal_ref[...] = total[ncl:]
    high, low = cut(total[:ncl])
    fill = jnp.zeros((values_ref.shape[0] - 3 * ncl, high.shape[1]), BF16)
    values = jnp.concatenate([high, low, high, fill], axis=0)
    values_ref[...] = values
    cap = out0.shape[0]
    for j, out in enumerate((out0, out1, out2, out3)):
        at = slice(j * cap, (j + 1) * cap)
        out[...] = pre_ref[at, :] + dot(pick_basis_ref[at, :], values)


def part_kernel(flat, values_ref, local_ref, weight_ref, basis3_ref, stiff_ref, pick_ref,
                part_ref, image_ref, pre_ref, cat, cat2):
    values = values_ref[...]
    small, large, shared_step = (FINE, FINE, FINE) if flat else (TILE, HALF, SLOTS)

    def field(lo):
        at = pl.ds(lo, small)
        part = weight_ref[at, :] * (local_ref[at, :] + dot(basis3_ref[at, :], values))
        part_ref[at, :] = part
        cat[at, :] = pair(part)

    def product(lo):
        at = pl.ds(lo, large)
        image = halves(dot(stiff_ref[at, :], cat[...]))
        image_ref[at, :] = image
        cat2[at, :] = pair(image)

    def shared(lo):
        at = pl.ds(lo, shared_step)
        pre_ref[at, :] = halves(dot(pick_ref[at, :], cat2[...]))

    each(local_ref.shape[0], small, field, flat)
    each(local_ref.shape[0], large, product, flat)
    each(pick_ref.shape[0], shared_step, shared, flat)


def shared_kernel(a0, a1, a2, a3, pre_ref, stiff_shared_ref,
                  arr_ref, out0, out1, out2, out3):
    arrivals((a0, a1, a2, a3), arr_ref)
    cap = out0.shape[0]
    for j, out in enumerate((out0, out1, out2, out3)):
        at = slice(j * cap, (j + 1) * cap)
        out[...] = pre_ref[at, :] + halves(dot(stiff_shared_ref[at, :], arr_ref[...]))


def completed(ref, at, table_ref, arr_ref):
    return ref[at, :] + halves(dot(table_ref[at, :], arr_ref[...]))


def collect(sums, rhs):
    rows = [jnp.sum(s, axis=0, keepdims=True) for s in sums]
    rows.append(jnp.zeros((SCAL - len(rows), rhs), F32))
    return jnp.concatenate(rows, axis=0)


def start_kernel(part_ref, image_ref, arr_ref, r_ref, place_ref, stiff_place_ref,
                 weight_ref, basis2_ref, inverse_from, local_place_from,
                 u_ref, w_ref, terms_ref, sums_ref,
                 inverse_ref, local_place_ref, sems):
    copies = bring(
        [
            (inverse_from, inverse_ref),
            (local_place_from, local_place_ref),
        ],
        sems,
    )
    ncl = basis2_ref.shape[0] // 2
    rhs = r_ref.shape[1]

    def some(lo, carry):
        ru, uw, terms = carry
        at = pl.ds(lo, TILE)
        u = completed(part_ref, at, place_ref, arr_ref)
        w = completed(image_ref, at, stiff_place_ref, arr_ref)
        u_ref[at, :] = u
        w_ref[at, :] = w
        weight = weight_ref[at, :]
        ru += folded(weight * u * r_ref[at, :])
        uw += folded(u * w)
        return ru, uw, terms + dot(basis2_ref[:, at], pair(weight * w))

    zero = jnp.zeros((8, rhs), F32)
    start = (zero, zero, jnp.zeros((2 * ncl, 2 * rhs), F32))
    *sums, terms = summed(r_ref.shape[0], TILE, some, start)
    terms_ref[...] = three(terms, ncl)
    sums_ref[...] = collect(sums, rhs)
    for copy in copies:
        copy.wait()


def second_kernel(part_ref, image_ref, arr_ref, scal_ref, r_ref, u_ref, w_ref,
                  place_ref, stiff_place_ref, weight_ref, basis2_ref,
                  m_ref, z_ref, x1_ref, r1_ref, u1_ref, w1_ref, terms_ref, sums_ref):
    ncl = basis2_ref.shape[0] // 2
    rhs = r_ref.shape[1]
    alpha = scal_ref[0:1, :] / scal_ref[1:2, :]

    def some(lo, carry):
        *sums, terms = carry
        at = pl.ds(lo, TILE)
        m = completed(part_ref, at, place_ref, arr_ref)
        z = completed(image_ref, at, stiff_place_ref, arr_ref)
        m_ref[at, :] = m
        z_ref[at, :] = z
        weight = weight_ref[at, :]
        p, s = u_ref[at, :], w_ref[at, :]
        x1_ref[at, :] = alpha * p
        r1 = r_ref[at, :] - alpha * s
        u1 = p - alpha * m
        w1 = s - alpha * z
        r1_ref[at, :] = r1
        u1_ref[at, :] = u1
        w1_ref[at, :] = w1
        left = weight * s - alpha * z
        weighted = weight * u1
        news = (weighted * r1, u1 * left, weighted * s, p * left)
        sums = [old + folded(new) for old, new in zip(sums, news)]
        return *sums, terms + dot(basis2_ref[:, at], pair(weight * w1))

    start = (jnp.zeros((8, rhs), F32),) * 4 + (jnp.zeros((2 * ncl, 2 * rhs), F32),)
    *sums, terms = summed(r_ref.shape[0], TILE, some, start)
    terms_ref[...] = three(terms, ncl)
    sums_ref[...] = collect(sums, rhs)


def terms_kernel(a0, a1, a2, a3, terms_ref, sums_ref, basis_place_ref, *refs):
    *scal, arr_ref, send_ref = refs
    ncl = terms_ref.shape[0]
    arrivals((a0, a1, a2, a3), arr_ref)
    added = three(dot(basis_place_ref[...], arr_ref[...]), ncl)
    if scal:
        added *= -scal[0][0:1, :] / scal[0][1:2, :]
    send_terms(terms_ref[...] + added, sums_ref[...], send_ref)


def local_part_kernel(w_ref, weight_ref, inverse_ref, pick_ref, local_ref, pre_ref, cat, cat2):
    for lo, n in tiles(w_ref.shape[0], FINE):
        at = slice(lo, lo + n)
        cat[at, :] = pair(weight_ref[at, :] * w_ref[at, :])
    front(inverse_ref, weight_ref, pick_ref, cat, local_ref, pre_ref, cat2, True)


def local_shared_kernel(pre_ref, arr_ref, after_ref, local_place_ref, weight_ref, pick_ref,
                        *refs):
    *scal, out_ref, cat = refs
    for lo, n in tiles(weight_ref.shape[0], FINE):
        at = slice(lo, lo + n)
        came = halves(dot(local_place_ref[at, :], arr_ref[...]))
        cat[at, :] = pair(weight_ref[at, :] * came)
    for lo, n in tiles(pre_ref.shape[0], FINE):
        at = slice(lo, lo + n)
        came = halves(dot(pick_ref[at, :], cat[...]))
        if scal:
            came *= -scal[0][0:1, :] / scal[0][1:2, :]
        out_ref[at, :] = pre_ref[at, :] + came


def complete_kernel(w_part_ref, local_part_ref, arr_ref, after_ref, place_ref, local_place_ref,
                    *refs):
    *more, w_ref, local_ref = refs
    if more:
        scal_ref, z_part_ref, z_ref = more
        factor = -scal_ref[0:1, :] / scal_ref[1:2, :]

    def some(lo):
        at = pl.ds(lo, TILE)
        came = halves(dot(place_ref[at, :], arr_ref[...]))
        local = halves(dot(local_place_ref[at, :], arr_ref[...]))
        if more:
            z_ref[at, :] = z_part_ref[at, :] + came
            came, local = factor * came, factor * local
        w_ref[at, :] = w_part_ref[at, :] + came
        local_ref[at, :] = local_part_ref[at, :] + local

    each(w_ref.shape[0], TILE, some)


def step_scalars(before, now):
    beta = now[0:1, :] / before[0:1, :]
    energy = now[1:2, :] + beta * (now[2:3, :] + now[3:4, :]) + beta * beta * before[1:2, :]
    return beta, now[0:1, :] / energy, energy


def third_kernel(part_ref, image_ref, arr_ref, before_ref, scal_ref,
                 x1_ref, r1_ref, u1_ref, w1_ref, p_ref, s_ref, q_ref, z_ref,
                 place_ref, stiff_place_ref, weight_ref,
                 send_ref, state_ref, x2_ref, r2_ref, u2_ref, half_ref, p1_ref, s1_ref):
    rhs = r1_ref.shape[1]
    beta, alpha, energy = step_scalars(before_ref[...], scal_ref[...])

    def some(lo, sums):
        at = pl.ds(lo, TILE)
        m = completed(part_ref, at, place_ref, arr_ref)
        image = completed(image_ref, at, stiff_place_ref, arr_ref)
        p1 = u1_ref[at, :] + beta * p_ref[at, :]
        s1 = w1_ref[at, :] + beta * s_ref[at, :]
        q1 = m + beta * q_ref[at, :]
        r2 = r1_ref[at, :] - alpha * s1
        u2 = u1_ref[at, :] - alpha * q1
        half = w1_ref[at, :] - (alpha * beta) * z_ref[at, :]
        weight = weight_ref[at, :]
        left = weight * half - alpha * image
        weighted = weight * u2
        x2_ref[at, :] = x1_ref[at, :] + alpha * p1
        r2_ref[at, :] = r2
        u2_ref[at, :] = u2
        half_ref[at, :] = half - alpha * image
        p1_ref[at, :] = p1
        s1_ref[at, :] = s1
        news = (weighted * r2, u2 * left, weighted * s1, p1 * left)
        return tuple(old + folded(new) for old, new in zip(sums, news))

    sums = summed(r1_ref.shape[0], TILE, some, (jnp.zeros((8, rhs), F32),) * 4)
    wide = jnp.concatenate([jnp.sum(s, axis=0, keepdims=True) for s in sums], axis=1)
    send_ref[...] = jnp.broadcast_to(wide, send_ref.shape)
    state_ref[...] = jnp.concatenate(
        [scal_ref[0:1, :], energy, alpha, jnp.zeros((SCAL - 3, rhs), F32)], axis=0
    )


def last_kernel(state_ref, got_ref, a0, a1, a2, a3, place_ref,
                x2, u2, p1, r2, half, s1,
                x3_to, r3_to, arr_cat, x3, r3, out_sems):
    state = state_ref[...]
    total = jnp.sum(got_ref[...], axis=0, keepdims=True)
    rhs = state.shape[1]
    now = jnp.concatenate([total[:, k * rhs : (k + 1) * rhs] for k in range(4)], axis=0)
    beta, alpha, _ = step_scalars(state, now)
    old = state[2:3, :]
    arrivals((a0, a1, a2, a3), arr_cat)
    outs = []
    for i, (lo, n) in enumerate(tiles(r2.shape[0])):
        at = slice(lo, lo + n)
        x3[at, :] = x2[at, :] + alpha * (u2[at, :] + beta * p1[at, :])
        w2 = half[at, :] - old * halves(dot(place_ref[at, :], arr_cat[...]))
        r3[at, :] = r2[at, :] - alpha * (w2 + beta * s1[at, :])
        rows = pl.ds(lo, n)
        outs += bring(
            [(x3.at[rows, :], x3_to.at[rows, :]), (r3.at[rows, :], r3_to.at[rows, :])],
            out_sems.at[i],
        )
    for copy in outs:
        copy.wait()


def body(
    stiffness, local_inverse, coarse_basis, loads, counts, shared_rows, coarse_map, coarse_inverse
):
    size = lax.axis_size("sub")
    me = lax.axis_index("sub")
    rows, rhs = loads.shape[1:]
    ncl = coarse_basis.shape[1]
    slots, cap = shared_rows.shape[1:]
    order = coarse_inverse.shape[1]
    lists = slots * cap
    stiff, inverse = aside(stiffness[0], local_inverse[0])

    def partner(distance, parity):
        def of(i):
            up = (i // distance) % 2 == parity
            return (i + distance if up else i - distance) % size

        return [(i, of(i)) for i in range(size)]

    inside = partner(1, 0)
    swaps = [inside, partner(1, 1), partner(STRIDE, 0), partner(STRIDE, 1)]
    swaps = [swaps[j] for j in ORDER]

    def exchange(outs):
        return [lax.ppermute(out, "sub", swap) for out, swap in zip(outs, swaps)]

    cores = [[2 * i + c for i in range(size // 2)] for c in range(2)]
    groups = size // 2
    block = ncl + SCAL

    fields = (rows, rhs)
    out4 = [far((cap, rhs))] * 4
    wide = pltpu.VMEM((rows, 2 * rhs), BF16)
    wide_arr = pltpu.VMEM((lists, 2 * rhs), BF16)
    place_like = pltpu.VMEM((rows, lists), BF16)
    pick_like = pltpu.VMEM((lists, rows), BF16)
    basis = coarse_basis[0]
    (loads_aside,) = aside(loads[0])

    listed, maps, *outs = call(
        loads_kernel,
        "loads",
        (*aside(shared_rows[0]), loads_aside, *aside(coarse_map)),
        [far((1, lists), jnp.int32), far((size, LANES * pl.cdiv(ncl, LANES)), jnp.int32)] + out4,
        [
            pick_like,
            wide,
            pltpu.VMEM(fields, F32),
            pltpu.VMEM((slots, cap), jnp.int32),
            pltpu.VMEM((1, ncl), jnp.int32),
            pltpu.SemaphoreType.DMA((3,)),
        ],
        {0: ASPEC, 1: ASPEC, 2: ASPEC},
    )
    arrived = exchange(outs)
    maps = lax.all_to_all(maps, "sub", 0, 0, tiled=True)
    maps, *arrived = lax.optimization_barrier((maps, *arrived))


    (picked,) = call(
        columns_kernel,
        "coarse_columns",
        (maps, *aside(coarse_inverse)),
        [far((size * ncl, coarse_inverse.shape[0]))],
        [
            pltpu.VMEM((order, coarse_inverse.shape[0]), F32),
            pltpu.VMEM((4, coarse_inverse.shape[0], order // 4), F32),
            pltpu.SemaphoreType.DMA((4,)),
        ],
        {0: SSPEC, 1: ASPEC},
        mib=30,
    )
    mine_rows = lax.all_to_all(picked, "sub", 0, 0, tiled=True)

    r0, local, pre, send = call(
        first_kernel,
        "residual_and_terms",
        (loads[0], *arrived, listed, counts, basis, inverse),
        [away(fields), away(fields), away((lists, rhs)), far((groups * ncl, rhs))],
        [
            wide,
            wide_arr,
            place_like,
            pick_like,
            pltpu.VMEM((2 * ncl, rows), BF16),
            pltpu.VMEM((rows, rows), BF16),
            pltpu.VMEM(fields, F32),
            wide,
            pltpu.SemaphoreType.DMA((1,)),
        ],
        {8: ASPEC},
        us=6,
        mib=30,
    )
    products = call(
        products_kernel,
        "products",
        (listed, counts, basis, stiff),
        [
            away((rows, lists), BF16),
            away((lists, lists), BF16),
            away((2 * ncl, lists), BF16),
            away((lists, 2 * LANES), BF16),
        ],
        [
            pick_like,
            place_like,
            pltpu.VMEM((rows, rows), BF16),
            pltpu.VMEM((2 * ncl, rows), BF16),
            pltpu.VMEM((rows, 2 * LANES), BF16),
            pltpu.SemaphoreType.DMA((1,)),
        ],
        {3: ASPEC},
        us=10,
        mib=30,
    )
    r0, local, pre = aside(r0, local, pre)

    keep, pass_on = call(
        coarse_kernel,
        "coarse_block",
        (maps, (me % 2).reshape(1), mine_rows),
        [far((ncl, groups * ncl)), far((ncl, groups * ncl))],
        [
            pltpu.VMEM((order, LANES), F32),
            pltpu.VMEM((size * ncl, LANES), F32),
        ],
        {0: SSPEC, 1: SSPEC},
        mib=30,
    )
    passed = lax.ppermute(pass_on, "sub", inside)

    def share(send):
        return lax.all_to_all(send, "sub", 0, 0, tiled=True, axis_index_groups=cores)

    send, *products = lax.optimization_barrier((send, *products))
    terms = share(send)
    local_products = call(
        local_products_kernel,
        "local_products",
        (listed, counts, send, inverse),
        [away((rows, lists), BF16)],
        [place_like, pltpu.VMEM((rows, rows), BF16), pltpu.SemaphoreType.DMA((1,))],
        {2: ASPEC, 3: ASPEC},
        us=10,
        mib=30,
    )
    terms, *local_products = lax.optimization_barrier((terms, *local_products))
    local_products = aside(*local_products)
    coarse, after = call(
        stack_kernel,
        "coarse_addends",
        (keep, passed, terms),
        [near((4 * ncl, groups * ncl), BF16), far((SCAL, LANES))],
    )
    stiff_place, stiff_shared, basis_place, pick_basis = aside(*products)
    tables = held(*call(
        tables_kernel,
        "tables",
        (listed, counts, basis, after, stiff, stiff_place, stiff_shared, local),
        [
            near((lists, rows), BF16),
            near((rows, lists), BF16),
            near(fields),
            near((2 * ncl, rows), BF16),
            near((rows, 2 * LANES), BF16),
            near((rows, rows), BF16),
            near((rows, lists), BF16),
            near((lists, lists), BF16),
            near(fields),
        ],
        [pltpu.SemaphoreType.DMA((4,))],
        {4: ASPEC, 5: ASPEC, 6: ASPEC, 7: ASPEC},
        us=5,
    ))
    pick, place, weight, basis2, basis3, stiff, stiff_place, stiff_shared, local = tables
    (coarse,) = held(coarse)

    def correct(terms, pre, bring_in=None):
        own, other = call(
            functools.partial(coarse_solve_kernel, 0 if bring_in else SCAL),
            "coarse_solve",
            (terms, coarse),
            [far((block, rhs)), far((block, rhs))],
            us=1,
        )
        came = lax.ppermute(other, "sub", inside)
        if bring_in:
            small.extend(bring_in(own))
        values, scal, *outs = call(
            back_kernel,
            "coarse_back",
            (own, came, pre(own), small[0]),
            [near((2 * LANES, rhs), BF16), far((SCAL, rhs))] + out4,
            us=1,
        )
        return *held(values), scal, exchange(outs)

    small = []

    def bring_small(own):
        return held(*call(
            small_kernel,
            "small_tables",
            (own, pick_basis, basis_place, pre),
            [near(pick_basis.shape, BF16), near(basis_place.shape, BF16), near(pre.shape)],
            [pltpu.SemaphoreType.DMA((3,))],
            {1: ASPEC, 2: ASPEC, 3: ASPEC},
            us=1,
        ))

    def operate(values, local, arrived, flat=False):
        part, image, pre = held(*call(
            functools.partial(part_kernel, flat),
            "field_part",
            (values, local, weight, basis3, stiff, pick),
            [near(fields), near(fields), near((lists, rhs))],
            [wide, wide],
            us=3,
        ))
        arr, *outs = call(
            shared_kernel,
            "image_shared",
            (*arrived, pre, stiff_shared),
            [near((lists, 2 * rhs), BF16)] + out4,
            us=1,
        )
        return part, image, *held(arr), exchange(outs)

    def share_terms(arrived, terms, sums, *scal):
        arr, send = call(
            terms_kernel,
            "terms",
            (*arrived, terms, sums, small[1], *scal),
            [near((lists, 2 * rhs), BF16), far((groups * block, rhs))],
            us=1,
        )
        return *held(arr), share(send)

    def local_part(w):
        return held(*call(
            local_part_kernel,
            "local_part",
            (w, weight, inverse, pick),
            [near(fields), near((lists, rhs))],
            [wide, wide],
            us=3,
        ))

    def local_shared(pre, arr, *scal):
        def of(own):
            return held(*call(
                local_shared_kernel,
                "local_shared",
                (pre, arr, own, local_place, weight, pick, *scal),
                [near((lists, rhs))],
                [wide],
                us=1,
            ))[0]

        return of

    def complete(w, local, arr, after, *more):
        return held(*call(
            complete_kernel,
            "complete",
            (w, local, arr, after, place, local_place, *more),
            [near(fields)] * (3 if more else 2),
            us=2,
        ))

    values, _, arrived = correct(terms, lambda own: small[2], bring_small)
    part, image, arr, arrived = operate(values, local, arrived, True)
    u0, w0, terms, sums, inverse, local_place = held(*call(
        start_kernel,
        "start",
        (part, image, arr, r0, place, stiff_place, weight, basis2, inverse, *local_products),
        [near(fields), near(fields), near((ncl, rhs)), near((SCAL, rhs))]
        + [near((rows, rows), BF16), near((rows, lists), BF16)],
        [pltpu.SemaphoreType.DMA((2,))],
        {8: ASPEC, 9: ASPEC},
        us=3,
    ))
    local, pre = local_part(w0)
    terms, pre = held(*lax.optimization_barrier((terms, pre)))
    arr, terms = share_terms(arrived, terms, sums)
    values, scal0, arrived = correct(terms, local_shared(pre, arr))
    w0, local = complete(w0, local, arr, values)
    part, image, arr, arrived = operate(values, local, arrived)
    m0, z0, x1, r1, u1, w1, terms, sums = held(*call(
        second_kernel,
        "first_update",
        (part, image, arr, scal0, r0, u0, w0, place, stiff_place, weight, basis2),
        [near(fields)] * 6 + [near((ncl, rhs)), near((SCAL, rhs))],
        us=4,
    ))
    local, pre = local_part(w1)
    terms, pre = held(*lax.optimization_barrier((terms, pre)))
    arr, terms = share_terms(arrived, terms, sums, scal0)
    values, scal1, arrived = correct(terms, local_shared(pre, arr, scal0))
    z0, w1, local = complete(w1, local, arr, values, scal0, z0)

    part, image, arr, arrived = operate(values, local, arrived)
    pieces = len(tiles(rows))
    send, state, *news = call(
        third_kernel,
        "second_update",
        (part, image, arr, scal0, scal1, x1, r1, u1, w1, u0, w0, m0, z0)
        + (place, stiff_place, weight),
        [far((size, 4 * rhs)), far((SCAL, rhs))] + [near(fields)] * 6,
        us=4,
    )
    x2, r2, u2, half, p1, s1 = held(*news)
    send, *arrived = lax.optimization_barrier((send, *arrived))
    sums = lax.all_to_all(send, "sub", 0, 0, tiled=True)
    sums, *arrived = lax.optimization_barrier((sums, *arrived))
    x3, r3 = call(
        last_kernel,
        "last_update",
        (state, sums, *arrived, place, x2, u2, p1, r2, half, s1),
        [far(fields), far(fields)],
        [wide_arr, pltpu.VMEM(fields, F32), pltpu.VMEM(fields, F32)]
        + [pltpu.SemaphoreType.DMA((pieces, 2))],
        sent=range(2),
    )
    return (x3[None], r3[None])


def solution(mesh):
    placed = (
        P("sub", None, None),
        P("sub", None, None),
        P("sub", None, None),
        P("sub", None, None),
        P("sub", None),
        P("sub", None, None),
        P("sub", None),
        P("sub", None),
    )
    return jax.shard_map(
        body,
        mesh=mesh,
        in_specs=placed,
        out_specs=(P("sub", None, None), P("sub", None, None)),
        check_vma=False,
    )
```
